512 devices in a mesh: img: 128 (over y, z, core), view: 4 (over x).
Axes of the slice: x: 4, y: 8, z: 8, core: 2. Of those that a mesh axis runs over, the one named last changes fastest.
Arguments:
- gauss_params: float32 [59, 1048576], P(None, 'img'), may hold values from -6 to 6, as said below
- camera: float32 [4, 6], P('view'), may hold values from -0.3 to 6, as said below
- background: float32 [3], replicated, may hold values from 0 to 1
- tile_lists: int32 [4, 512, 256], P('view', 'img'), may hold values from 0 to 1048575, as said below
- tile_lengths: int32 [4, 512], P('view', 'img'), may hold values from 1 to 256, 78643 in all within a row
- pixel_cotangent: float32 [4, 3, 512, 256], P('view', None, 'img'), may hold values from -24 to 24
Outputs:
- gauss_grads: float32 [59, 1048576], P(None, 'img')
The draws below stay inside these ranges and needn't reach their ends.
Inputs may be any that keep to these rules, and one draw needn't show every extreme that they name: `tile_lists`: entry g names Gaussian g, owned by index g // 8192 of img at column g % 8192; slots are composited in list order. Within the 4 tiles of one view on one index of img, at most 16 slots name Gaussians of one owner, and exactly 16 for some owner; a Gaussian may stand in several slots. `tile_lengths`: slots at or beyond a tile's length are empty. `gauss_params`: rows 0 to 2 lie in [-6, 6]; rows 3 to 5 in [-3, -0.5]; row 6 in [0.5, 1.5], rows 7 to 9 in [-1.5, 1.5]; row 10 in [-5, -2]; rows 11 to 58 in [-1, 1]. `camera`: columns 0 to 2 lie in [-0.15, 0.15], columns 3 and 4 in [-0.3, 0.3], column 5 in [4, 6].
All inputs are finite; a program needn't handle non-finite values. No bound on the sum of `tile_lengths` on one device may be relied on, other than what follows from the above.
Results may differ from the reference program's by a relative error of at most 0.0003.
Values sent between devices are 32-bit elements; how exact they have to be, the bound alone decides.
No kernel may reach another device: no remote copies, remote signals or barrier semaphores. Data moves between devices by JAX's collectives and lax.ppermute only.
A program may use at most 128 MiB of HBM per device.

```python
import math
import jax
import jax.numpy as jnp
import numpy as np
from jax import lax

SIDE = 16
PIX = 256
SLOTS = 256
TX = 16
TILES_DEV = 4
G_DEV = 8192
VIEWS = 4
OWNERS = 128
TILES = 512
GAUSS = 1048576
CAP = 16


def camera_common(key):
    key = jax.random.fold_in(key, 7)
    first, second, third = jax.random.split(key, 3)
    angles = jax.random.uniform(first, (VIEWS, 3), jnp.float32, -0.15, 0.15)
    lateral = jax.random.uniform(second, (VIEWS, 2), jnp.float32, -0.3, 0.3)
    distance = jax.random.uniform(third, (VIEWS, 1), jnp.float32, 4.0, 6.0)
    return jnp.concatenate([angles, lateral, distance], axis=1)


def lists_common(key):
    key = jax.random.fold_in(key, 11)
    block_key, column_key = jax.random.split(key, 2)
    block_rows = TILES_DEV * SLOTS

    def one_block(one_key):
        first, second, third = jax.random.split(one_key, 3)
        busiest = jax.random.randint(first, (), 0, OWNERS)
        others = (busiest + 1 + jnp.arange((OWNERS - 1) * CAP) // CAP) % OWNERS
        others = jax.random.permutation(second, others)[:block_rows - CAP]
        owners = jnp.concatenate([jnp.full((CAP,), busiest, jnp.int32), others.astype(jnp.int32)])
        return jax.random.permutation(third, owners)
    owners_flat = jax.vmap(one_block)(jax.random.split(block_key, VIEWS * OWNERS)).reshape(-1).astype(jnp.int32)
    total = owners_flat.shape[0]
    ordering = jnp.argsort(owners_flat, stable=True)
    sorted_owner = owners_flat[ordering]
    counts = jax.ops.segment_sum(jnp.ones((total,), jnp.int32), owners_flat, num_segments=OWNERS)
    starts = jnp.cumsum(counts) - counts
    rank_sorted = jnp.arange(total, dtype=jnp.int32) - starts[sorted_owner]
    rank = jnp.zeros((total,), jnp.int32).at[ordering].set(rank_sorted)
    shuffles = jax.vmap(lambda one_key: jax.random.permutation(one_key, G_DEV))(jax.random.split(column_key, OWNERS))
    columns = shuffles[owners_flat, rank % G_DEV].astype(jnp.int32)
    return (owners_flat * G_DEV + columns).reshape(VIEWS, TILES, SLOTS).astype(jnp.int32)


def draw_camera(key, part):
    return camera_common(key)


def draw_tile_lists(key, part):
    return lists_common(key)


def draw_gauss_params(key, part):
    listed = lists_common(key)
    cameras = camera_common(key)
    key = jax.random.fold_in(key, 5)
    keys = jax.random.split(key, 10)
    count = GAUSS
    plane = jax.random.uniform(keys[0], (2, count), jnp.float32, -1.5, 1.5)
    depth = jax.random.uniform(keys[1], (1, count), jnp.float32, -1.0, 1.0)
    log_scale = jax.random.uniform(keys[2], (3, count), jnp.float32, -3.0, -0.5)
    real_part = jax.random.uniform(keys[3], (1, count), jnp.float32, 0.5, 1.5)
    imag_part = jnp.clip(0.5 * jax.random.normal(keys[4], (3, count), jnp.float32), -1.5, 1.5)
    logit = jax.random.uniform(keys[5], (1, count), jnp.float32, -5.0, -2.0)
    coeffs = jnp.clip(0.3 * jax.random.normal(keys[6], (48, count), jnp.float32), -1.0, 1.0)
    flat = listed.reshape(-1)
    slot_total = flat.shape[0]
    slot_index = jnp.full((count,), -1, jnp.int32).at[flat].max(jnp.arange(slot_total, dtype=jnp.int32))
    is_listed = slot_index >= 0
    safe = jnp.maximum(slot_index, 0)
    view_of = safe // (TILES * SLOTS)
    tile_of = safe // SLOTS % TILES
    slot_of = safe % SLOTS
    jitter_x = jax.random.uniform(keys[7], (count,), jnp.float32, -0.4, 0.4)
    jitter_y = jax.random.uniform(keys[8], (count,), jnp.float32, -0.4, 0.4)
    jitter_d = jax.random.uniform(keys[9], (count,), jnp.float32, 0.0, 1.0)
    height = TILES // TX
    screen_x = ((tile_of % TX).astype(jnp.float32) + 0.5 + jitter_x) / TX * 2.0 - 1.0
    screen_y = ((tile_of // TX).astype(jnp.float32) + 0.5 + jitter_y) / height * 2.0 - 1.0
    chosen = cameras[view_of]
    view_depth = chosen[:, 5] - 0.9 + 1.8 * (slot_of.astype(jnp.float32) + jitter_d) / SLOTS
    shift_x = screen_x * view_depth * 0.5 - chosen[:, 3]
    shift_y = screen_y * view_depth * 0.5 - chosen[:, 4]
    shift_z = view_depth - chosen[:, 5]
    cos_x, sin_x = (jnp.cos(chosen[:, 0]), jnp.sin(chosen[:, 0]))
    cos_y, sin_y = (jnp.cos(chosen[:, 1]), jnp.sin(chosen[:, 1]))
    cos_z, sin_z = (jnp.cos(chosen[:, 2]), jnp.sin(chosen[:, 2]))
    step_a0 = cos_z * shift_x + sin_z * shift_y
    step_a1 = -sin_z * shift_x + cos_z * shift_y
    step_b0 = cos_y * step_a0 - sin_y * shift_z
    step_b2 = sin_y * step_a0 + cos_y * shift_z
    center_x = step_b0
    center_y = cos_x * step_a1 + sin_x * step_b2
    center_z = -sin_x * step_a1 + cos_x * step_b2
    placed = jnp.stack([center_x, center_y, center_z])
    initial = jnp.concatenate([plane, depth], axis=0)
    centers = jnp.where(is_listed[None, :], placed, initial)
    return jnp.concatenate([centers, log_scale, real_part, imag_part, logit, coeffs], axis=0)


def level_of(own_key, shape, pieces, smallest, largest):
    loudness = 1.0
    for position, blocks in pieces:
        draws = jax.random.uniform(jax.random.fold_in(jax.random.fold_in(own_key, 6), position), (blocks,), jnp.float32, smallest / len(pieces), largest / len(pieces))
        loudness = loudness * jnp.repeat(jnp.exp(draws), shape[position] // blocks).reshape((-1,) + (1,) * (len(shape) - 1 - position))
    return loudness


def split_up(amount, total, reach, lean):
    portions = [(1 << 20) // math.isqrt(standing ** lean) + 1 for standing in range(2, amount + 1)]
    surplus, holding = total - reach - (amount - 1), [1] * (amount - 1)
    while surplus > 0:
        movable = [i for i in range(amount - 1) if holding[i] < reach]
        whole, remaining = sum([portions[i] for i in movable]), surplus
        for i in movable:
            addition = min(reach - holding[i], max(1, remaining * portions[i] // whole), surplus)
            holding[i] = holding[i] + addition
            surplus = surplus - addition
    return np.array([reach] + holding)


def uneven_parts(key, amount, total, bound, lean):
    if amount == 2:
        one = jax.random.randint(key, (), max(1, total - bound), min(bound, total - 1) + 1)
        return jnp.stack([one, total - one])
    sizes = jnp.asarray(split_up(amount, total, bound, lean), jnp.int32)
    twos = (amount - 1) // 2
    donor, receiver = sizes[1:1 + 2 * twos:2], sizes[2:2 + 2 * twos:2]
    slack = jnp.minimum(donor - 1, bound - receiver)
    passed = jax.random.randint(jax.random.fold_in(key, 1), (twos,), 0, 1 << 20) % (slack + 1)
    sizes = sizes.at[1:1 + 2 * twos:2].set(donor - passed).at[2:2 + 2 * twos:2].set(receiver + passed)
    return sizes[jax.random.permutation(jax.random.fold_in(key, 2), amount)]


def gaussian(own_key, extent, scale, bound, shards=(), held_as=jnp.bfloat16):
    entries = scale * jax.random.normal(own_key, extent, jnp.float32)
    if shards:
        entries = entries * level_of(own_key, extent, shards, -0.22, 0.18)
    return jnp.clip(entries, -bound, bound).astype(held_as)


def setup_inputs(seed: int = 0) -> dict:
    splits = jax.random.split(jax.random.key(seed), 7)
    gauss_params = draw_gauss_params(jax.random.fold_in(splits[6], 71), 0)
    camera = draw_camera(jax.random.fold_in(splits[6], 71), 0)
    background = jnp.clip(jax.random.uniform(splits[2], (3,), jnp.float32, 0.0, 1.0), 0.0, 1.0)
    tile_lists = draw_tile_lists(jax.random.fold_in(splits[6], 71), 0)
    tile_lengths = jax.vmap(lambda own: uneven_parts(own, TILES, TILES * SLOTS * 3 // 5, SLOTS, 2))(jax.random.split(splits[4], VIEWS)).reshape((VIEWS, TILES)).astype(jnp.int32)
    pixel_cotangent = gaussian(splits[5], (VIEWS, 3, TILES, PIX), 4.0, 24.0, ((0, 4), (2, 128)), jnp.float32)
    return dict(gauss_params=gauss_params, camera=camera, background=background, tile_lists=tile_lists, tile_lengths=tile_lengths, pixel_cotangent=pixel_cotangent)


FOCAL = 2.0
DILATION = 0.0001
SH_ZERO = 0.28209479177387814
SH_ONE = 0.4886025119029199
SH_TWO = (1.0925484305920792, -1.0925484305920792, 0.31539156525252005, -1.0925484305920792, 0.5462742152960396)
SH_THREE = (-0.5900435899266435, 2.890611442640554, -0.4570457994644658, 0.3731763325901154, -0.4570457994644658, 1.445305721320277, -0.5900435899266435)

def rotation(angles):
    cos_x, sin_x = (jnp.cos(angles[0]), jnp.sin(angles[0]))
    cos_y, sin_y = (jnp.cos(angles[1]), jnp.sin(angles[1]))
    cos_z, sin_z = (jnp.cos(angles[2]), jnp.sin(angles[2]))
    unity = jnp.ones_like(cos_x)
    zeros = jnp.zeros_like(cos_x)
    about_x = jnp.stack([jnp.stack([unity, zeros, zeros]), jnp.stack([zeros, cos_x, -sin_x]), jnp.stack([zeros, sin_x, cos_x])])
    about_y = jnp.stack([jnp.stack([cos_y, zeros, sin_y]), jnp.stack([zeros, unity, zeros]), jnp.stack([-sin_y, zeros, cos_y])])
    about_z = jnp.stack([jnp.stack([cos_z, -sin_z, zeros]), jnp.stack([sin_z, cos_z, zeros]), jnp.stack([zeros, zeros, unity])])
    inner_pair = jnp.dot(about_y, about_x, precision=lax.Precision.HIGHEST)
    return jnp.dot(about_z, inner_pair, precision=lax.Precision.HIGHEST)

def harmonics(direction):
    along_x, along_y, along_z = (direction[0], direction[1], direction[2])
    square_x, square_y, square_z = (along_x * along_x, along_y * along_y, along_z * along_z)
    return [SH_ZERO * jnp.ones_like(along_x), -SH_ONE * along_y, SH_ONE * along_z, -SH_ONE * along_x, SH_TWO[0] * along_x * along_y, SH_TWO[1] * along_y * along_z, SH_TWO[2] * (2.0 * square_z - square_x - square_y), SH_TWO[3] * along_x * along_z, SH_TWO[4] * (square_x - square_y), SH_THREE[0] * along_y * (3.0 * square_x - square_y), SH_THREE[1] * along_x * along_y * along_z, SH_THREE[2] * along_y * (4.0 * square_z - square_x - square_y), SH_THREE[3] * along_z * (2.0 * square_z - 3.0 * square_x - 3.0 * square_y), SH_THREE[4] * along_x * (4.0 * square_z - square_x - square_y), SH_THREE[5] * along_z * (square_x - square_y), SH_THREE[6] * along_x * (square_x - 3.0 * square_y)]

def project(params, camera):
    rotate = rotation(camera[0:3])
    offset = camera[3:6]
    centers = params[0:3]
    viewed = jnp.dot(rotate, centers, precision=lax.Precision.HIGHEST) + offset[:, None]
    depth_inv = 1.0 / viewed[2]
    screen_x = FOCAL * viewed[0] * depth_inv
    screen_y = FOCAL * viewed[1] * depth_inv
    scales = jnp.exp(params[3:6])
    quaternion = params[6:10]
    quaternion = quaternion * lax.rsqrt(lax.optimization_barrier(jnp.sum(quaternion * quaternion, axis=0, keepdims=True)))
    real_part, imag_i, imag_j, imag_k = (quaternion[0], quaternion[1], quaternion[2], quaternion[3])
    local_rot = [[1.0 - 2.0 * (imag_j * imag_j + imag_k * imag_k), 2.0 * (imag_i * imag_j - real_part * imag_k), 2.0 * (imag_i * imag_k + real_part * imag_j)], [2.0 * (imag_i * imag_j + real_part * imag_k), 1.0 - 2.0 * (imag_i * imag_i + imag_k * imag_k), 2.0 * (imag_j * imag_k - real_part * imag_i)], [2.0 * (imag_i * imag_k - real_part * imag_j), 2.0 * (imag_j * imag_k + real_part * imag_i), 1.0 - 2.0 * (imag_i * imag_i + imag_j * imag_j)]]
    scaled = [[local_rot[row_index][col_index] * scales[col_index] for col_index in range(3)] for row_index in range(3)]
    jacobian = [[FOCAL * depth_inv, 0.0, -FOCAL * viewed[0] * depth_inv * depth_inv], [0.0, FOCAL * depth_inv, -FOCAL * viewed[1] * depth_inv * depth_inv]]
    to_camera = [[sum((jacobian[row_index][mid_index] * rotate[mid_index, col_index] for mid_index in range(3))) for col_index in range(3)] for row_index in range(2)]
    screen_map = [[sum((to_camera[row_index][mid_index] * scaled[mid_index][col_index] for mid_index in range(3))) for col_index in range(3)] for row_index in range(2)]
    cov_a = sum((screen_map[0][col_index] * screen_map[0][col_index] for col_index in range(3))) + DILATION
    cov_b = sum((screen_map[0][col_index] * screen_map[1][col_index] for col_index in range(3)))
    cov_c = sum((screen_map[1][col_index] * screen_map[1][col_index] for col_index in range(3))) + DILATION
    determinant = cov_a * cov_c - cov_b * cov_b
    opacity = jax.nn.sigmoid(params[10])
    center = -jnp.dot(rotate.T, offset, precision=lax.Precision.HIGHEST)
    toward = centers - center[:, None]
    toward = toward * lax.rsqrt(lax.optimization_barrier(jnp.sum(toward * toward, axis=0, keepdims=True)))
    sh_basis = jnp.stack(harmonics(toward))
    coeffs = params[11:59].reshape(16, 3, -1)
    colors = 0.5 + lax.optimization_barrier(jnp.sum(sh_basis[:, None, :] * coeffs, axis=0))
    screen = jnp.stack([screen_x, screen_y, cov_c / determinant, -cov_b / determinant, cov_a / determinant, opacity])
    return jnp.concatenate([screen, colors], axis=0)

def render_tile(feature, live_mask, pixel_x, pixel_y, background):
    delta_x = pixel_x[:, None] - feature[0][None, :]
    delta_y = pixel_y[:, None] - feature[1][None, :]
    quadric = feature[2] * delta_x * delta_x + 2.0 * feature[3] * delta_x * delta_y + feature[4] * delta_y * delta_y
    coverage = (feature[5] * live_mask)[None, :] * jnp.exp(-0.5 * quadric)
    log_pass = jnp.log1p(-coverage)
    positions = jnp.arange(live_mask.shape[0])
    earlier = (positions[:, None] < positions[None, :]).astype(jnp.float32)
    prefix = jnp.dot(log_pass, earlier, precision=lax.Precision.HIGHEST)
    weights = coverage * jnp.exp(prefix)
    shaded = lax.dot_general(feature[6:9], weights, (((1,), (1,)), ((), ())), precision=lax.Precision.HIGHEST)
    remain = jnp.exp(lax.optimization_barrier(jnp.sum(log_pass, axis=1)))
    return shaded + background[:, None] * remain[None, :]

def tile_grads(feature, live_mask, pixel_x, pixel_y, background, cotangent):
    unused, pullback = jax.vjp(lambda values: render_tile(values, live_mask, pixel_x, pixel_y, background), feature)
    return pullback(cotangent)[0]

def grads_for_tiles(features, live_mask, pixel_x, pixel_y, background, cotangent):
    pair_count = features.shape[0] // 2

    def one_group(blocks):
        return jax.vmap(tile_grads, in_axes=(0, 0, 0, 0, None, 0))(blocks[0], blocks[1], blocks[2], blocks[3], background, blocks[4])
    grouped = tuple((member.reshape((pair_count, 2) + member.shape[1:]) for member in (features, live_mask, pixel_x, pixel_y, cotangent)))
    stacked = lax.map(one_group, grouped)
    return stacked.reshape(features.shape)

def pixel_grid(first_tile, tile_count, tiles_total):
    tile_ids = first_tile + jnp.arange(tile_count)
    tile_row = tile_ids // TX
    tile_col = tile_ids % TX
    height = tiles_total // TX
    within = jnp.arange(SIDE * SIDE)
    local_row = within // SIDE
    local_col = within % SIDE
    pixel_x = ((tile_col[:, None] * SIDE + local_col[None, :]).astype(jnp.float32) + 0.5) / (TX * SIDE) * 2.0 - 1.0
    pixel_y = ((tile_row[:, None] * SIDE + local_row[None, :]).astype(jnp.float32) + 0.5) / (height * SIDE) * 2.0 - 1.0
    return (pixel_x, pixel_y)

def reference(gauss_params, camera, background, tile_lists, tile_lengths, pixel_cotangent):
    gradient = jnp.zeros(gauss_params.shape, jnp.float32)
    pixel_x, pixel_y = pixel_grid(0, TILES, TILES)
    for view_index in range(VIEWS):
        view_camera = camera[view_index]
        all_feats, own_back = jax.vjp(lambda values: project(values, view_camera), gauss_params)
        listed = tile_lists[view_index]
        live_mask = (jnp.arange(SLOTS)[None, :] < tile_lengths[view_index][:, None]).astype(jnp.float32)
        slot_feats = jnp.transpose(all_feats[:, listed], (1, 0, 2))
        cotangent = jnp.transpose(pixel_cotangent[view_index], (1, 0, 2))
        slot_grads = grads_for_tiles(slot_feats, live_mask, pixel_x, pixel_y, background, cotangent)
        flat_grads = jnp.transpose(slot_grads, (1, 0, 2)).reshape(9, -1)
        summed = jnp.zeros(all_feats.shape, jnp.float32).at[:, listed.reshape(-1)].add(flat_grads)
        gradient = gradient + own_back(summed)[0]
    return gradient
```

```python
import functools

import jax
import jax.numpy as jnp
from jax import lax
from jax.experimental import pallas as pl
from jax.experimental.pallas import tpu as pltpu
from jax.sharding import PartitionSpec as P

SIDE = 16
TX = 16
PIX = 256
SLOTS = 256
TILES_DEV = 4
OWNERS = 128
CAP = 16
LANES = 128
G_DEV = 8192
GROUPS = G_DEV // LANES
PARAMS = 59
PITCH = 64
CHUNKS = 8
CHUNK = G_DEV // CHUNKS
FEATS = 9
PACK = 256

FOCAL = 2.0
DILATION = 0.0001
SH_ZERO = 0.28209479177387814
SH_ONE = 0.4886025119029199
SH_TWO = (
    1.0925484305920792,
    -1.0925484305920792,
    0.31539156525252005,
    -1.0925484305920792,
    0.5462742152960396,
)
SH_THREE = (
    -0.5900435899266435,
    2.890611442640554,
    -0.4570457994644658,
    0.3731763325901154,
    -0.4570457994644658,
    1.445305721320277,
    -0.5900435899266435,
)

F32 = jnp.float32
BF16 = jnp.bfloat16
VMEM_LIMIT = 32 * 1024 * 1024


def iota(shape, axis, dtype=jnp.int32):
    return lax.broadcasted_iota(dtype, shape, axis)


def spread(row, shape):
    return jnp.broadcast_to(row, shape)


def halves(values):
    high = values.astype(BF16)
    low = (values - high.astype(F32)).astype(BF16)
    return high, low


def dot(left, right):
    return jnp.dot(left, right, preferred_element_type=F32)


def dot_lanes(left, right):
    return lax.dot_general(left, right, (((1,), (1,)), ((), ())), preferred_element_type=F32)


def camera_rows(camera_ref):
    row = iota((8, LANES), 0)
    block = jnp.zeros((8, LANES), F32)
    for index in range(6):
        block = jnp.where(row == index, camera_ref[0, index], block)
    return block


def rotation(block):
    cosines, sines = jnp.cos(block), jnp.sin(block)

    def take(values, index):
        return spread(values[index : index + 1, :], (8, LANES))

    cx, cy, cz = (take(cosines, index) for index in range(3))
    sx, sy, sz = (take(sines, index) for index in range(3))
    inner = [
        [cy, sy * sx, sy * cx],
        [None, cx, -sx],
        [-sy, cy * sx, cy * cx],
    ]
    rotate = [
        [cz * inner[0][0], cz * inner[0][1] - sz * inner[1][1], cz * inner[0][2] - sz * inner[1][2]],
        [sz * inner[0][0], sz * inner[0][1] + cz * inner[1][1], sz * inner[0][2] + cz * inner[1][2]],
        inner[2],
    ]
    offset = [take(block, 3 + index) for index in range(3)]
    return rotate, offset


def camera_center(rotate, offset):
    return [
        -(rotate[0][col] * offset[0] + rotate[1][col] * offset[1] + rotate[2][col] * offset[2])
        for col in range(3)
    ]


def shape_matrix(log_scales, quaternion):
    scales = [jnp.exp(value) for value in log_scales]
    norm = lax.rsqrt(
        quaternion[0] * quaternion[0]
        + quaternion[1] * quaternion[1]
        + quaternion[2] * quaternion[2]
        + quaternion[3] * quaternion[3]
    )
    real, im_i, im_j, im_k = (part * norm for part in quaternion)
    local = [
        [1.0 - 2.0 * (im_j * im_j + im_k * im_k), 2.0 * (im_i * im_j - real * im_k), 2.0 * (im_i * im_k + real * im_j)],
        [2.0 * (im_i * im_j + real * im_k), 1.0 - 2.0 * (im_i * im_i + im_k * im_k), 2.0 * (im_j * im_k - real * im_i)],
        [2.0 * (im_i * im_k - real * im_j), 2.0 * (im_j * im_k + real * im_i), 1.0 - 2.0 * (im_i * im_i + im_j * im_j)],
    ]
    return [[local[row][col] * scales[col] for col in range(3)] for row in range(3)]


def harmonics(along_x, along_y, along_z):
    square_x, square_y, square_z = along_x * along_x, along_y * along_y, along_z * along_z
    return [
        jnp.full_like(along_x, SH_ZERO),
        -SH_ONE * along_y,
        SH_ONE * along_z,
        -SH_ONE * along_x,
        SH_TWO[0] * along_x * along_y,
        SH_TWO[1] * along_y * along_z,
        SH_TWO[2] * (2.0 * square_z - square_x - square_y),
        SH_TWO[3] * along_x * along_z,
        SH_TWO[4] * (square_x - square_y),
        SH_THREE[0] * along_y * (3.0 * square_x - square_y),
        SH_THREE[1] * along_x * along_y * along_z,
        SH_THREE[2] * along_y * (4.0 * square_z - square_x - square_y),
        SH_THREE[3] * along_z * (2.0 * square_z - 3.0 * square_x - 3.0 * square_y),
        SH_THREE[4] * along_x * (4.0 * square_z - square_x - square_y),
        SH_THREE[5] * along_z * (square_x - square_y),
        SH_THREE[6] * along_x * (square_x - 3.0 * square_y),
    ]


def screen_features(center, shape, rotate, offset):
    viewed = [
        rotate[row][0] * center[0] + rotate[row][1] * center[1] + rotate[row][2] * center[2] + offset[row]
        for row in range(3)
    ]
    depth_inv = 1.0 / viewed[2]
    near = FOCAL * depth_inv
    screen_x = viewed[0] * near
    screen_y = viewed[1] * near
    slope_x = -screen_x * depth_inv
    slope_y = -screen_y * depth_inv
    to_camera = [
        [near * rotate[0][col] + slope_x * rotate[2][col] for col in range(3)],
        [near * rotate[1][col] + slope_y * rotate[2][col] for col in range(3)],
    ]
    mapped = [
        [
            to_camera[row][0] * shape[0][col] + to_camera[row][1] * shape[1][col] + to_camera[row][2] * shape[2][col]
            for col in range(3)
        ]
        for row in range(2)
    ]
    first, second = mapped
    cov_a = first[0] * first[0] + first[1] * first[1] + first[2] * first[2] + DILATION
    cov_b = first[0] * second[0] + first[1] * second[1] + first[2] * second[2]
    cov_c = second[0] * second[0] + second[1] * second[1] + second[2] * second[2] + DILATION
    inverse = 1.0 / (cov_a * cov_c - cov_b * cov_b)
    return [screen_x, screen_y, cov_c * inverse, -cov_b * inverse, cov_a * inverse]


def direction_basis(center, eye):
    toward = [center[index] - eye[index] for index in range(3)]
    norm = lax.rsqrt(toward[0] * toward[0] + toward[1] * toward[1] + toward[2] * toward[2])
    return harmonics(toward[0] * norm, toward[1] * norm, toward[2] * norm)


def spread_columns(params_ref, held_ref):
    for group in range(CHUNK // LANES):
        columns = slice(group * LANES, (group + 1) * LANES)
        held_ref[group * PITCH : group * PITCH + 56, :] = params_ref[0:56, columns]
        held_ref[group * PITCH + 56 : group * PITCH + PARAMS, :] = params_ref[56:PARAMS, columns]


def project_kernel(camera_ref, params_ref, feats_ref, held_ref):
    spread_columns(params_ref, held_ref)

    def param(index):
        return held_ref[pl.ds(index, 8, stride=PITCH), :]

    rotate, offset = rotation(camera_rows(camera_ref))
    center = [param(index) for index in range(3)]
    shape = shape_matrix([param(3 + index) for index in range(3)], [param(6 + index) for index in range(4)])
    screen = screen_features(center, shape, rotate, offset)
    basis = direction_basis(center, camera_center(rotate, offset))
    opacity = 1.0 / (1.0 + jnp.exp(-param(10)))
    colors = []
    for channel in range(3):
        total = basis[0] * param(11 + channel)
        for term in range(1, 16):
            total = total + basis[term] * param(11 + 3 * term + channel)
        colors.append(total + 0.5)
    for index, value in enumerate(screen + [opacity] + colors):
        feats_ref[index] = value


def route_kernel(lists_ref, request_ref, aux_ref):
    owner_iota = iota((OWNERS, LANES), 0)
    before = (iota((LANES, 2 * LANES), 0) < iota((LANES, 2 * LANES), 1)).astype(F32)
    before = before.astype(BF16)
    rank_iota = iota((CAP, LANES), 0)
    lane = iota((1, LANES), 1)
    carried = jnp.zeros((OWNERS, LANES), F32)
    table = jnp.zeros((4 * CAP, OWNERS), F32)
    for row in range(8):
        ids = lists_ref[0, row // 2 : row // 2 + 1, (row % 2) * LANES : (row % 2 + 1) * LANES]
        owner = ids // G_DEV
        column = ids % G_DEV
        hot = owner_iota == spread(owner, (OWNERS, LANES))
        hot_f32 = hot.astype(F32)
        hot_bf16 = hot_f32.astype(BF16)
        counts = dot(hot_bf16, before)
        rank = jnp.sum(jnp.where(hot, counts[:, :LANES] + carried, 0.0), axis=0, keepdims=True)
        carried = carried + counts[:, LANES:]
        rank = rank.astype(jnp.int32)
        at_rank = rank_iota == spread(rank, (CAP, LANES))
        pieces = [column // LANES, column % LANES, lane * 0 + row, lane + 1]
        stacked = jnp.concatenate(
            [jnp.where(at_rank, spread(piece.astype(F32), (CAP, LANES)), 0.0) for piece in pieces], axis=0
        )
        table = table + dot_lanes(stacked.astype(BF16), hot_bf16)
        aux_ref[row : row + 1, :] = owner
        aux_ref[8 + row : 9 + row, :] = rank
    high, low, slot_row, slot_lane = (table[CAP * part : CAP * (part + 1)] for part in range(4))
    used = slot_lane > 0.5
    slot = jnp.where(used, slot_row * LANES + slot_lane - 1.0, -1.0)
    wanted = jnp.where(used, high * LANES + low, -1.0)
    aux_ref[16 : 16 + CAP, :] = slot.astype(jnp.int32)
    aux_ref[16 + CAP : 16 + 2 * CAP, :] = wanted.astype(jnp.int32)
    padded = jnp.concatenate([wanted, jnp.zeros((LANES - CAP, OWNERS), F32)], axis=0)
    request_ref[...] = padded.T.astype(jnp.int32)


def pick(row, lanes_at):
    return jnp.take_along_axis(spread(row, (8, LANES)), lanes_at, axis=1, mode="promise_in_bounds")


def store_rows(out_ref, table):
    out_ref[pl.ds(0, LANES, stride=2), :] = table[:LANES].T
    out_ref[pl.ds(1, LANES, stride=2), :] = table[LANES:].T


def gather_kernel(request_ref, feats_ref, out_ref):
    wanted = request_ref[...].astype(F32).T[:CAP].astype(jnp.int32)
    high, low = wanted >> 7, wanted & (LANES - 1)
    parts = [(high[:8], low[:8]), (high[8:], low[8:])]

    def step(group, found):
        found = list(found)
        for index in range(FEATS):
            row = feats_ref[index, pl.ds(group, 1), :]
            for part, (at_group, at_lane) in enumerate(parts):
                place = 2 * index + part
                found[place] = jnp.where(at_group == group, pick(row, at_lane), found[place])
        return tuple(found)

    start = tuple(jnp.zeros((8, LANES), F32) for _ in range(2 * FEATS))
    found = lax.fori_loop(0, GROUPS, step, start, unroll=8)
    table = jnp.concatenate(list(found) + [jnp.zeros((PACK - FEATS * CAP, LANES), F32)], axis=0)
    store_rows(out_ref, table)


PIX_CHUNK = 64


def render_kernel(
    height, lengths_ref, background_ref, camera_ref, first_ref, arrived_ref, aux_ref, cotangent_ref, out_ref,
    slot_ref, table_ref, grad_ref, pixel_ref, weight_ref,
):
    table_ref[:LANES, :] = arrived_ref[pl.ds(0, LANES, stride=2), :].T
    table_ref[LANES:, :] = arrived_ref[pl.ds(1, LANES, stride=2), :].T
    owner = aux_ref[0:8, :]
    rank = aux_ref[8:16, :]
    at_rank = [rank == place for place in range(CAP)]
    for index in range(FEATS):
        value = jnp.zeros((8, LANES), F32)
        for place in range(CAP):
            row = table_ref[index * CAP + place : index * CAP + place + 1, :]
            value = jnp.where(at_rank[place], pick(row, owner), value)
        slot_ref[index * 8 : index * 8 + 8, :] = value

    within = iota((PIX, SLOTS), 0)
    pixel_ref[0] = (within % SIDE).astype(F32) * (2.0 / (TX * SIDE))
    pixel_ref[1] = (within // SIDE).astype(F32) * (2.0 / (height * SIDE))
    slot_row, slot_col = iota((SLOTS, SLOTS), 0), iota((SLOTS, SLOTS), 1)
    weight_ref[0] = (slot_row < slot_col).astype(F32).astype(BF16)
    weight_ref[1] = (slot_row > slot_col).astype(F32).astype(BF16)
    slot_place = iota((1, SLOTS), 1)

    def tile(index, carry):
        def slots(feature):
            return jnp.concatenate(
                [slot_ref[pl.ds(feature * 8 + 2 * index + half, 1), :] for half in range(2)], axis=1
            )

        tile_id = first_ref[0] + index
        tile_x = ((tile_id % TX * SIDE).astype(F32) + 0.5) * (2.0 / (TX * SIDE)) - 1.0
        tile_y = ((tile_id // TX * SIDE).astype(F32) + 0.5) * (2.0 / (height * SIDE)) - 1.0
        at_x = slots(0) - tile_x
        at_y = slots(1) - tile_y
        conic_a, conic_b, conic_c = slots(2), slots(3), slots(4)
        opacity = slots(5)
        live_opacity = jnp.where(slot_place < lengths_ref[0, index], opacity, 0.0)
        colors = [slots(6 + channel) for channel in range(3)]
        half_a, full_b, half_c = -0.5 * conic_a, -conic_b, -0.5 * conic_c
        shades = [cotangent_ref[0, channel, pl.ds(index, 1), :] for channel in range(3)]
        behind = (
            shades[0] * background_ref[0] + shades[1] * background_ref[1] + shades[2] * background_ref[2]
        )
        columns = jnp.concatenate(shades + [behind, jnp.zeros((4, PIX), F32)], axis=0).T

        sums = [jnp.zeros((8, SLOTS), F32) for _ in range(9)]

        def fold(values):
            return jnp.sum(values.reshape(PIX_CHUNK // 8, 8, SLOTS), axis=0)

        for chunk in range(PIX // PIX_CHUNK):
            rows = slice(chunk * PIX_CHUNK, (chunk + 1) * PIX_CHUNK)
            shape = (PIX_CHUNK, SLOTS)
            delta_x = pixel_ref[0, rows, :] - at_x
            delta_y = pixel_ref[1, rows, :] - at_y
            exponent = (half_a * delta_x + full_b * delta_y) * delta_x + half_c * delta_y * delta_y
            coverage = live_opacity * jnp.exp(exponent)
            log_pass = jnp.log(1.0 - coverage)
            high, low = halves(log_pass)
            prefix = dot(high, weight_ref[0]) + dot(low, weight_ref[0])
            passed = jnp.exp(prefix)
            weight = coverage * passed
            shade = [spread(columns[rows, channel : channel + 1], shape) for channel in range(3)]
            gain = shade[0] * colors[0] + shade[1] * colors[1] + shade[2] * colors[2]
            product = weight * gain
            high, low = halves(product)
            later = dot(high, weight_ref[1]) + dot(low, weight_ref[1])
            remain = jnp.exp(prefix[:, SLOTS - 1 :] + log_pass[:, SLOTS - 1 :])
            later = later + spread(columns[rows, 3:4] * remain, shape)
            slope = -0.5 * (product - coverage / (1.0 - coverage) * later)
            slope_x = slope * delta_x
            slope_y = slope * delta_y
            parts = [slope, slope_x, slope_y, slope_x * delta_x, slope_x * delta_y, slope_y * delta_y]
            parts += [shade[channel] * weight for channel in range(3)]
            sums = [total + fold(part) for total, part in zip(sums, parts)]

        sums = [jnp.sum(total, axis=0, keepdims=True) for total in sums]
        total, sum_x, sum_y, sum_xx, sum_xy, sum_yy = sums[:6]
        grads = [
            -2.0 * (conic_a * sum_x + conic_b * sum_y),
            -2.0 * (conic_b * sum_x + conic_c * sum_y),
            sum_xx,
            2.0 * sum_xy,
            sum_yy,
            -2.0 * total / opacity,
        ] + sums[6:]
        for feature, value in enumerate(grads):
            for half in range(2):
                grad_ref[pl.ds(feature * 8 + 2 * index + half, 1), :] = value[:, half * LANES : (half + 1) * LANES]
        return carry

    lax.fori_loop(0, TILES_DEV, tile, 0)

    slot = aux_ref[16 : 16 + CAP, :]
    wanted = aux_ref[16 + CAP : 16 + 2 * CAP, :].astype(F32)
    parts = [(slot[8 * part : 8 * part + 8] >> 7, slot[8 * part : 8 * part + 8] & (LANES - 1)) for part in range(2)]
    blocks = []
    for feature in range(FEATS):
        for at_row, at_lane in parts:
            value = jnp.zeros((8, LANES), F32)
            for row in range(8):
                grads = grad_ref[feature * 8 + row : feature * 8 + row + 1, :]
                value = jnp.where(at_row == row, pick(grads, at_lane), value)
            blocks.append(value)
    blocks += [wanted, camera_rows(camera_ref), jnp.zeros((PACK - FEATS * CAP - CAP - 8, LANES), F32)]
    store_rows(out_ref, jnp.concatenate(blocks, axis=0))


WIDE = 256
TALL = G_DEV // WIDE


def scatter_view(view, arrived_ref, grads_ref, camera_ref):
    tall_iota = iota((TALL, LANES), 0)
    wide_iota = iota((WIDE, LANES), 0)
    first = arrived_ref[view, pl.ds(0, LANES, stride=2), :].T
    second = arrived_ref[view, pl.ds(1, LANES, stride=2), :].T
    rest = FEATS * CAP - LANES
    values = jnp.concatenate([first, second[:rest]], axis=0)
    wanted = second[rest : rest + CAP].astype(jnp.int32)
    camera_ref[view] = second[rest + CAP : rest + CAP + 8]
    high_place, low_place = wanted >> 8, wanted & (WIDE - 1)
    high, low = halves(values)
    high, low = high.astype(F32), low.astype(F32)
    lefts, rights = [], []
    for place in range(CAP):
        at_high = tall_iota == spread(high_place[place : place + 1], (TALL, LANES))
        at_low = wide_iota == spread(low_place[place : place + 1], (WIDE, LANES))
        at_low = at_low.astype(F32).astype(BF16)
        for source in (high, low):
            rows = [source[index * CAP + place : index * CAP + place + 1] for index in range(FEATS)]
            left = [jnp.where(at_high, spread(row, (TALL, LANES)), 0.0) for row in rows]
            lefts.append(jnp.concatenate(left, axis=0).astype(BF16))
            rights.append(at_low)
    total = dot_lanes(jnp.concatenate(lefts, axis=1), jnp.concatenate(rights, axis=1))
    for half in range(2):
        grads_ref[view, pl.ds(half, FEATS * TALL, stride=2), :] = total[:, half * LANES : (half + 1) * LANES]


def pullback_kernel(arrived_ref, params_ref, out_ref, held_ref, sums_ref, grads_ref, camera_ref):
    views = arrived_ref.shape[0]
    chunk = pl.program_id(0)

    @pl.when(chunk == 0)
    def scatter():
        def one_view(view, carry):
            scatter_view(view, arrived_ref, grads_ref, camera_ref)
            return carry

        lax.fori_loop(0, views, one_view, 0)

    spread_columns(params_ref, held_ref)

    def param(index):
        return held_ref[pl.ds(index, 8, stride=PITCH), :]

    def keep(index, value):
        sums_ref[pl.ds(index, 8, stride=PITCH), :] = value

    def kept(index):
        return sums_ref[pl.ds(index, 8, stride=PITCH), :]

    center = [param(index) for index in range(3)]
    shape, shape_back = jax.vjp(
        shape_matrix, [param(3 + index) for index in range(3)], [param(6 + index) for index in range(4)]
    )
    center_grad, shape_grad, opacity_grad = None, None, None
    for view in range(views):
        def cotangent(feature):
            return grads_ref[view, pl.ds(pl.multiple_of(feature * GROUPS + chunk * 8, 8), 8), :]

        rotate, offset = rotation(camera_ref[view])
        eye = camera_center(rotate, offset)
        basis, basis_back = jax.vjp(lambda place: direction_basis(place, eye), center)
        colors = [cotangent(6 + channel) for channel in range(3)]
        basis_grad = []
        for term in range(16):
            total = None
            for channel in range(3):
                index = 11 + 3 * term + channel
                piece = basis[term] * colors[channel]
                keep(index, piece if view == 0 else kept(index) + piece)
                piece = param(index) * colors[channel]
                total = piece if total is None else total + piece
            basis_grad.append(total)
        (along,) = basis_back(basis_grad)
        unused, screen_back = jax.vjp(
            lambda place, matrix: screen_features(place, matrix, rotate, offset), center, shape
        )
        moved, bent = screen_back([cotangent(index) for index in range(5)])
        pieces = [along[axis] + moved[axis] for axis in range(3)]
        faded = cotangent(5)
        if view == 0:
            center_grad, shape_grad, opacity_grad = pieces, bent, faded
        else:
            center_grad = [one + other for one, other in zip(center_grad, pieces)]
            shape_grad = [[one + other for one, other in zip(*rows)] for rows in zip(shape_grad, bent)]
            opacity_grad = opacity_grad + faded
    scale_grad, quaternion_grad = shape_back(shape_grad)
    opacity = 1.0 / (1.0 + jnp.exp(-param(10)))
    firsts = center_grad + list(scale_grad) + list(quaternion_grad) + [opacity * (1.0 - opacity) * opacity_grad]
    for index, value in enumerate(firsts):
        keep(index, value)
    for group in range(CHUNK // LANES):
        columns = slice(group * LANES, (group + 1) * LANES)
        out_ref[0:56, columns] = sums_ref[group * PITCH : group * PITCH + 56, :]
        out_ref[56:PARAMS, columns] = sums_ref[group * PITCH + 56 : group * PITCH + PARAMS, :]


def call(kernel, out_shape, operands, smalls=(), scratch=(), **kwargs):
    spaces = [pltpu.SMEM if index < smalls else pltpu.VMEM for index in range(len(operands))]
    single = not isinstance(out_shape, (list, tuple))
    outs = pl.BlockSpec(memory_space=pltpu.VMEM)
    return pl.pallas_call(
        kernel,
        out_shape=out_shape,
        in_specs=[pl.BlockSpec(memory_space=space) for space in spaces],
        out_specs=outs if single else [outs] * len(out_shape),
        scratch_shapes=list(scratch),
        compiler_params=pltpu.CompilerParams(vmem_limit_bytes=VMEM_LIMIT),
        **kwargs,
    )(*operands)


def route(tile_lists):
    return call(
        route_kernel,
        [jax.ShapeDtypeStruct((OWNERS, LANES), jnp.int32), jax.ShapeDtypeStruct((16 + 2 * CAP, LANES), jnp.int32)],
        [tile_lists],
        smalls=0,
    )


def project(camera, gauss_params):
    return pl.pallas_call(
        project_kernel,
        grid=(CHUNKS,),
        out_shape=jax.ShapeDtypeStruct((FEATS, GROUPS, LANES), F32),
        in_specs=[
            pl.BlockSpec(memory_space=pltpu.SMEM),
            pl.BlockSpec((PARAMS, CHUNK), lambda chunk: (0, chunk)),
        ],
        out_specs=pl.BlockSpec((FEATS, 8, LANES), lambda chunk: (0, chunk, 0)),
        scratch_shapes=[pltpu.VMEM((8 * PITCH, LANES), F32)],
        compiler_params=pltpu.CompilerParams(vmem_limit_bytes=VMEM_LIMIT),
    )(camera, gauss_params)


def gather(requested, features):
    return call(
        gather_kernel, jax.ShapeDtypeStruct((2 * OWNERS, LANES), F32), [requested, features], smalls=0
    )


def render(height, tile_lengths, background, camera, first_tile, arrived, aux, cotangent):
    return call(
        functools.partial(render_kernel, height),
        jax.ShapeDtypeStruct((2 * OWNERS, LANES), F32),
        [tile_lengths, background, camera, first_tile, arrived, aux, cotangent],
        smalls=4,
        scratch=[
            pltpu.VMEM((FEATS * 8, LANES), F32),
            pltpu.VMEM((2 * OWNERS, LANES), F32),
            pltpu.VMEM((FEATS * 8, LANES), F32),
            pltpu.VMEM((2, PIX, SLOTS), F32),
            pltpu.VMEM((2, SLOTS, SLOTS), BF16),
        ],
    )


def pullback(arrived, gauss_params):
    views = arrived.shape[0]
    return pl.pallas_call(
        pullback_kernel,
        grid=(CHUNKS,),
        out_shape=jax.ShapeDtypeStruct((PARAMS, G_DEV), F32),
        in_specs=[
            pl.BlockSpec((views, 2 * OWNERS, LANES), lambda chunk: (0, 0, 0)),
            pl.BlockSpec((PARAMS, CHUNK), lambda chunk: (0, chunk)),
        ],
        out_specs=pl.BlockSpec((PARAMS, CHUNK), lambda chunk: (0, chunk)),
        scratch_shapes=[
            pltpu.VMEM((8 * PITCH, LANES), F32),
            pltpu.VMEM((8 * PITCH, LANES), F32),
            pltpu.VMEM((views, FEATS * GROUPS, LANES), F32),
            pltpu.VMEM((views, 8, LANES), F32),
        ],
        compiler_params=pltpu.CompilerParams(vmem_limit_bytes=VMEM_LIMIT),
    )(arrived, gauss_params)


def per_device(gauss_params, camera, background, tile_lists, tile_lengths, pixel_cotangent):
    owners_total = lax.axis_size("img")
    views = lax.axis_size("view")
    tiles_here = tile_lists.shape[1]
    height = tiles_here * owners_total // TX
    first_tile = (lax.axis_index("img") * tiles_here).astype(jnp.int32).reshape(1)
    requests, aux = route(tile_lists)
    features = project(camera, gauss_params)
    requested = lax.all_to_all(requests, "img", split_axis=0, concat_axis=0, tiled=True)
    outgoing = gather(requested, features)
    arrived = lax.all_to_all(outgoing, "img", split_axis=0, concat_axis=0, tiled=True)
    slot_grads = render(
        height, tile_lengths, background, camera, first_tile, arrived, aux, pixel_cotangent
    )
    returned = lax.all_to_all(slot_grads, "img", split_axis=0, concat_axis=0, tiled=True)
    copies = jnp.broadcast_to(returned[None], (views,) + returned.shape)
    everyone = lax.all_to_all(copies, "view", split_axis=0, concat_axis=0, tiled=True)
    return pullback(everyone, gauss_params)


def solution(mesh):
    placed = (
        P(None, "img"),
        P("view", None),
        P(),
        P("view", "img", None),
        P("view", "img"),
        P("view", None, "img", None),
    )
    return jax.shard_map(
        per_device, mesh=mesh, in_specs=placed, out_specs=P(None, "img"), check_vma=False
    )
```

```python
import functools

import jax
import jax.numpy as jnp
from jax import lax
from jax.experimental import pallas as pl
from jax.experimental.pallas import tpu as pltpu
from jax.sharding import PartitionSpec as P

SIDE = 16
TX = 16
PIX = 256
SLOTS = 256
TILES_DEV = 4
OWNERS = 128
CAP = 16
LANES = 128
G_DEV = 8192
GROUPS = G_DEV // LANES
PARAMS = 59
PITCH = 65
CHUNKS = 8
CHUNK = G_DEV // CHUNKS
FEATS = 9
PACK = 256

FOCAL = 2.0
DILATION = 0.0001
SH_ZERO = 0.28209479177387814
SH_ONE = 0.4886025119029199
SH_TWO = (
    1.0925484305920792,
    -1.0925484305920792,
    0.31539156525252005,
    -1.0925484305920792,
    0.5462742152960396,
)
SH_THREE = (
    -0.5900435899266435,
    2.890611442640554,
    -0.4570457994644658,
    0.3731763325901154,
    -0.4570457994644658,
    1.445305721320277,
    -0.5900435899266435,
)

F32 = jnp.float32
BF16 = jnp.bfloat16
VMEM_LIMIT = 32 * 1024 * 1024


def iota(shape, axis, dtype=jnp.int32):
    return lax.broadcasted_iota(dtype, shape, axis)


def spread(row, shape):
    return jnp.broadcast_to(row, shape)


def halves(values):
    high = values.astype(BF16)
    low = (values - high.astype(F32)).astype(BF16)
    return high, low


def dot(left, right):
    return jnp.dot(left, right, preferred_element_type=F32)


def dot_lanes(left, right):
    return lax.dot_general(left, right, (((1,), (1,)), ((), ())), preferred_element_type=F32)


GEO = 24


def write_geometry(geo_ref, camera_ref, first_ref, height):
    row = iota((8, LANES), 0)
    block = jnp.zeros((8, LANES), F32)
    for index in range(6):
        block = jnp.where(row == index, camera_ref[0, index], block)
    cosines, sines = jnp.cos(block), jnp.sin(block)
    cx, cy, cz = (cosines[index : index + 1, :] for index in range(3))
    sx, sy, sz = (sines[index : index + 1, :] for index in range(3))
    inner = [
        [cy, sy * sx, sy * cx],
        [None, cx, -sx],
        [-sy, cy * sx, cy * cx],
    ]
    entries = [
        [cz * inner[0][0], cz * inner[0][1] - sz * inner[1][1], cz * inner[0][2] - sz * inner[1][2]],
        [sz * inner[0][0], sz * inner[0][1] + cz * inner[1][1], sz * inner[0][2] + cz * inner[1][2]],
        inner[2],
    ]
    for index, value in enumerate(entries[0] + entries[1] + entries[2]):
        geo_ref[index : index + 1, :] = value
    geo_ref[9:12, :] = block[3:6, :]
    for index in range(TILES_DEV):
        tile_id = first_ref[0] + index
        tile_x = ((tile_id % TX * SIDE).astype(F32) + 0.5) * (2.0 / (TX * SIDE)) - 1.0
        tile_y = ((tile_id // TX * SIDE).astype(F32) + 0.5) * (2.0 / (height * SIDE)) - 1.0
        geo_ref[12 + index : 13 + index, :] = jnp.full((1, LANES), tile_x, F32)
        geo_ref[16 + index : 17 + index, :] = jnp.full((1, LANES), tile_y, F32)
    geo_ref[20:GEO, :] = jnp.zeros((GEO - 20, LANES), F32)


def camera_of(geo):
    entries = [spread(geo[index : index + 1, :], (8, LANES)) for index in range(12)]
    return [entries[0:3], entries[3:6], entries[6:9]], entries[9:12]


def camera_center(rotate, offset):
    return [
        -(rotate[0][col] * offset[0] + rotate[1][col] * offset[1] + rotate[2][col] * offset[2])
        for col in range(3)
    ]


def shape_matrix(log_scales, quaternion):
    scales = [jnp.exp(value) for value in log_scales]
    norm = lax.rsqrt(
        quaternion[0] * quaternion[0]
        + quaternion[1] * quaternion[1]
        + quaternion[2] * quaternion[2]
        + quaternion[3] * quaternion[3]
    )
    real, im_i, im_j, im_k = (part * norm for part in quaternion)
    local = [
        [1.0 - 2.0 * (im_j * im_j + im_k * im_k), 2.0 * (im_i * im_j - real * im_k), 2.0 * (im_i * im_k + real * im_j)],
        [2.0 * (im_i * im_j + real * im_k), 1.0 - 2.0 * (im_i * im_i + im_k * im_k), 2.0 * (im_j * im_k - real * im_i)],
        [2.0 * (im_i * im_k - real * im_j), 2.0 * (im_j * im_k + real * im_i), 1.0 - 2.0 * (im_i * im_i + im_j * im_j)],
    ]
    return [[local[row][col] * scales[col] for col in range(3)] for row in range(3)]


def harmonics(along_x, along_y, along_z):
    square_x, square_y, square_z = along_x * along_x, along_y * along_y, along_z * along_z
    return [
        jnp.full_like(along_x, SH_ZERO),
        -SH_ONE * along_y,
        SH_ONE * along_z,
        -SH_ONE * along_x,
        SH_TWO[0] * along_x * along_y,
        SH_TWO[1] * along_y * along_z,
        SH_TWO[2] * (2.0 * square_z - square_x - square_y),
        SH_TWO[3] * along_x * along_z,
        SH_TWO[4] * (square_x - square_y),
        SH_THREE[0] * along_y * (3.0 * square_x - square_y),
        SH_THREE[1] * along_x * along_y * along_z,
        SH_THREE[2] * along_y * (4.0 * square_z - square_x - square_y),
        SH_THREE[3] * along_z * (2.0 * square_z - 3.0 * square_x - 3.0 * square_y),
        SH_THREE[4] * along_x * (4.0 * square_z - square_x - square_y),
        SH_THREE[5] * along_z * (square_x - square_y),
        SH_THREE[6] * along_x * (square_x - 3.0 * square_y),
    ]


def screen_features(center, shape, rotate, offset):
    viewed = [
        rotate[row][0] * center[0] + rotate[row][1] * center[1] + rotate[row][2] * center[2] + offset[row]
        for row in range(3)
    ]
    depth_inv = 1.0 / viewed[2]
    near = FOCAL * depth_inv
    screen_x = viewed[0] * near
    screen_y = viewed[1] * near
    slope_x = -screen_x * depth_inv
    slope_y = -screen_y * depth_inv
    to_camera = [
        [near * rotate[0][col] + slope_x * rotate[2][col] for col in range(3)],
        [near * rotate[1][col] + slope_y * rotate[2][col] for col in range(3)],
    ]
    mapped = [
        [
            to_camera[row][0] * shape[0][col] + to_camera[row][1] * shape[1][col] + to_camera[row][2] * shape[2][col]
            for col in range(3)
        ]
        for row in range(2)
    ]
    first, second = mapped
    cov_a = first[0] * first[0] + first[1] * first[1] + first[2] * first[2] + DILATION
    cov_b = first[0] * second[0] + first[1] * second[1] + first[2] * second[2]
    cov_c = second[0] * second[0] + second[1] * second[1] + second[2] * second[2] + DILATION
    inverse = 1.0 / (cov_a * cov_c - cov_b * cov_b)
    return [screen_x, screen_y, cov_c * inverse, -cov_b * inverse, cov_a * inverse]


def direction_basis(center, eye):
    toward = [center[index] - eye[index] for index in range(3)]
    norm = lax.rsqrt(toward[0] * toward[0] + toward[1] * toward[1] + toward[2] * toward[2])
    return harmonics(toward[0] * norm, toward[1] * norm, toward[2] * norm)


def chunk_columns(chunk):
    return pl.ds(pl.multiple_of(chunk * CHUNK, CHUNK), CHUNK)


def spread_columns(params_ref, held_ref, chunk):
    for group in range(CHUNK // LANES):
        columns = pl.ds(pl.multiple_of(chunk * CHUNK + group * LANES, LANES), LANES)
        held_ref[group * PITCH : group * PITCH + PARAMS, :] = params_ref[:, columns]


def project_kernel(params_ref, geo_ref, feats_ref, staged_ref, held_ref, semaphores):
    def fetch(chunk):
        columns = chunk_columns(chunk)
        return pltpu.make_async_copy(params_ref.at[:, columns], staged_ref.at[:, columns], semaphores.at[chunk])

    def start(chunk, carry):
        fetch(chunk).start()
        return carry

    lax.fori_loop(0, CHUNKS, start, 0)
    rotate, offset = camera_of(geo_ref[...])
    eye = camera_center(rotate, offset)

    def step(chunk, carry):
        fetch(chunk).wait()
        spread_columns(staged_ref, held_ref, chunk)

        def param(index):
            return held_ref[pl.ds(index, 8, stride=PITCH), :]

        center = [param(index) for index in range(3)]
        shape = shape_matrix([param(3 + index) for index in range(3)], [param(6 + index) for index in range(4)])
        screen = screen_features(center, shape, rotate, offset)
        basis = direction_basis(center, eye)
        opacity = 1.0 / (1.0 + jnp.exp(-param(10)))
        colors = []
        for channel in range(3):
            total = basis[0] * param(11 + channel)
            for term in range(1, 16):
                total = total + basis[term] * param(11 + 3 * term + channel)
            colors.append(total + 0.5)
        rows = pl.ds(pl.multiple_of(chunk * 8, 8), 8)
        for index, value in enumerate(screen + [opacity] + colors):
            feats_ref[index, rows, :] = value
        return carry

    lax.fori_loop(0, CHUNKS, step, 0)


def route_kernel(height, camera_ref, first_ref, lists_ref, request_ref, aux_ref, geo_ref):
    write_geometry(geo_ref, camera_ref, first_ref, height)
    owner_iota = iota((OWNERS, LANES), 0)
    before = (iota((LANES, 2 * LANES), 0) < iota((LANES, 2 * LANES), 1)).astype(F32)
    before = before.astype(BF16)
    rank_iota = iota((CAP, LANES), 0)
    lane = iota((1, LANES), 1)
    carried = jnp.zeros((OWNERS, LANES), F32)
    table = jnp.zeros((4 * CAP, OWNERS), F32)
    for row in range(8):
        ids = lists_ref[0, row // 2 : row // 2 + 1, (row % 2) * LANES : (row % 2 + 1) * LANES]
        owner = ids // G_DEV
        column = ids % G_DEV
        hot = owner_iota == spread(owner, (OWNERS, LANES))
        hot_f32 = hot.astype(F32)
        hot_bf16 = hot_f32.astype(BF16)
        counts = dot(hot_bf16, before)
        rank = jnp.sum(jnp.where(hot, counts[:, :LANES] + carried, 0.0), axis=0, keepdims=True)
        carried = carried + counts[:, LANES:]
        rank = rank.astype(jnp.int32)
        at_rank = rank_iota == spread(rank, (CAP, LANES))
        pieces = [column // LANES, column % LANES, lane * 0 + row, lane + 1]
        stacked = jnp.concatenate(
            [jnp.where(at_rank, spread(piece.astype(F32), (CAP, LANES)), 0.0) for piece in pieces], axis=0
        )
        table = table + dot_lanes(stacked.astype(BF16), hot_bf16)
        aux_ref[row : row + 1, :] = owner
        aux_ref[8 + row : 9 + row, :] = rank
    high, low, slot_row, slot_lane = (table[CAP * part : CAP * (part + 1)] for part in range(4))
    used = slot_lane > 0.5
    slot = jnp.where(used, slot_row * LANES + slot_lane - 1.0, -1.0)
    wanted = jnp.where(used, high * LANES + low, -1.0)
    aux_ref[16 : 16 + CAP, :] = slot.astype(jnp.int32)
    aux_ref[16 + CAP : 16 + 2 * CAP, :] = wanted.astype(jnp.int32)
    padded = jnp.concatenate([wanted, jnp.zeros((LANES - CAP, OWNERS), F32)], axis=0)
    request_ref[...] = padded.T.astype(jnp.int32)


LANE_GATHER = lax.GatherDimensionNumbers(
    offset_dims=(),
    collapsed_slice_dims=(1,),
    start_index_map=(1,),
    operand_batching_dims=(0,),
    start_indices_batching_dims=(0,),
)


def pick(row, lanes_at):
    return lax.gather(
        spread(row, (8, LANES)),
        lanes_at[:, :, None],
        LANE_GATHER,
        slice_sizes=(1, 1),
        mode=lax.GatherScatterMode.PROMISE_IN_BOUNDS,
    )


def store_rows(out_ref, table):
    out_ref[pl.ds(0, LANES, stride=2), :] = table[:LANES].T
    out_ref[pl.ds(1, LANES, stride=2), :] = table[LANES:].T


def gather_kernel(request_ref, feats_ref, out_ref):
    wanted = request_ref[...].astype(F32).T[:CAP].astype(jnp.int32)
    high, low = wanted >> 7, wanted & (LANES - 1)
    parts = [(high[:8], low[:8]), (high[8:], low[8:])]

    def step(group, found):
        found = list(found)
        for index in range(FEATS):
            row = feats_ref[index, pl.ds(group, 1), :]
            for part, (at_group, at_lane) in enumerate(parts):
                place = 2 * index + part
                found[place] = jnp.where(at_group == group, pick(row, at_lane), found[place])
        return tuple(found)

    start = tuple(jnp.zeros((8, LANES), F32) for _ in range(2 * FEATS))
    found = lax.fori_loop(0, GROUPS, step, start, unroll=8)
    table = jnp.concatenate(list(found) + [jnp.zeros((PACK - FEATS * CAP, LANES), F32)], axis=0)
    store_rows(out_ref, table)


PIX_CHUNK = 64


def render_kernel(
    height, lengths_ref, background_ref, geo_ref, arrived_ref, aux_ref, cotangent_ref, out_ref,
    slot_ref, table_ref, grad_ref, pixel_ref, weight_ref,
):
    table_ref[:LANES, :] = arrived_ref[pl.ds(0, LANES, stride=2), :].T
    table_ref[LANES:, :] = arrived_ref[pl.ds(1, LANES, stride=2), :].T
    owner = aux_ref[0:8, :]
    rank = aux_ref[8:16, :]
    at_rank = [rank == place for place in range(CAP)]
    for index in range(FEATS):
        value = jnp.zeros((8, LANES), F32)
        for place in range(CAP):
            row = table_ref[index * CAP + place : index * CAP + place + 1, :]
            value = jnp.where(at_rank[place], pick(row, owner), value)
        slot_ref[index * 8 : index * 8 + 8, :] = value

    within = iota((PIX, SLOTS), 0)
    pixel_ref[0] = (within % SIDE).astype(F32) * (2.0 / (TX * SIDE))
    pixel_ref[1] = (within // SIDE).astype(F32) * (2.0 / (height * SIDE))
    slot_row, slot_col = iota((SLOTS, SLOTS), 0), iota((SLOTS, SLOTS), 1)
    weight_ref[0] = (slot_row < slot_col).astype(F32).astype(BF16)
    weight_ref[1] = (slot_row > slot_col).astype(F32).astype(BF16)
    slot_place = iota((1, SLOTS), 1)

    def tile(index, carry):
        def slots(feature):
            return jnp.concatenate(
                [slot_ref[pl.ds(feature * 8 + 2 * index + half, 1), :] for half in range(2)], axis=1
            )

        tile_x, tile_y = geo_ref[pl.ds(12 + index, 1), :], geo_ref[pl.ds(16 + index, 1), :]
        at_x = slots(0) - jnp.concatenate([tile_x] * 2, axis=1)
        at_y = slots(1) - jnp.concatenate([tile_y] * 2, axis=1)
        conic_a, conic_b, conic_c = slots(2), slots(3), slots(4)
        opacity = slots(5)
        live_opacity = jnp.where(slot_place < lengths_ref[0, index], opacity, 0.0)
        colors = [slots(6 + channel) for channel in range(3)]
        half_a, full_b, half_c = -0.5 * conic_a, -conic_b, -0.5 * conic_c
        shades = [cotangent_ref[0, channel, pl.ds(index, 1), :] for channel in range(3)]
        behind = (
            shades[0] * background_ref[0] + shades[1] * background_ref[1] + shades[2] * background_ref[2]
        )
        columns = jnp.concatenate(shades + [behind, jnp.zeros((4, PIX), F32)], axis=0).T

        sums = [jnp.zeros((8, SLOTS), F32) for _ in range(9)]

        def fold(values):
            return jnp.sum(values.reshape(PIX_CHUNK // 8, 8, SLOTS), axis=0)

        for chunk in range(PIX // PIX_CHUNK):
            rows = slice(chunk * PIX_CHUNK, (chunk + 1) * PIX_CHUNK)
            shape = (PIX_CHUNK, SLOTS)
            delta_x = pixel_ref[0, rows, :] - at_x
            delta_y = pixel_ref[1, rows, :] - at_y
            exponent = (half_a * delta_x + full_b * delta_y) * delta_x + half_c * delta_y * delta_y
            coverage = live_opacity * jnp.exp(exponent)
            log_pass = jnp.log(1.0 - coverage)
            high, low = halves(log_pass)
            prefix = dot(high, weight_ref[0]) + dot(low, weight_ref[0])
            passed = jnp.exp(prefix)
            weight = coverage * passed
            shade = [spread(columns[rows, channel : channel + 1], shape) for channel in range(3)]
            gain = shade[0] * colors[0] + shade[1] * colors[1] + shade[2] * colors[2]
            product = weight * gain
            high, low = halves(product)
            later = dot(high, weight_ref[1]) + dot(low, weight_ref[1])
            remain = jnp.exp(prefix[:, SLOTS - 1 :] + log_pass[:, SLOTS - 1 :])
            later = later + spread(columns[rows, 3:4] * remain, shape)
            slope = -0.5 * (product - coverage / (1.0 - coverage) * later)
            slope_x = slope * delta_x
            slope_y = slope * delta_y
            parts = [slope, slope_x, slope_y, slope_x * delta_x, slope_x * delta_y, slope_y * delta_y]
            parts += [shade[channel] * weight for channel in range(3)]
            sums = [total + fold(part) for total, part in zip(sums, parts)]

        sums = [jnp.sum(total, axis=0, keepdims=True) for total in sums]
        total, sum_x, sum_y, sum_xx, sum_xy, sum_yy = sums[:6]
        grads = [
            -2.0 * (conic_a * sum_x + conic_b * sum_y),
            -2.0 * (conic_b * sum_x + conic_c * sum_y),
            sum_xx,
            2.0 * sum_xy,
            sum_yy,
            -2.0 * total / opacity,
        ] + sums[6:]
        for feature, value in enumerate(grads):
            for half in range(2):
                grad_ref[pl.ds(feature * 8 + 2 * index + half, 1), :] = value[:, half * LANES : (half + 1) * LANES]
        return carry

    lax.fori_loop(0, TILES_DEV, tile, 0)

    slot = aux_ref[16 : 16 + CAP, :]
    wanted = aux_ref[16 + CAP : 16 + 2 * CAP, :].astype(F32)
    parts = [(slot[8 * part : 8 * part + 8] >> 7, slot[8 * part : 8 * part + 8] & (LANES - 1)) for part in range(2)]
    blocks = []
    for feature in range(FEATS):
        for at_row, at_lane in parts:
            value = jnp.zeros((8, LANES), F32)
            for row in range(8):
                grads = grad_ref[feature * 8 + row : feature * 8 + row + 1, :]
                value = jnp.where(at_row == row, pick(grads, at_lane), value)
            blocks.append(value)
    blocks += [wanted, geo_ref[0:16, :], jnp.zeros((PACK - FEATS * CAP - CAP - 16, LANES), F32)]
    store_rows(out_ref, jnp.concatenate(blocks, axis=0))


WIDE = 256
TALL = G_DEV // WIDE


def scatter_view(view, arrived_ref, grads_ref, camera_ref):
    tall_iota = iota((TALL, LANES), 0)
    wide_iota = iota((WIDE, LANES), 0)
    first = arrived_ref[view, pl.ds(0, LANES, stride=2), :].T
    second = arrived_ref[view, pl.ds(1, LANES, stride=2), :].T
    rest = FEATS * CAP - LANES
    values = jnp.concatenate([first, second[:rest]], axis=0)
    wanted = second[rest : rest + CAP].astype(jnp.int32)
    camera_ref[view] = second[rest + CAP : rest + CAP + 16]
    high_place, low_place = wanted >> 8, wanted & (WIDE - 1)
    high, low = halves(values)
    high, low = high.astype(F32), low.astype(F32)
    lefts, rights = [], []
    for place in range(CAP):
        at_high = tall_iota == spread(high_place[place : place + 1], (TALL, LANES))
        at_low = wide_iota == spread(low_place[place : place + 1], (WIDE, LANES))
        at_low = at_low.astype(F32).astype(BF16)
        for source in (high, low):
            rows = [source[index * CAP + place : index * CAP + place + 1] for index in range(FEATS)]
            left = [jnp.where(at_high, spread(row, (TALL, LANES)), 0.0) for row in rows]
            lefts.append(jnp.concatenate(left, axis=0).astype(BF16))
            rights.append(at_low)
    total = dot_lanes(jnp.concatenate(lefts, axis=1), jnp.concatenate(rights, axis=1))
    for half in range(2):
        grads_ref[view, pl.ds(half, FEATS * TALL, stride=2), :] = total[:, half * LANES : (half + 1) * LANES]


def pullback_kernel(
    arrived_ref, params_ref, out_ref, held_ref, sums_ref, grads_ref, camera_ref, staged_ref, semaphores
):
    views = arrived_ref.shape[0]

    def one_view(view, carry):
        scatter_view(view, arrived_ref, grads_ref, camera_ref)
        return carry

    lax.fori_loop(0, views, one_view, 0)

    def send(chunk):
        columns = chunk_columns(chunk)
        return pltpu.make_async_copy(staged_ref.at[:, columns], out_ref.at[:, columns], semaphores.at[chunk])

    def param(index):
        return held_ref[pl.ds(index, 8, stride=PITCH), :]

    def keep(index, value):
        sums_ref[pl.ds(index, 8, stride=PITCH), :] = value

    def kept(index):
        return sums_ref[pl.ds(index, 8, stride=PITCH), :]

    def step(chunk, carry):
        spread_columns(params_ref, held_ref, chunk)
        center = [param(index) for index in range(3)]
        shape, shape_back = jax.vjp(
            shape_matrix, [param(3 + index) for index in range(3)], [param(6 + index) for index in range(4)]
        )
        center_grad, shape_grad, opacity_grad = None, None, None
        for view in range(views):
            def cotangent(feature):
                return grads_ref[view, pl.ds(pl.multiple_of(feature * GROUPS + chunk * 8, 8), 8), :]

            rotate, offset = camera_of(camera_ref[view])
            eye = camera_center(rotate, offset)
            basis, basis_back = jax.vjp(lambda place: direction_basis(place, eye), center)
            colors = [cotangent(6 + channel) for channel in range(3)]
            basis_grad = []
            for term in range(16):
                total = None
                for channel in range(3):
                    index = 11 + 3 * term + channel
                    piece = basis[term] * colors[channel]
                    keep(index, piece if view == 0 else kept(index) + piece)
                    piece = param(index) * colors[channel]
                    total = piece if total is None else total + piece
                basis_grad.append(total)
            (along,) = basis_back(basis_grad)
            unused, screen_back = jax.vjp(
                lambda place, matrix: screen_features(place, matrix, rotate, offset), center, shape
            )
            moved, bent = screen_back([cotangent(index) for index in range(5)])
            pieces = [along[axis] + moved[axis] for axis in range(3)]
            faded = cotangent(5)
            if view == 0:
                center_grad, shape_grad, opacity_grad = pieces, bent, faded
            else:
                center_grad = [one + other for one, other in zip(center_grad, pieces)]
                shape_grad = [[one + other for one, other in zip(*rows)] for rows in zip(shape_grad, bent)]
                opacity_grad = opacity_grad + faded
        scale_grad, quaternion_grad = shape_back(shape_grad)
        opacity = 1.0 / (1.0 + jnp.exp(-param(10)))
        firsts = center_grad + list(scale_grad) + list(quaternion_grad) + [opacity * (1.0 - opacity) * opacity_grad]
        for index, value in enumerate(firsts):
            keep(index, value)
        for group in range(CHUNK // LANES):
            columns = pl.ds(pl.multiple_of(chunk * CHUNK + group * LANES, LANES), LANES)
            staged_ref[:, columns] = sums_ref[group * PITCH : group * PITCH + PARAMS, :]
        send(chunk).start()
        return carry

    lax.fori_loop(0, CHUNKS, step, 0)

    def finish(chunk, carry):
        send(chunk).wait()
        return carry

    lax.fori_loop(0, CHUNKS, finish, 0)


def call(kernel, out_shape, operands, smalls=(), scratch=(), **kwargs):
    spaces = [pltpu.SMEM if index < smalls else pltpu.VMEM for index in range(len(operands))]
    single = not isinstance(out_shape, (list, tuple))
    outs = pl.BlockSpec(memory_space=pltpu.VMEM)
    return pl.pallas_call(
        kernel,
        out_shape=out_shape,
        in_specs=[pl.BlockSpec(memory_space=space) for space in spaces],
        out_specs=outs if single else [outs] * len(out_shape),
        scratch_shapes=list(scratch),
        compiler_params=pltpu.CompilerParams(vmem_limit_bytes=VMEM_LIMIT),
        **kwargs,
    )(*operands)


def route(height, camera, first_tile, tile_lists):
    return call(
        functools.partial(route_kernel, height),
        [
            jax.ShapeDtypeStruct((OWNERS, LANES), jnp.int32),
            jax.ShapeDtypeStruct((16 + 2 * CAP, LANES), jnp.int32),
            jax.ShapeDtypeStruct((GEO, LANES), F32),
        ],
        [camera, first_tile, tile_lists],
        smalls=2,
    )


def project(gauss_params, geometry):
    return pl.pallas_call(
        project_kernel,
        out_shape=jax.ShapeDtypeStruct((FEATS, GROUPS, LANES), F32),
        in_specs=[pl.BlockSpec(memory_space=pltpu.HBM), pl.BlockSpec(memory_space=pltpu.VMEM)],
        out_specs=pl.BlockSpec(memory_space=pltpu.VMEM),
        scratch_shapes=[
            pltpu.VMEM((PARAMS, G_DEV), F32),
            pltpu.VMEM((8 * PITCH, LANES), F32),
            pltpu.SemaphoreType.DMA((CHUNKS,)),
        ],
        compiler_params=pltpu.CompilerParams(vmem_limit_bytes=VMEM_LIMIT),
    )(gauss_params, geometry)


def gather(requested, features):
    return call(
        gather_kernel, jax.ShapeDtypeStruct((2 * OWNERS, LANES), F32), [requested, features], smalls=0
    )


def render(height, tile_lengths, background, geometry, arrived, aux, cotangent):
    return call(
        functools.partial(render_kernel, height),
        jax.ShapeDtypeStruct((2 * OWNERS, LANES), F32),
        [tile_lengths, background, geometry, arrived, aux, cotangent],
        smalls=2,
        scratch=[
            pltpu.VMEM((FEATS * 8, LANES), F32),
            pltpu.VMEM((2 * OWNERS, LANES), F32),
            pltpu.VMEM((FEATS * 8, LANES), F32),
            pltpu.VMEM((2, PIX, SLOTS), F32),
            pltpu.VMEM((2, SLOTS, SLOTS), BF16),
        ],
    )


def pullback(arrived, gauss_params):
    views = arrived.shape[0]
    return pl.pallas_call(
        pullback_kernel,
        out_shape=jax.ShapeDtypeStruct((PARAMS, G_DEV), F32),
        in_specs=[pl.BlockSpec(memory_space=pltpu.VMEM)] * 2,
        out_specs=pl.BlockSpec(memory_space=pltpu.HBM),
        scratch_shapes=[
            pltpu.VMEM((8 * PITCH, LANES), F32),
            pltpu.VMEM((8 * PITCH, LANES), F32),
            pltpu.VMEM((views, FEATS * GROUPS, LANES), F32),
            pltpu.VMEM((views, 16, LANES), F32),
            pltpu.VMEM((PARAMS, G_DEV), F32),
            pltpu.SemaphoreType.DMA((CHUNKS,)),
        ],
        compiler_params=pltpu.CompilerParams(vmem_limit_bytes=VMEM_LIMIT),
    )(arrived, gauss_params)


def per_device(gauss_params, camera, background, tile_lists, tile_lengths, pixel_cotangent):
    owners_total = lax.axis_size("img")
    views = lax.axis_size("view")
    tiles_here = tile_lists.shape[1]
    height = tiles_here * owners_total // TX
    first_tile = (lax.axis_index("img") * tiles_here).astype(jnp.int32).reshape(1)
    requests, aux, geometry = route(height, camera, first_tile, tile_lists)
    features = project(gauss_params, geometry)
    requested = lax.all_to_all(requests, "img", split_axis=0, concat_axis=0, tiled=True)
    outgoing = gather(requested, features)
    arrived = lax.all_to_all(outgoing, "img", split_axis=0, concat_axis=0, tiled=True)
    slot_grads = render(height, tile_lengths, background, geometry, arrived, aux, pixel_cotangent)
    returned = lax.all_to_all(slot_grads, "img", split_axis=0, concat_axis=0, tiled=True)
    copies = jnp.broadcast_to(returned[None], (views,) + returned.shape)
    everyone = lax.all_to_all(copies, "view", split_axis=0, concat_axis=0, tiled=True)
    return pullback(everyone, gauss_params)


def solution(mesh):
    placed = (
        P(None, "img"),
        P("view", None),
        P(),
        P("view", "img", None),
        P("view", "img"),
        P("view", None, "img", None),
    )
    return jax.shard_map(
        per_device, mesh=mesh, in_specs=placed, out_specs=P(None, "img"), check_vma=False
    )
```

```python
import functools

import jax
import jax.numpy as jnp
from jax import lax
from jax.experimental import pallas as pl
from jax.experimental.pallas import tpu as pltpu
from jax.sharding import PartitionSpec as P

SIDE = 16
TX = 16
PIX = 256
SLOTS = 256
TILES_DEV = 4
OWNERS = 128
CAP = 16
LANES = 128
G_DEV = 8192
GROUPS = G_DEV // LANES
PARAMS = 59
PITCH = 65
CHUNKS = 8
CHUNK = G_DEV // CHUNKS
FEATS = 9
PACK = 256

FOCAL = 2.0
DILATION = 0.0001
SH_ZERO = 0.28209479177387814
SH_ONE = 0.4886025119029199
SH_TWO = (
    1.0925484305920792,
    -1.0925484305920792,
    0.31539156525252005,
    -1.0925484305920792,
    0.5462742152960396,
)
SH_THREE = (
    -0.5900435899266435,
    2.890611442640554,
    -0.4570457994644658,
    0.3731763325901154,
    -0.4570457994644658,
    1.445305721320277,
    -0.5900435899266435,
)

LOG2_E = 1.4426950408889634
F32 = jnp.float32
BF16 = jnp.bfloat16
VMEM_LIMIT = 32 * 1024 * 1024


def iota(shape, axis, dtype=jnp.int32):
    return lax.broadcasted_iota(dtype, shape, axis)


def spread(row, shape):
    return jnp.broadcast_to(row, shape)


def halves(values):
    high = values.astype(BF16)
    low = (values - high.astype(F32)).astype(BF16)
    return high, low


def dot(left, right):
    return jnp.dot(left, right, preferred_element_type=F32)


def dot_lanes(left, right):
    return lax.dot_general(left, right, (((1,), (1,)), ((), ())), preferred_element_type=F32)


GEO = 24


def write_geometry(height, camera_ref, first_ref, geo_ref):
    row = iota((8, LANES), 0)
    block = jnp.zeros((8, LANES), F32)
    for index in range(6):
        block = jnp.where(row == index, camera_ref[0, index], block)
    cosines, sines = jnp.cos(block), jnp.sin(block)
    cx, cy, cz = (cosines[index : index + 1, :] for index in range(3))
    sx, sy, sz = (sines[index : index + 1, :] for index in range(3))
    inner = [
        [cy, sy * sx, sy * cx],
        [None, cx, -sx],
        [-sy, cy * sx, cy * cx],
    ]
    entries = [
        [cz * inner[0][0], cz * inner[0][1] - sz * inner[1][1], cz * inner[0][2] - sz * inner[1][2]],
        [sz * inner[0][0], sz * inner[0][1] + cz * inner[1][1], sz * inner[0][2] + cz * inner[1][2]],
        inner[2],
    ]
    for index, value in enumerate(entries[0] + entries[1] + entries[2]):
        geo_ref[index : index + 1, :] = value
    geo_ref[9:12, :] = block[3:6, :]
    for index in range(TILES_DEV):
        tile_id = first_ref[0] + index
        tile_x = ((tile_id % TX * SIDE).astype(F32) + 0.5) * (2.0 / (TX * SIDE)) - 1.0
        tile_y = ((tile_id // TX * SIDE).astype(F32) + 0.5) * (2.0 / (height * SIDE)) - 1.0
        geo_ref[12 + index : 13 + index, :] = jnp.full((1, LANES), tile_x, F32)
        geo_ref[16 + index : 17 + index, :] = jnp.full((1, LANES), tile_y, F32)
    geo_ref[20:GEO, :] = jnp.zeros((GEO - 20, LANES), F32)


def camera_of(geo):
    entries = [spread(geo[index : index + 1, :], (8, LANES)) for index in range(12)]
    return [entries[0:3], entries[3:6], entries[6:9]], entries[9:12]


def camera_center(rotate, offset):
    return [
        -(rotate[0][col] * offset[0] + rotate[1][col] * offset[1] + rotate[2][col] * offset[2])
        for col in range(3)
    ]


def shape_matrix(log_scales, quaternion):
    scales = [jnp.exp(value) for value in log_scales]
    norm = lax.rsqrt(
        quaternion[0] * quaternion[0]
        + quaternion[1] * quaternion[1]
        + quaternion[2] * quaternion[2]
        + quaternion[3] * quaternion[3]
    )
    real, im_i, im_j, im_k = (part * norm for part in quaternion)
    local = [
        [1.0 - 2.0 * (im_j * im_j + im_k * im_k), 2.0 * (im_i * im_j - real * im_k), 2.0 * (im_i * im_k + real * im_j)],
        [2.0 * (im_i * im_j + real * im_k), 1.0 - 2.0 * (im_i * im_i + im_k * im_k), 2.0 * (im_j * im_k - real * im_i)],
        [2.0 * (im_i * im_k - real * im_j), 2.0 * (im_j * im_k + real * im_i), 1.0 - 2.0 * (im_i * im_i + im_j * im_j)],
    ]
    return [[local[row][col] * scales[col] for col in range(3)] for row in range(3)]


def harmonics(along_x, along_y, along_z):
    square_x, square_y, square_z = along_x * along_x, along_y * along_y, along_z * along_z
    return [
        jnp.full_like(along_x, SH_ZERO),
        -SH_ONE * along_y,
        SH_ONE * along_z,
        -SH_ONE * along_x,
        SH_TWO[0] * along_x * along_y,
        SH_TWO[1] * along_y * along_z,
        SH_TWO[2] * (2.0 * square_z - square_x - square_y),
        SH_TWO[3] * along_x * along_z,
        SH_TWO[4] * (square_x - square_y),
        SH_THREE[0] * along_y * (3.0 * square_x - square_y),
        SH_THREE[1] * along_x * along_y * along_z,
        SH_THREE[2] * along_y * (4.0 * square_z - square_x - square_y),
        SH_THREE[3] * along_z * (2.0 * square_z - 3.0 * square_x - 3.0 * square_y),
        SH_THREE[4] * along_x * (4.0 * square_z - square_x - square_y),
        SH_THREE[5] * along_z * (square_x - square_y),
        SH_THREE[6] * along_x * (square_x - 3.0 * square_y),
    ]


def screen_features(center, shape, rotate, offset):
    viewed = [
        rotate[row][0] * center[0] + rotate[row][1] * center[1] + rotate[row][2] * center[2] + offset[row]
        for row in range(3)
    ]
    depth_inv = 1.0 / viewed[2]
    near = FOCAL * depth_inv
    screen_x = viewed[0] * near
    screen_y = viewed[1] * near
    slope_x = -screen_x * depth_inv
    slope_y = -screen_y * depth_inv
    to_camera = [
        [near * rotate[0][col] + slope_x * rotate[2][col] for col in range(3)],
        [near * rotate[1][col] + slope_y * rotate[2][col] for col in range(3)],
    ]
    mapped = [
        [
            to_camera[row][0] * shape[0][col] + to_camera[row][1] * shape[1][col] + to_camera[row][2] * shape[2][col]
            for col in range(3)
        ]
        for row in range(2)
    ]
    first, second = mapped
    cov_a = first[0] * first[0] + first[1] * first[1] + first[2] * first[2] + DILATION
    cov_b = first[0] * second[0] + first[1] * second[1] + first[2] * second[2]
    cov_c = second[0] * second[0] + second[1] * second[1] + second[2] * second[2] + DILATION
    inverse = 1.0 / (cov_a * cov_c - cov_b * cov_b)
    return [screen_x, screen_y, cov_c * inverse, -cov_b * inverse, cov_a * inverse]


def direction_basis(center, eye):
    toward = [center[index] - eye[index] for index in range(3)]
    norm = lax.rsqrt(toward[0] * toward[0] + toward[1] * toward[1] + toward[2] * toward[2])
    return harmonics(toward[0] * norm, toward[1] * norm, toward[2] * norm)


def chunk_columns(chunk):
    return pl.ds(pl.multiple_of(chunk * CHUNK, CHUNK), CHUNK)


def spread_columns(params_ref, held_ref, chunk):
    for group in range(CHUNK // LANES):
        columns = pl.ds(pl.multiple_of(chunk * CHUNK + group * LANES, LANES), LANES)
        held_ref[chunk, group * PITCH : group * PITCH + PARAMS, :] = params_ref[:, columns]


def project_kernel(height, camera_ref, first_ref, view_ref, params_ref, feats_ref, held_ref, geo_ref, staged_ref, semaphores):
    def fetch(chunk):
        columns = chunk_columns(chunk)
        return pltpu.make_async_copy(params_ref.at[:, columns], staged_ref.at[:, columns], semaphores.at[chunk])

    def start(chunk, carry):
        fetch(chunk).start()
        return carry

    lax.fori_loop(0, CHUNKS, start, 0)
    write_geometry(height, camera_ref, first_ref, geo_ref)
    geo_ref[20:21, :] = jnp.full((1, LANES), view_ref[0].astype(F32), F32)
    rotate, offset = camera_of(geo_ref[...])
    eye = camera_center(rotate, offset)

    def step(chunk, carry):
        fetch(chunk).wait()
        spread_columns(staged_ref, held_ref, chunk)

        def param(index):
            return held_ref[chunk, pl.ds(index, 8, stride=PITCH), :]

        center = [param(index) for index in range(3)]
        shape = shape_matrix([param(3 + index) for index in range(3)], [param(6 + index) for index in range(4)])
        screen = screen_features(center, shape, rotate, offset)
        basis = direction_basis(center, eye)
        opacity = 1.0 / (1.0 + jnp.exp(-param(10)))
        colors = []
        for channel in range(3):
            total = basis[0] * param(11 + channel)
            for term in range(1, 16):
                total = total + basis[term] * param(11 + 3 * term + channel)
            colors.append(total + 0.5)
        rows = pl.ds(pl.multiple_of(chunk * 8, 8), 8)
        for index, value in enumerate(screen + [opacity] + colors):
            feats_ref[index, rows, :] = value
        return carry

    lax.fori_loop(0, CHUNKS, step, 0)


def route_kernel(lists_ref, request_ref, aux_ref):
    owner_iota = iota((OWNERS, LANES), 0)
    before = (iota((LANES, 2 * LANES), 0) < iota((LANES, 2 * LANES), 1)).astype(F32)
    before = before.astype(BF16)
    rank_iota = iota((CAP, LANES), 0)
    lane = iota((1, LANES), 1)
    carried = jnp.zeros((OWNERS, LANES), F32)
    table = jnp.zeros((4 * CAP, OWNERS), F32)
    for row in range(8):
        ids = lists_ref[0, row // 2 : row // 2 + 1, (row % 2) * LANES : (row % 2 + 1) * LANES]
        owner = ids // G_DEV
        column = ids % G_DEV
        hot = owner_iota == spread(owner, (OWNERS, LANES))
        hot_f32 = hot.astype(F32)
        hot_bf16 = hot_f32.astype(BF16)
        counts = dot(hot_bf16, before)
        rank = jnp.sum(jnp.where(hot, counts[:, :LANES] + carried, 0.0), axis=0, keepdims=True)
        carried = carried + counts[:, LANES:]
        rank = rank.astype(jnp.int32)
        at_rank = rank_iota == spread(rank, (CAP, LANES))
        pieces = [column // LANES, column % LANES, lane * 0 + row, lane + 1]
        stacked = jnp.concatenate(
            [jnp.where(at_rank, spread(piece.astype(F32), (CAP, LANES)), 0.0) for piece in pieces], axis=0
        )
        table = table + dot_lanes(stacked.astype(BF16), hot_bf16)
        aux_ref[row : row + 1, :] = owner
        aux_ref[8 + row : 9 + row, :] = rank
    high, low, slot_row, slot_lane = (table[CAP * part : CAP * (part + 1)] for part in range(4))
    used = slot_lane > 0.5
    slot = jnp.where(used, slot_row * LANES + slot_lane - 1.0, -1.0)
    wanted = jnp.where(used, high * LANES + low, -1.0)
    aux_ref[16 : 16 + CAP, :] = slot.astype(jnp.int32)
    aux_ref[16 + CAP : 16 + 2 * CAP, :] = wanted.astype(jnp.int32)
    padded = jnp.concatenate([wanted, jnp.zeros((LANES - CAP, OWNERS), F32)], axis=0)
    request_ref[...] = padded.T.astype(jnp.int32)


LANE_GATHER = lax.GatherDimensionNumbers(
    offset_dims=(),
    collapsed_slice_dims=(1,),
    start_index_map=(1,),
    operand_batching_dims=(0,),
    start_indices_batching_dims=(0,),
)


def pick(row, lanes_at):
    return lax.gather(
        spread(row, (8, LANES)),
        lanes_at[:, :, None],
        LANE_GATHER,
        slice_sizes=(1, 1),
        mode=lax.GatherScatterMode.PROMISE_IN_BOUNDS,
    )


def store_rows(out_ref, table):
    out_ref[pl.ds(0, LANES, stride=2), :] = table[:LANES].T
    out_ref[pl.ds(1, LANES, stride=2), :] = table[LANES:].T


def gather_kernel(request_ref, feats_ref, out_ref):
    wanted = request_ref[...].astype(F32).T[:CAP].astype(jnp.int32)
    high, low = wanted >> 7, wanted & (LANES - 1)
    parts = [(high[:8], low[:8]), (high[8:], low[8:])]

    def step(group, found):
        found = list(found)
        for index in range(FEATS):
            row = feats_ref[index, pl.ds(group, 1), :]
            for part, (at_group, at_lane) in enumerate(parts):
                place = 2 * index + part
                found[place] = jnp.where(at_group == group, pick(row, at_lane), found[place])
        return tuple(found)

    start = tuple(jnp.zeros((8, LANES), F32) for _ in range(2 * FEATS))
    found = lax.fori_loop(0, GROUPS, step, start, unroll=16)
    table = jnp.concatenate(list(found) + [jnp.zeros((PACK - FEATS * CAP, LANES), F32)], axis=0)
    store_rows(out_ref, table)


PIX_CHUNK = 128


def render_kernel(
    height, lengths_ref, background_ref, geo_ref, arrived_ref, aux_ref, cotangent_ref, out_ref,
    slot_ref, table_ref, grad_ref, pixel_ref, weight_ref,
):
    table_ref[:LANES, :] = arrived_ref[pl.ds(0, LANES, stride=2), :].T
    table_ref[LANES:, :] = arrived_ref[pl.ds(1, LANES, stride=2), :].T
    owner = aux_ref[0:8, :]
    rank = aux_ref[8:16, :]
    at_rank = [rank == place for place in range(CAP)]
    for index in range(FEATS):
        value = jnp.zeros((8, LANES), F32)
        for place in range(CAP):
            row = table_ref[index * CAP + place : index * CAP + place + 1, :]
            value = jnp.where(at_rank[place], pick(row, owner), value)
        slot_ref[index * 8 : index * 8 + 8, :] = value

    within = iota((PIX, SLOTS), 0)
    pixel_ref[0] = (within % SIDE).astype(F32) * (2.0 / (TX * SIDE))
    pixel_ref[1] = (within // SIDE).astype(F32) * (2.0 / (height * SIDE))
    slot_row, slot_col = iota((SLOTS, SLOTS), 0), iota((SLOTS, SLOTS), 1)
    weight_ref[0] = (slot_row < slot_col).astype(F32).astype(BF16)
    weight_ref[1] = (slot_row > slot_col).astype(F32).astype(BF16)
    slot_place = iota((1, SLOTS), 1)
    def tile(index, carry):
        def slots(feature):
            return jnp.concatenate(
                [slot_ref[pl.ds(feature * 8 + 2 * index + half, 1), :] for half in range(2)], axis=1
            )

        tile_x, tile_y = geo_ref[pl.ds(12 + index, 1), :], geo_ref[pl.ds(16 + index, 1), :]
        at_x = slots(0) - jnp.concatenate([tile_x] * 2, axis=1)
        at_y = slots(1) - jnp.concatenate([tile_y] * 2, axis=1)
        conic_a, conic_b, conic_c = slots(2), slots(3), slots(4)
        opacity = slots(5)
        live_opacity = jnp.where(slot_place < lengths_ref[0, index], opacity, 0.0)
        colors = [slots(6 + channel) for channel in range(3)]
        scaled_a, scaled_b, scaled_c = (-0.5 * LOG2_E) * conic_a, -LOG2_E * conic_b, (-0.5 * LOG2_E) * conic_c
        shades = [cotangent_ref[0, channel, pl.ds(index, 1), :] for channel in range(3)]
        behind = (
            shades[0] * background_ref[0] + shades[1] * background_ref[1] + shades[2] * background_ref[2]
        )
        columns = jnp.concatenate(shades + [behind, jnp.zeros((4, PIX), F32)], axis=0).T

        def fold(values):
            return jnp.sum(values.reshape(PIX_CHUNK // 8, 8, SLOTS), axis=0)

        sums = [jnp.zeros((8, SLOTS), F32) for _ in range(9)]
        for chunk in range(PIX // PIX_CHUNK):
            rows = slice(chunk * PIX_CHUNK, (chunk + 1) * PIX_CHUNK)
            shape = (PIX_CHUNK, SLOTS)
            delta_x = pixel_ref[0, rows, :] - at_x
            delta_y = pixel_ref[1, rows, :] - at_y
            exponent = (scaled_a * delta_x + scaled_b * delta_y) * delta_x + scaled_c * delta_y * delta_y
            coverage = live_opacity * jnp.exp2(exponent)
            log_pass = jnp.log2(1.0 - coverage)
            high, low = halves(log_pass)
            prefix = dot(high, weight_ref[0]) + dot(low, weight_ref[0])
            weight = coverage * jnp.exp2(prefix)
            shade = [spread(columns[rows, channel : channel + 1], shape) for channel in range(3)]
            gain = shade[0] * colors[0] + shade[1] * colors[1] + shade[2] * colors[2]
            product = weight * gain
            high, low = halves(product)
            later = dot(high, weight_ref[1]) + dot(low, weight_ref[1])
            remain = jnp.exp2(prefix[:, SLOTS - 1 :] + log_pass[:, SLOTS - 1 :])
            later = later + spread(columns[rows, 3:4] * remain, shape)
            slope = product - coverage * jnp.exp2(-log_pass) * later
            slope_x = slope * delta_x
            slope_y = slope * delta_y
            parts = [slope, slope_x, slope_y, slope_x * delta_x, slope_x * delta_y, slope_y * delta_y]
            parts += [part * weight for part in shade]
            sums = [total + fold(part) for total, part in zip(sums, parts)]

        sums = [jnp.sum(part, axis=0, keepdims=True) for part in sums]
        total, sum_x, sum_y, sum_xx, sum_xy, sum_yy = (part * -0.5 for part in sums[:6])
        grads = [
            -2.0 * (conic_a * sum_x + conic_b * sum_y),
            -2.0 * (conic_b * sum_x + conic_c * sum_y),
            sum_xx,
            2.0 * sum_xy,
            sum_yy,
            -2.0 * total / opacity,
        ] + sums[6:]
        for feature, value in enumerate(grads):
            for half in range(2):
                grad_ref[pl.ds(feature * 8 + 2 * index + half, 1), :] = value[:, half * LANES : (half + 1) * LANES]
        return carry

    lax.fori_loop(0, TILES_DEV, tile, 0, unroll=TILES_DEV)

    slot = aux_ref[16 : 16 + CAP, :]
    wanted = aux_ref[16 + CAP : 16 + 2 * CAP, :].astype(F32)
    parts = [(slot[8 * part : 8 * part + 8] >> 7, slot[8 * part : 8 * part + 8] & (LANES - 1)) for part in range(2)]
    blocks = []
    for feature in range(FEATS):
        for at_row, at_lane in parts:
            value = jnp.zeros((8, LANES), F32)
            for row in range(8):
                grads = grad_ref[feature * 8 + row : feature * 8 + row + 1, :]
                value = jnp.where(at_row == row, pick(grads, at_lane), value)
            blocks.append(value)
    blocks += [wanted, geo_ref[0:16, :], jnp.zeros((PACK - FEATS * CAP - CAP - 16, LANES), F32)]
    store_rows(out_ref, jnp.concatenate(blocks, axis=0))


WIDE = 256
TALL = G_DEV // WIDE


def scatter_view(view, arrived_ref, place, grads_ref, camera_ref):
    tall_iota = iota((TALL, LANES), 0)
    wide_iota = iota((WIDE, LANES), 0)
    first = arrived_ref[view, pl.ds(0, LANES, stride=2), :].T
    second = arrived_ref[view, pl.ds(1, LANES, stride=2), :].T
    rest = FEATS * CAP - LANES
    values = jnp.concatenate([first, second[:rest]], axis=0)
    wanted = second[rest : rest + CAP].astype(jnp.int32)
    camera_ref[place] = second[rest + CAP : rest + CAP + 16]
    high_place, low_place = wanted >> 8, wanted & (WIDE - 1)
    high, low = halves(values)
    high, low = high.astype(F32), low.astype(F32)
    lefts, rights = [], []
    for rank in range(CAP):
        at_high = tall_iota == spread(high_place[rank : rank + 1], (TALL, LANES))
        at_low = wide_iota == spread(low_place[rank : rank + 1], (WIDE, LANES))
        at_low = at_low.astype(F32).astype(BF16)
        for source in (high, low):
            rows = [source[index * CAP + rank : index * CAP + rank + 1] for index in range(FEATS)]
            left = [jnp.where(at_high, spread(row, (TALL, LANES)), 0.0) for row in rows]
            lefts.append(jnp.concatenate(left, axis=0).astype(BF16))
            rights.append(at_low)
    total = dot_lanes(jnp.concatenate(lefts, axis=1), jnp.concatenate(rights, axis=1))
    for half in range(2):
        grads_ref[place, pl.ds(half, FEATS * TALL, stride=2), :] = total[:, half * LANES : (half + 1) * LANES]


SHAPE_ROWS = (3, 4, 5, 6, 7, 8, 9, 59, 60)


def pull_view(chunk, place, center, shape, param, grads_ref, camera_ref, kept, keep):
    def cotangent(feature):
        return grads_ref[place, pl.ds(pl.multiple_of(feature * GROUPS + chunk * 8, 8), 8), :]

    def add(index, value):
        before = kept(index)
        keep(index, value if before is None else before + value)

    rotate, offset = camera_of(camera_ref[place])
    eye = camera_center(rotate, offset)
    basis, basis_back = jax.vjp(lambda spot: direction_basis(spot, eye), center)
    colors = [cotangent(6 + channel) for channel in range(3)]
    basis_grad = []
    for term in range(16):
        total = None
        for channel in range(3):
            index = 11 + 3 * term + channel
            add(index, basis[term] * colors[channel])
            piece = param(index) * colors[channel]
            total = piece if total is None else total + piece
        basis_grad.append(total)
    (along,) = basis_back(basis_grad)
    unused, screen_back = jax.vjp(
        lambda spot, matrix: screen_features(spot, matrix, rotate, offset), center, shape
    )
    moved, bent = screen_back([cotangent(index) for index in range(5)])
    for axis in range(3):
        add(axis, along[axis] + moved[axis])
    for row in range(3):
        for col in range(3):
            add(SHAPE_ROWS[3 * row + col], bent[row][col])
    add(10, cotangent(5))


def own_pullback_kernel(returned_ref, held_ref, partial_ref, grads_ref, camera_ref):
    scatter_view(0, returned_ref, 0, grads_ref, camera_ref)

    def step(chunk, carry):
        def param(index):
            return held_ref[chunk, pl.ds(index, 8, stride=PITCH), :]

        def keep(index, value):
            partial_ref[chunk, pl.ds(index, 8, stride=PITCH), :] = value

        center = [param(index) for index in range(3)]
        shape = shape_matrix([param(3 + index) for index in range(3)], [param(6 + index) for index in range(4)])
        pull_view(chunk, 0, center, shape, param, grads_ref, camera_ref, lambda index: None, keep)
        return carry

    lax.fori_loop(0, CHUNKS, step, 0)


def pullback_kernel(
    view_ref, arrived_ref, held_ref, partial_ref, out_ref, sums_ref, grads_ref, camera_ref, staged_ref, semaphores
):
    views = arrived_ref.shape[0]

    def one_view(place, carry):
        view = lax.rem(view_ref[0] + 1 + place, views)
        scatter_view(view, arrived_ref, place, grads_ref, camera_ref)
        return carry

    lax.fori_loop(0, views - 1, one_view, 0)

    def send(chunk):
        columns = chunk_columns(chunk)
        return pltpu.make_async_copy(staged_ref.at[:, columns], out_ref.at[:, columns], semaphores.at[chunk])

    def step(chunk, carry):
        def param(index):
            return held_ref[chunk, pl.ds(index, 8, stride=PITCH), :]

        def first(index):
            return partial_ref[chunk, pl.ds(index, 8, stride=PITCH), :]

        def keep(index, value):
            sums_ref[pl.ds(index, 8, stride=PITCH), :] = value

        def kept(index):
            return sums_ref[pl.ds(index, 8, stride=PITCH), :]

        center = [param(index) for index in range(3)]
        shape, shape_back = jax.vjp(
            shape_matrix, [param(3 + index) for index in range(3)], [param(6 + index) for index in range(4)]
        )
        for place in range(views - 1):
            pull_view(
                chunk, place, center, shape, param, grads_ref, camera_ref, kept if place else first, keep
            )
        scale_grad, quaternion_grad = shape_back(
            [[kept(SHAPE_ROWS[3 * row + col]) for col in range(3)] for row in range(3)]
        )
        opacity = 1.0 / (1.0 + jnp.exp(-param(10)))
        finals = list(scale_grad) + list(quaternion_grad) + [opacity * (1.0 - opacity) * kept(10)]
        for index, value in enumerate(finals):
            keep(3 + index, value)
        for group in range(CHUNK // LANES):
            columns = pl.ds(pl.multiple_of(chunk * CHUNK + group * LANES, LANES), LANES)
            staged_ref[:, columns] = sums_ref[group * PITCH : group * PITCH + PARAMS, :]
        send(chunk).start()
        return carry

    lax.fori_loop(0, CHUNKS, step, 0)

    def finish(chunk, carry):
        send(chunk).wait()
        return carry

    lax.fori_loop(0, CHUNKS, finish, 0)


def call(kernel, out_shape, operands, smalls=(), scratch=(), **kwargs):
    spaces = [pltpu.SMEM if index < smalls else pltpu.VMEM for index in range(len(operands))]
    single = not isinstance(out_shape, (list, tuple))
    outs = pl.BlockSpec(memory_space=pltpu.VMEM)
    return pl.pallas_call(
        kernel,
        out_shape=out_shape,
        in_specs=[pl.BlockSpec(memory_space=space) for space in spaces],
        out_specs=outs if single else [outs] * len(out_shape),
        scratch_shapes=list(scratch),
        compiler_params=pltpu.CompilerParams(vmem_limit_bytes=VMEM_LIMIT),
        **kwargs,
    )(*operands)


HELD = jax.ShapeDtypeStruct((CHUNKS, 8 * PITCH, LANES), F32)


def route(tile_lists):
    return call(
        route_kernel,
        [
            jax.ShapeDtypeStruct((OWNERS, LANES), jnp.int32),
            jax.ShapeDtypeStruct((16 + 2 * CAP, LANES), jnp.int32),
        ],
        [tile_lists],
        smalls=0,
    )


def project(height, camera, first_tile, view, gauss_params):
    return pl.pallas_call(
        functools.partial(project_kernel, height),
        out_shape=[
            jax.ShapeDtypeStruct((FEATS, GROUPS, LANES), F32),
            HELD,
            jax.ShapeDtypeStruct((GEO, LANES), F32),
        ],
        in_specs=[pl.BlockSpec(memory_space=pltpu.SMEM)] * 3 + [pl.BlockSpec(memory_space=pltpu.HBM)],
        out_specs=[pl.BlockSpec(memory_space=pltpu.VMEM)] * 3,
        scratch_shapes=[
            pltpu.VMEM((PARAMS, G_DEV), F32),
            pltpu.SemaphoreType.DMA((CHUNKS,)),
        ],
        compiler_params=pltpu.CompilerParams(vmem_limit_bytes=VMEM_LIMIT),
    )(camera, first_tile, view, gauss_params)


def gather(requested, features):
    return call(
        gather_kernel, jax.ShapeDtypeStruct((2 * OWNERS, LANES), F32), [requested, features], smalls=0
    )


def render(height, tile_lengths, background, geometry, arrived, aux, cotangent):
    return call(
        functools.partial(render_kernel, height),
        jax.ShapeDtypeStruct((2 * OWNERS, LANES), F32),
        [tile_lengths, background, geometry, arrived, aux, cotangent],
        smalls=2,
        scratch=[
            pltpu.VMEM((FEATS * 8, LANES), F32),
            pltpu.VMEM((2 * OWNERS, LANES), F32),
            pltpu.VMEM((FEATS * 8, LANES), F32),
            pltpu.VMEM((2, PIX, SLOTS), F32),
            pltpu.VMEM((2, SLOTS, SLOTS), BF16),
        ],
    )


def own_pullback(returned, held):
    return call(
        own_pullback_kernel,
        HELD,
        [returned.reshape((1,) + returned.shape), held],
        smalls=0,
        scratch=[pltpu.VMEM((1, FEATS * GROUPS, LANES), F32), pltpu.VMEM((1, 16, LANES), F32)],
        cost_estimate=pl.CostEstimate(flops=20_000_000, bytes_accessed=4_000_000, transcendentals=0),
    )


def pullback(view, arrived, held, partial):
    others = arrived.shape[0] - 1
    return pl.pallas_call(
        pullback_kernel,
        out_shape=jax.ShapeDtypeStruct((PARAMS, G_DEV), F32),
        in_specs=[pl.BlockSpec(memory_space=pltpu.SMEM)] + [pl.BlockSpec(memory_space=pltpu.VMEM)] * 3,
        out_specs=pl.BlockSpec(memory_space=pltpu.HBM),
        scratch_shapes=[
            pltpu.VMEM((8 * PITCH, LANES), F32),
            pltpu.VMEM((others, FEATS * GROUPS, LANES), F32),
            pltpu.VMEM((others, 16, LANES), F32),
            pltpu.VMEM((PARAMS, G_DEV), F32),
            pltpu.SemaphoreType.DMA((CHUNKS,)),
        ],
        compiler_params=pltpu.CompilerParams(vmem_limit_bytes=VMEM_LIMIT),
    )(view, arrived, held, partial)


def per_device(gauss_params, camera, background, tile_lists, tile_lengths, pixel_cotangent):
    owners_total = lax.axis_size("img")
    views = lax.axis_size("view")
    tiles_here = tile_lists.shape[1]
    height = tiles_here * owners_total // TX
    first_tile = (lax.axis_index("img") * tiles_here).astype(jnp.int32).reshape(1)
    view = lax.axis_index("view").astype(jnp.int32).reshape(1)
    requests, aux = route(tile_lists)
    features, held, geometry = project(height, camera, first_tile, view, gauss_params)
    requested = lax.all_to_all(requests, "img", split_axis=0, concat_axis=0, tiled=True)
    outgoing = gather(requested, features)
    arrived = lax.all_to_all(outgoing, "img", split_axis=0, concat_axis=0, tiled=True)
    slot_grads = render(height, tile_lengths, background, geometry, arrived, aux, pixel_cotangent)
    returned = lax.all_to_all(slot_grads, "img", split_axis=0, concat_axis=0, tiled=True)
    copies = jnp.broadcast_to(returned[None], (views,) + returned.shape)
    everyone = lax.all_to_all(copies, "view", split_axis=0, concat_axis=0, tiled=True)
    partial = own_pullback(returned, held)
    return pullback(view, everyone, held, partial)


def solution(mesh):
    placed = (
        P(None, "img"),
        P("view", None),
        P(),
        P("view", "img", None),
        P("view", "img"),
        P("view", None, "img", None),
    )
    return jax.shard_map(
        per_device, mesh=mesh, in_specs=placed, out_specs=P(None, "img"), check_vma=False
    )
```

```python
import functools

import jax
import jax.numpy as jnp
from jax import lax
from jax.experimental import pallas as pl
from jax.experimental.pallas import tpu as pltpu
from jax.sharding import PartitionSpec as P

SIDE = 16
TX = 16
PIX = 256
SLOTS = 256
TILES_DEV = 4
OWNERS = 128
CAP = 16
LANES = 128
G_DEV = 8192
GROUPS = G_DEV // LANES
PARAMS = 59
PITCH = 65
CHUNKS = 8
CHUNK = G_DEV // CHUNKS
FEATS = 9
PACK = 256
SENT = FEATS * CAP + CAP + 16

FOCAL = 2.0
DILATION = 0.0001
SH_ZERO = 0.28209479177387814
SH_ONE = 0.4886025119029199
SH_TWO = (
    1.0925484305920792,
    -1.0925484305920792,
    0.31539156525252005,
    -1.0925484305920792,
    0.5462742152960396,
)
SH_THREE = (
    -0.5900435899266435,
    2.890611442640554,
    -0.4570457994644658,
    0.3731763325901154,
    -0.4570457994644658,
    1.445305721320277,
    -0.5900435899266435,
)

LOG2_E = 1.4426950408889634
F32 = jnp.float32
BF16 = jnp.bfloat16
VMEM_LIMIT = 16 * 1024 * 1024
LAST_VMEM_LIMIT = 52 * 1024 * 1024


def iota(shape, axis, dtype=jnp.int32):
    return lax.broadcasted_iota(dtype, shape, axis)


def spread(row, shape):
    return jnp.broadcast_to(row, shape)


def halves(values):
    high = values.astype(BF16)
    low = (values - high.astype(F32)).astype(BF16)
    return high, low


def dot(left, right):
    return jnp.dot(left, right, preferred_element_type=F32)


def dot_lanes(left, right):
    return lax.dot_general(left, right, (((1,), (1,)), ((), ())), preferred_element_type=F32)


GEO = 24


def write_geometry(height, camera_ref, first_ref, geo_ref):
    row = iota((8, LANES), 0)
    block = jnp.zeros((8, LANES), F32)
    for index in range(6):
        block = jnp.where(row == index, camera_ref[0, index], block)
    cosines, sines = jnp.cos(block), jnp.sin(block)
    cx, cy, cz = (cosines[index : index + 1, :] for index in range(3))
    sx, sy, sz = (sines[index : index + 1, :] for index in range(3))
    inner = [
        [cy, sy * sx, sy * cx],
        [None, cx, -sx],
        [-sy, cy * sx, cy * cx],
    ]
    entries = [
        [cz * inner[0][0], cz * inner[0][1] - sz * inner[1][1], cz * inner[0][2] - sz * inner[1][2]],
        [sz * inner[0][0], sz * inner[0][1] + cz * inner[1][1], sz * inner[0][2] + cz * inner[1][2]],
        inner[2],
    ]
    for index, value in enumerate(entries[0] + entries[1] + entries[2]):
        geo_ref[index : index + 1, :] = value
    geo_ref[9:12, :] = block[3:6, :]
    for index in range(TILES_DEV):
        tile_id = first_ref[0] + index
        tile_x = ((tile_id % TX * SIDE).astype(F32) + 0.5) * (2.0 / (TX * SIDE)) - 1.0
        tile_y = ((tile_id // TX * SIDE).astype(F32) + 0.5) * (2.0 / (height * SIDE)) - 1.0
        geo_ref[12 + index : 13 + index, :] = jnp.full((1, LANES), tile_x, F32)
        geo_ref[16 + index : 17 + index, :] = jnp.full((1, LANES), tile_y, F32)
    geo_ref[20:GEO, :] = jnp.zeros((GEO - 20, LANES), F32)


def camera_of(geo):
    entries = [spread(geo[index : index + 1, :], (8, LANES)) for index in range(12)]
    return [entries[0:3], entries[3:6], entries[6:9]], entries[9:12]


def camera_center(rotate, offset):
    return [
        -(rotate[0][col] * offset[0] + rotate[1][col] * offset[1] + rotate[2][col] * offset[2])
        for col in range(3)
    ]


def shape_matrix(log_scales, quaternion):
    scales = [jnp.exp(value) for value in log_scales]
    norm = lax.rsqrt(
        quaternion[0] * quaternion[0]
        + quaternion[1] * quaternion[1]
        + quaternion[2] * quaternion[2]
        + quaternion[3] * quaternion[3]
    )
    real, im_i, im_j, im_k = (part * norm for part in quaternion)
    local = [
        [1.0 - 2.0 * (im_j * im_j + im_k * im_k), 2.0 * (im_i * im_j - real * im_k), 2.0 * (im_i * im_k + real * im_j)],
        [2.0 * (im_i * im_j + real * im_k), 1.0 - 2.0 * (im_i * im_i + im_k * im_k), 2.0 * (im_j * im_k - real * im_i)],
        [2.0 * (im_i * im_k - real * im_j), 2.0 * (im_j * im_k + real * im_i), 1.0 - 2.0 * (im_i * im_i + im_j * im_j)],
    ]
    return [[local[row][col] * scales[col] for col in range(3)] for row in range(3)]


def harmonics(along_x, along_y, along_z):
    square_x, square_y, square_z = along_x * along_x, along_y * along_y, along_z * along_z
    return [
        jnp.full_like(along_x, SH_ZERO),
        -SH_ONE * along_y,
        SH_ONE * along_z,
        -SH_ONE * along_x,
        SH_TWO[0] * along_x * along_y,
        SH_TWO[1] * along_y * along_z,
        SH_TWO[2] * (2.0 * square_z - square_x - square_y),
        SH_TWO[3] * along_x * along_z,
        SH_TWO[4] * (square_x - square_y),
        SH_THREE[0] * along_y * (3.0 * square_x - square_y),
        SH_THREE[1] * along_x * along_y * along_z,
        SH_THREE[2] * along_y * (4.0 * square_z - square_x - square_y),
        SH_THREE[3] * along_z * (2.0 * square_z - 3.0 * square_x - 3.0 * square_y),
        SH_THREE[4] * along_x * (4.0 * square_z - square_x - square_y),
        SH_THREE[5] * along_z * (square_x - square_y),
        SH_THREE[6] * along_x * (square_x - 3.0 * square_y),
    ]


def screen_features(center, shape, rotate, offset):
    viewed = [
        rotate[row][0] * center[0] + rotate[row][1] * center[1] + rotate[row][2] * center[2] + offset[row]
        for row in range(3)
    ]
    depth_inv = 1.0 / viewed[2]
    near = FOCAL * depth_inv
    screen_x = viewed[0] * near
    screen_y = viewed[1] * near
    slope_x = -screen_x * depth_inv
    slope_y = -screen_y * depth_inv
    to_camera = [
        [near * rotate[0][col] + slope_x * rotate[2][col] for col in range(3)],
        [near * rotate[1][col] + slope_y * rotate[2][col] for col in range(3)],
    ]
    mapped = [
        [
            to_camera[row][0] * shape[0][col] + to_camera[row][1] * shape[1][col] + to_camera[row][2] * shape[2][col]
            for col in range(3)
        ]
        for row in range(2)
    ]
    first, second = mapped
    cov_a = first[0] * first[0] + first[1] * first[1] + first[2] * first[2] + DILATION
    cov_b = first[0] * second[0] + first[1] * second[1] + first[2] * second[2]
    cov_c = second[0] * second[0] + second[1] * second[1] + second[2] * second[2] + DILATION
    inverse = 1.0 / (cov_a * cov_c - cov_b * cov_b)
    return [screen_x, screen_y, cov_c * inverse, -cov_b * inverse, cov_a * inverse]


def direction_basis(center, eye):
    toward = [center[index] - eye[index] for index in range(3)]
    norm = lax.rsqrt(toward[0] * toward[0] + toward[1] * toward[1] + toward[2] * toward[2])
    return harmonics(toward[0] * norm, toward[1] * norm, toward[2] * norm)


def chunk_columns(chunk):
    return pl.ds(pl.multiple_of(chunk * CHUNK, CHUNK), CHUNK)


def spread_columns(params_ref, held_ref, chunk):
    for group in range(CHUNK // LANES):
        columns = pl.ds(pl.multiple_of(chunk * CHUNK + group * LANES, LANES), LANES)
        held_ref[chunk, group * PITCH : group * PITCH + PARAMS, :] = params_ref[:, columns]


def project_kernel(height, camera_ref, first_ref, view_ref, params_ref, feats_ref, held_ref, geo_ref, staged_ref, semaphores):
    def fetch(chunk):
        columns = chunk_columns(chunk)
        return pltpu.make_async_copy(params_ref.at[:, columns], staged_ref.at[:, columns], semaphores.at[chunk])

    def start(chunk, carry):
        fetch(chunk).start()
        return carry

    lax.fori_loop(0, CHUNKS, start, 0)
    write_geometry(height, camera_ref, first_ref, geo_ref)
    geo_ref[20:21, :] = jnp.full((1, LANES), view_ref[0].astype(F32), F32)
    rotate, offset = camera_of(geo_ref[...])
    eye = camera_center(rotate, offset)

    def step(chunk, carry):
        fetch(chunk).wait()
        spread_columns(staged_ref, held_ref, chunk)

        def param(index):
            return held_ref[chunk, pl.ds(index, 8, stride=PITCH), :]

        center = [param(index) for index in range(3)]
        shape = shape_matrix([param(3 + index) for index in range(3)], [param(6 + index) for index in range(4)])
        screen = screen_features(center, shape, rotate, offset)
        basis = direction_basis(center, eye)
        opacity = 1.0 / (1.0 + jnp.exp(-param(10)))
        colors = []
        for channel in range(3):
            total = basis[0] * param(11 + channel)
            for term in range(1, 16):
                total = total + basis[term] * param(11 + 3 * term + channel)
            colors.append(total + 0.5)
        rows = pl.ds(pl.multiple_of(chunk * 8, 8), 8)
        for index, value in enumerate(screen + [opacity] + colors):
            feats_ref[index, rows, :] = value
        return carry

    lax.fori_loop(0, CHUNKS, step, 0)


def route_kernel(lists_ref, request_ref, aux_ref):
    owner_iota = iota((OWNERS, LANES), 0)
    before = (iota((LANES, 2 * LANES), 0) < iota((LANES, 2 * LANES), 1)).astype(F32)
    before = before.astype(BF16)
    rank_iota = iota((CAP, LANES), 0)
    lane = iota((1, LANES), 1)
    carried = jnp.zeros((OWNERS, LANES), F32)
    table = jnp.zeros((4 * CAP, OWNERS), F32)
    for row in range(8):
        ids = lists_ref[0, row // 2 : row // 2 + 1, (row % 2) * LANES : (row % 2 + 1) * LANES]
        owner = ids // G_DEV
        column = ids % G_DEV
        hot = owner_iota == spread(owner, (OWNERS, LANES))
        hot_f32 = hot.astype(F32)
        hot_bf16 = hot_f32.astype(BF16)
        counts = dot(hot_bf16, before)
        rank = jnp.sum(jnp.where(hot, counts[:, :LANES] + carried, 0.0), axis=0, keepdims=True)
        carried = carried + counts[:, LANES:]
        rank = rank.astype(jnp.int32)
        at_rank = rank_iota == spread(rank, (CAP, LANES))
        pieces = [column // LANES, column % LANES, lane * 0 + row, lane + 1]
        stacked = jnp.concatenate(
            [jnp.where(at_rank, spread(piece.astype(F32), (CAP, LANES)), 0.0) for piece in pieces], axis=0
        )
        table = table + dot_lanes(stacked.astype(BF16), hot_bf16)
        aux_ref[row : row + 1, :] = owner
        aux_ref[8 + row : 9 + row, :] = rank
    high, low, slot_row, slot_lane = (table[CAP * part : CAP * (part + 1)] for part in range(4))
    used = slot_lane > 0.5
    slot = jnp.where(used, slot_row * LANES + slot_lane - 1.0, -1.0)
    wanted = jnp.where(used, high * LANES + low, -1.0)
    aux_ref[16 : 16 + CAP, :] = slot.astype(jnp.int32)
    aux_ref[16 + CAP : 16 + 2 * CAP, :] = wanted.astype(jnp.int32)
    padded = jnp.concatenate([wanted, jnp.zeros((LANES - CAP, OWNERS), F32)], axis=0)
    request_ref[...] = padded.T.astype(jnp.int32)


LANE_GATHER = lax.GatherDimensionNumbers(
    offset_dims=(),
    collapsed_slice_dims=(1,),
    start_index_map=(1,),
    operand_batching_dims=(0,),
    start_indices_batching_dims=(0,),
)


def pick(row, lanes_at):
    return lax.gather(
        spread(row, (8, LANES)),
        lanes_at[:, :, None],
        LANE_GATHER,
        slice_sizes=(1, 1),
        mode=lax.GatherScatterMode.PROMISE_IN_BOUNDS,
    )


def store_rows(out_ref, table):
    out_ref[pl.ds(0, LANES, stride=2), :] = table[:LANES].T
    out_ref[pl.ds(1, LANES, stride=2), :] = table[LANES:].T


def gather_kernel(request_ref, feats_ref, out_ref):
    wanted = request_ref[...].astype(F32).T[:CAP].astype(jnp.int32)
    high, low = wanted >> 7, wanted & (LANES - 1)
    parts = [(high[:8], low[:8]), (high[8:], low[8:])]

    def step(group, found):
        found = list(found)
        for index in range(FEATS):
            row = feats_ref[index, pl.ds(group, 1), :]
            for part, (at_group, at_lane) in enumerate(parts):
                place = 2 * index + part
                found[place] = jnp.where(at_group == group, pick(row, at_lane), found[place])
        return tuple(found)

    start = tuple(jnp.zeros((8, LANES), F32) for _ in range(2 * FEATS))
    found = lax.fori_loop(0, GROUPS, step, start, unroll=16)
    table = jnp.concatenate(list(found) + [jnp.zeros((PACK - FEATS * CAP, LANES), F32)], axis=0)
    store_rows(out_ref, table)


PIX_CHUNK = 128


def render_kernel(
    height, lengths_ref, background_ref, geo_ref, arrived_ref, aux_ref, cotangent_ref, out_ref,
    slot_ref, table_ref, grad_ref, pixel_ref, weight_ref,
):
    table_ref[:LANES, :] = arrived_ref[pl.ds(0, LANES, stride=2), :].T
    table_ref[LANES:, :] = arrived_ref[pl.ds(1, LANES, stride=2), :].T
    owner = aux_ref[0:8, :]
    rank = aux_ref[8:16, :]
    at_rank = [rank == place for place in range(CAP)]
    for index in range(FEATS):
        value = jnp.zeros((8, LANES), F32)
        for place in range(CAP):
            row = table_ref[index * CAP + place : index * CAP + place + 1, :]
            value = jnp.where(at_rank[place], pick(row, owner), value)
        slot_ref[index * 8 : index * 8 + 8, :] = value

    within = iota((PIX, SLOTS), 0)
    pixel_ref[0] = (within % SIDE).astype(F32) * (2.0 / (TX * SIDE))
    pixel_ref[1] = (within // SIDE).astype(F32) * (2.0 / (height * SIDE))
    slot_row, slot_col = iota((SLOTS, SLOTS), 0), iota((SLOTS, SLOTS), 1)
    weight_ref[0] = (slot_row < slot_col).astype(F32).astype(BF16)
    weight_ref[1] = (slot_row > slot_col).astype(F32).astype(BF16)
    slot_place = iota((1, SLOTS), 1)
    def tile(index, carry):
        def slots(feature):
            return jnp.concatenate(
                [slot_ref[pl.ds(feature * 8 + 2 * index + half, 1), :] for half in range(2)], axis=1
            )

        tile_x, tile_y = geo_ref[pl.ds(12 + index, 1), :], geo_ref[pl.ds(16 + index, 1), :]
        at_x = slots(0) - jnp.concatenate([tile_x] * 2, axis=1)
        at_y = slots(1) - jnp.concatenate([tile_y] * 2, axis=1)
        conic_a, conic_b, conic_c = slots(2), slots(3), slots(4)
        opacity = slots(5)
        live_opacity = jnp.where(slot_place < lengths_ref[0, index], opacity, 0.0)
        colors = [slots(6 + channel) for channel in range(3)]
        scaled_a, scaled_b, scaled_c = (-0.5 * LOG2_E) * conic_a, -LOG2_E * conic_b, (-0.5 * LOG2_E) * conic_c
        shades = [cotangent_ref[0, channel, pl.ds(index, 1), :] for channel in range(3)]
        behind = (
            shades[0] * background_ref[0] + shades[1] * background_ref[1] + shades[2] * background_ref[2]
        )
        columns = jnp.concatenate(shades + [behind, jnp.zeros((4, PIX), F32)], axis=0).T

        def fold(values):
            return jnp.sum(values.reshape(PIX_CHUNK // 8, 8, SLOTS), axis=0)

        sums = [jnp.zeros((8, SLOTS), F32) for _ in range(9)]
        for chunk in range(PIX // PIX_CHUNK):
            rows = slice(chunk * PIX_CHUNK, (chunk + 1) * PIX_CHUNK)
            shape = (PIX_CHUNK, SLOTS)
            delta_x = pixel_ref[0, rows, :] - at_x
            delta_y = pixel_ref[1, rows, :] - at_y
            exponent = (scaled_a * delta_x + scaled_b * delta_y) * delta_x + scaled_c * delta_y * delta_y
            coverage = live_opacity * jnp.exp2(exponent)
            log_pass = jnp.log2(1.0 - coverage)
            high, low = halves(log_pass)
            prefix = dot(high, weight_ref[0]) + dot(low, weight_ref[0])
            weight = coverage * jnp.exp2(prefix)
            shade = [spread(columns[rows, channel : channel + 1], shape) for channel in range(3)]
            gain = shade[0] * colors[0] + shade[1] * colors[1] + shade[2] * colors[2]
            product = weight * gain
            high, low = halves(product)
            later = dot(high, weight_ref[1]) + dot(low, weight_ref[1])
            remain = jnp.exp2(prefix[:, SLOTS - 1 :] + log_pass[:, SLOTS - 1 :])
            later = later + spread(columns[rows, 3:4] * remain, shape)
            slope = product - coverage * jnp.exp2(-log_pass) * later
            slope_x = slope * delta_x
            slope_y = slope * delta_y
            parts = [slope, slope_x, slope_y, slope_x * delta_x, slope_x * delta_y, slope_y * delta_y]
            parts += [part * weight for part in shade]
            sums = [total + fold(part) for total, part in zip(sums, parts)]

        sums = [jnp.sum(part, axis=0, keepdims=True) for part in sums]
        total, sum_x, sum_y, sum_xx, sum_xy, sum_yy = (part * -0.5 for part in sums[:6])
        grads = [
            -2.0 * (conic_a * sum_x + conic_b * sum_y),
            -2.0 * (conic_b * sum_x + conic_c * sum_y),
            sum_xx,
            2.0 * sum_xy,
            sum_yy,
            -2.0 * total / opacity,
        ] + sums[6:]
        for feature, value in enumerate(grads):
            for half in range(2):
                grad_ref[pl.ds(feature * 8 + 2 * index + half, 1), :] = value[:, half * LANES : (half + 1) * LANES]
        return carry

    lax.fori_loop(0, TILES_DEV, tile, 0, unroll=TILES_DEV)

    slot = aux_ref[16 : 16 + CAP, :]
    wanted = aux_ref[16 + CAP : 16 + 2 * CAP, :].astype(F32)
    parts = [(slot[8 * part : 8 * part + 8] >> 7, slot[8 * part : 8 * part + 8] & (LANES - 1)) for part in range(2)]
    blocks = []
    for feature in range(FEATS):
        for at_row, at_lane in parts:
            value = jnp.zeros((8, LANES), F32)
            for row in range(8):
                grads = grad_ref[feature * 8 + row : feature * 8 + row + 1, :]
                value = jnp.where(at_row == row, pick(grads, at_lane), value)
            blocks.append(value)
    blocks += [wanted, geo_ref[0:16, :], jnp.zeros((PACK - FEATS * CAP - CAP - 16, LANES), F32)]
    store_rows(out_ref, jnp.concatenate(blocks, axis=0))


WIDE = 256
TALL = G_DEV // WIDE


def duplicate_kernel(returned_ref, own_ref, copies_ref, semaphores):
    own_ref[:LANES, :] = returned_ref[pl.ds(0, LANES, stride=2), :].T
    own_ref[LANES:, :] = returned_ref[pl.ds(1, LANES, stride=2), :].T[: SENT - LANES]
    copies = [
        pltpu.make_async_copy(own_ref, copies_ref.at[view], semaphores.at[view])
        for view in range(copies_ref.shape[0])
    ]
    for copy in copies:
        copy.start()
    for copy in copies:
        copy.wait()


def scatter_view(view, arrived_ref, place, grads_ref, camera_ref):
    tall_iota = iota((TALL, LANES), 0)
    wide_iota = iota((WIDE, LANES), 0)
    values = arrived_ref[view, : FEATS * CAP, :]
    wanted = arrived_ref[view, FEATS * CAP : FEATS * CAP + CAP, :].astype(jnp.int32)
    camera_ref[place] = arrived_ref[view, FEATS * CAP + CAP : SENT, :]
    high_place, low_place = wanted >> 8, wanted & (WIDE - 1)
    high, low = halves(values)
    high, low = high.astype(F32), low.astype(F32)
    lefts, rights = [], []
    for rank in range(CAP):
        at_high = tall_iota == spread(high_place[rank : rank + 1], (TALL, LANES))
        at_low = wide_iota == spread(low_place[rank : rank + 1], (WIDE, LANES))
        at_low = at_low.astype(F32).astype(BF16)
        for source in (high, low):
            rows = [source[index * CAP + rank : index * CAP + rank + 1] for index in range(FEATS)]
            left = [jnp.where(at_high, spread(row, (TALL, LANES)), 0.0) for row in rows]
            lefts.append(jnp.concatenate(left, axis=0).astype(BF16))
            rights.append(at_low)
    total = dot_lanes(jnp.concatenate(lefts, axis=1), jnp.concatenate(rights, axis=1))
    for half in range(2):
        grads_ref[place, pl.ds(half, FEATS * TALL, stride=2), :] = total[:, half * LANES : (half + 1) * LANES]


SHAPE_ROWS = (3, 4, 5, 6, 7, 8, 9, 59, 60)


def pull_view(chunk, place, center, shape, param, grads_ref, camera_ref, kept, keep):
    def cotangent(feature):
        return grads_ref[place, pl.ds(pl.multiple_of(feature * GROUPS + chunk * 8, 8), 8), :]

    def add(index, value):
        before = kept(index)
        keep(index, value if before is None else before + value)

    rotate, offset = camera_of(camera_ref[place])
    eye = camera_center(rotate, offset)
    basis, basis_back = jax.vjp(lambda spot: direction_basis(spot, eye), center)
    colors = [cotangent(6 + channel) for channel in range(3)]
    basis_grad = []
    for term in range(16):
        total = None
        for channel in range(3):
            index = 11 + 3 * term + channel
            add(index, basis[term] * colors[channel])
            piece = param(index) * colors[channel]
            total = piece if total is None else total + piece
        basis_grad.append(total)
    (along,) = basis_back(basis_grad)
    unused, screen_back = jax.vjp(
        lambda spot, matrix: screen_features(spot, matrix, rotate, offset), center, shape
    )
    moved, bent = screen_back([cotangent(index) for index in range(5)])
    for axis in range(3):
        add(axis, along[axis] + moved[axis])
    for row in range(3):
        for col in range(3):
            add(SHAPE_ROWS[3 * row + col], bent[row][col])
    add(10, cotangent(5))


def each_chunk(action):
    def body(chunk, carry):
        action(chunk)
        return carry

    lax.fori_loop(0, CHUNKS, body, 0)


def own_pullback_kernel(returned_ref, held_ref, out_ref, grads_ref, camera_ref, partial_ref, semaphores):
    def send(chunk):
        return pltpu.make_async_copy(partial_ref.at[chunk], out_ref.at[chunk], semaphores.at[chunk])

    scatter_view(0, returned_ref, 0, grads_ref, camera_ref)

    def step(chunk, carry):
        def param(index):
            return held_ref[chunk, pl.ds(index, 8, stride=PITCH), :]

        def keep(index, value):
            partial_ref[chunk, pl.ds(index, 8, stride=PITCH), :] = value

        center = [param(index) for index in range(3)]
        shape = shape_matrix([param(3 + index) for index in range(3)], [param(6 + index) for index in range(4)])
        pull_view(chunk, 0, center, shape, param, grads_ref, camera_ref, lambda index: None, keep)
        send(chunk).start()
        return carry

    lax.fori_loop(0, CHUNKS, step, 0)
    each_chunk(lambda chunk: send(chunk).wait())


def pullback_kernel(
    view_ref, arrived_ref, held_hbm, partial_hbm, out_ref,
    held_ref, partial_ref, sums_ref, grads_ref, camera_ref, staged_ref, held_sems, partial_sems, semaphores,
):
    views = arrived_ref.shape[0]

    def fetch_held(chunk):
        return pltpu.make_async_copy(held_hbm.at[chunk], held_ref.at[chunk], held_sems.at[chunk])

    def fetch_partial(chunk):
        return pltpu.make_async_copy(partial_hbm.at[chunk], partial_ref.at[chunk], partial_sems.at[chunk])

    def start(chunk):
        fetch_held(chunk).start()
        fetch_partial(chunk).start()

    each_chunk(start)

    def one_view(place, carry):
        view = lax.rem(view_ref[0] + 1 + place, views)
        scatter_view(view, arrived_ref, place, grads_ref, camera_ref)
        return carry

    lax.fori_loop(0, views - 1, one_view, 0)

    def send(chunk):
        columns = chunk_columns(chunk)
        return pltpu.make_async_copy(staged_ref.at[:, columns], out_ref.at[:, columns], semaphores.at[chunk])

    def step(chunk, carry):
        fetch_held(chunk).wait()
        fetch_partial(chunk).wait()

        def param(index):
            return held_ref[chunk, pl.ds(index, 8, stride=PITCH), :]

        def first(index):
            return partial_ref[chunk, pl.ds(index, 8, stride=PITCH), :]

        def keep(index, value):
            sums_ref[pl.ds(index, 8, stride=PITCH), :] = value

        def kept(index):
            return sums_ref[pl.ds(index, 8, stride=PITCH), :]

        center = [param(index) for index in range(3)]
        shape, shape_back = jax.vjp(
            shape_matrix, [param(3 + index) for index in range(3)], [param(6 + index) for index in range(4)]
        )
        for place in range(views - 1):
            pull_view(
                chunk, place, center, shape, param, grads_ref, camera_ref, kept if place else first, keep
            )
        scale_grad, quaternion_grad = shape_back(
            [[kept(SHAPE_ROWS[3 * row + col]) for col in range(3)] for row in range(3)]
        )
        opacity = 1.0 / (1.0 + jnp.exp(-param(10)))
        finals = list(scale_grad) + list(quaternion_grad) + [opacity * (1.0 - opacity) * kept(10)]
        for index, value in enumerate(finals):
            keep(3 + index, value)
        for group in range(CHUNK // LANES):
            columns = pl.ds(pl.multiple_of(chunk * CHUNK + group * LANES, LANES), LANES)
            staged_ref[:, columns] = sums_ref[group * PITCH : group * PITCH + PARAMS, :]
        send(chunk).start()
        return carry

    lax.fori_loop(0, CHUNKS, step, 0)
    each_chunk(lambda chunk: send(chunk).wait())


def call(kernel, out_shape, operands, smalls=(), scratch=(), **kwargs):
    spaces = [pltpu.SMEM if index < smalls else pltpu.VMEM for index in range(len(operands))]
    single = not isinstance(out_shape, (list, tuple))
    outs = pl.BlockSpec(memory_space=pltpu.VMEM)
    return pl.pallas_call(
        kernel,
        out_shape=out_shape,
        in_specs=[pl.BlockSpec(memory_space=space) for space in spaces],
        out_specs=outs if single else [outs] * len(out_shape),
        scratch_shapes=list(scratch),
        compiler_params=pltpu.CompilerParams(vmem_limit_bytes=VMEM_LIMIT),
        **kwargs,
    )(*operands)


HELD = jax.ShapeDtypeStruct((CHUNKS, 8 * PITCH, LANES), F32)


def route(tile_lists):
    return call(
        route_kernel,
        [
            jax.ShapeDtypeStruct((OWNERS, LANES), jnp.int32),
            jax.ShapeDtypeStruct((16 + 2 * CAP, LANES), jnp.int32),
        ],
        [tile_lists],
        smalls=0,
    )


def project(height, camera, first_tile, view, gauss_params):
    return pl.pallas_call(
        functools.partial(project_kernel, height),
        out_shape=[
            jax.ShapeDtypeStruct((FEATS, GROUPS, LANES), F32),
            HELD,
            jax.ShapeDtypeStruct((GEO, LANES), F32),
        ],
        in_specs=[pl.BlockSpec(memory_space=pltpu.SMEM)] * 3 + [pl.BlockSpec(memory_space=pltpu.HBM)],
        out_specs=[pl.BlockSpec(memory_space=pltpu.VMEM)] * 3,
        scratch_shapes=[
            pltpu.VMEM((PARAMS, G_DEV), F32),
            pltpu.SemaphoreType.DMA((CHUNKS,)),
        ],
        compiler_params=pltpu.CompilerParams(vmem_limit_bytes=VMEM_LIMIT),
    )(camera, first_tile, view, gauss_params)


def gather(requested, features):
    return call(
        gather_kernel, jax.ShapeDtypeStruct((2 * OWNERS, LANES), F32), [requested, features], smalls=0
    )


def render(height, tile_lengths, background, geometry, arrived, aux, cotangent):
    return call(
        functools.partial(render_kernel, height),
        jax.ShapeDtypeStruct((2 * OWNERS, LANES), F32),
        [tile_lengths, background, geometry, arrived, aux, cotangent],
        smalls=2,
        scratch=[
            pltpu.VMEM((FEATS * 8, LANES), F32),
            pltpu.VMEM((2 * OWNERS, LANES), F32),
            pltpu.VMEM((FEATS * 8, LANES), F32),
            pltpu.VMEM((2, PIX, SLOTS), F32),
            pltpu.VMEM((2, SLOTS, SLOTS), BF16),
        ],
    )


def duplicate(returned, views):
    return pl.pallas_call(
        duplicate_kernel,
        out_shape=[
            jax.ShapeDtypeStruct((SENT, LANES), F32),
            jax.ShapeDtypeStruct((views, SENT, LANES), F32),
        ],
        in_specs=[pl.BlockSpec(memory_space=pltpu.VMEM)],
        out_specs=[pl.BlockSpec(memory_space=pltpu.VMEM), pl.BlockSpec(memory_space=pltpu.HBM)],
        scratch_shapes=[pltpu.SemaphoreType.DMA((views,))],
        compiler_params=pltpu.CompilerParams(vmem_limit_bytes=VMEM_LIMIT),
    )(returned)


def own_pullback(own, held):
    return pl.pallas_call(
        own_pullback_kernel,
        out_shape=HELD,
        in_specs=[pl.BlockSpec(memory_space=pltpu.VMEM)] * 2,
        out_specs=pl.BlockSpec(memory_space=pltpu.HBM),
        scratch_shapes=[
            pltpu.VMEM((1, FEATS * GROUPS, LANES), F32),
            pltpu.VMEM((1, 16, LANES), F32),
            pltpu.VMEM(HELD.shape, F32),
            pltpu.SemaphoreType.DMA((CHUNKS,)),
        ],
        compiler_params=pltpu.CompilerParams(vmem_limit_bytes=VMEM_LIMIT),
        cost_estimate=pl.CostEstimate(flops=20_000_000, bytes_accessed=4_000_000, transcendentals=0),
    )(own.reshape((1,) + own.shape), held)


def pullback(view, arrived, held, partial):
    others = arrived.shape[0] - 1
    return pl.pallas_call(
        pullback_kernel,
        out_shape=jax.ShapeDtypeStruct((PARAMS, G_DEV), F32),
        in_specs=[
            pl.BlockSpec(memory_space=space) for space in (pltpu.SMEM, pltpu.VMEM, pltpu.HBM, pltpu.HBM)
        ],
        out_specs=pl.BlockSpec(memory_space=pltpu.HBM),
        scratch_shapes=[
            pltpu.VMEM(HELD.shape, F32),
            pltpu.VMEM(HELD.shape, F32),
            pltpu.VMEM((8 * PITCH, LANES), F32),
            pltpu.VMEM((others, FEATS * GROUPS, LANES), F32),
            pltpu.VMEM((others, 16, LANES), F32),
            pltpu.VMEM((PARAMS, G_DEV), F32),
            pltpu.SemaphoreType.DMA((CHUNKS,)),
            pltpu.SemaphoreType.DMA((CHUNKS,)),
            pltpu.SemaphoreType.DMA((CHUNKS,)),
        ],
        compiler_params=pltpu.CompilerParams(vmem_limit_bytes=LAST_VMEM_LIMIT),
    )(view, arrived, held, partial)


def per_device(gauss_params, camera, background, tile_lists, tile_lengths, pixel_cotangent):
    owners_total = lax.axis_size("img")
    views = lax.axis_size("view")
    tiles_here = tile_lists.shape[1]
    height = tiles_here * owners_total // TX
    first_tile = (lax.axis_index("img") * tiles_here).astype(jnp.int32).reshape(1)
    view = lax.axis_index("view").astype(jnp.int32).reshape(1)
    requests, aux = route(tile_lists)
    features, held, geometry = project(height, camera, first_tile, view, gauss_params)
    requested = lax.all_to_all(requests, "img", split_axis=0, concat_axis=0, tiled=True)
    outgoing = gather(requested, features)
    arrived = lax.all_to_all(outgoing, "img", split_axis=0, concat_axis=0, tiled=True)
    slot_grads = render(height, tile_lengths, background, geometry, arrived, aux, pixel_cotangent)
    returned = lax.all_to_all(slot_grads, "img", split_axis=0, concat_axis=0, tiled=True)
    own, copies = duplicate(returned, views)
    everyone = lax.all_to_all(copies, "view", split_axis=0, concat_axis=0, tiled=True)
    partial = own_pullback(own, held)
    return pullback(view, everyone, held, partial)


def solution(mesh):
    placed = (
        P(None, "img"),
        P("view", None),
        P(),
        P("view", "img", None),
        P("view", "img"),
        P("view", None, "img", None),
    )
    return jax.shard_map(
        per_device, mesh=mesh, in_specs=placed, out_specs=P(None, "img"), check_vma=False
    )
```

```python
import functools

import jax
import jax.numpy as jnp
from jax import lax
from jax.experimental import pallas as pl
from jax.experimental.pallas import tpu as pltpu
from jax.sharding import PartitionSpec as P

SIDE = 16
TX = 16
PIX = 256
SLOTS = 256
TILES_DEV = 4
OWNERS = 128
CAP = 16
LANES = 128
G_DEV = 8192
GROUPS = G_DEV // LANES
PARAMS = 59
PITCH = 65
CHUNKS = 8
CHUNK = G_DEV // CHUNKS
FEATS = 9
PACK = 256
SENT = FEATS * CAP + CAP + 16

FOCAL = 2.0
DILATION = 0.0001
SH_ZERO = 0.28209479177387814
SH_ONE = 0.4886025119029199
SH_TWO = (
    1.0925484305920792,
    -1.0925484305920792,
    0.31539156525252005,
    -1.0925484305920792,
    0.5462742152960396,
)
SH_THREE = (
    -0.5900435899266435,
    2.890611442640554,
    -0.4570457994644658,
    0.3731763325901154,
    -0.4570457994644658,
    1.445305721320277,
    -0.5900435899266435,
)

LOG2_E = 1.4426950408889634
F32 = jnp.float32
BF16 = jnp.bfloat16
VMEM_LIMIT = 16 * 1024 * 1024
ROUTE_VMEM_LIMIT = 60 * 1024 * 1024
WIDE_VMEM_LIMIT = 52 * 1024 * 1024


def iota(shape, axis, dtype=jnp.int32):
    return lax.broadcasted_iota(dtype, shape, axis)


def spread(row, shape):
    return jnp.broadcast_to(row, shape)


def halves(values):
    high = values.astype(BF16)
    low = (values - high.astype(F32)).astype(BF16)
    return high, low


def dot(left, right):
    return jnp.dot(left, right, preferred_element_type=F32)


def dot_lanes(left, right):
    return lax.dot_general(left, right, (((1,), (1,)), ((), ())), preferred_element_type=F32)


GEO = 24


def write_geometry(height, camera_ref, geo_ref):
    row = iota((8, LANES), 0)
    block = jnp.zeros((8, LANES), F32)
    for index in range(6):
        block = jnp.where(row == index, camera_ref[0, index], block)
    cosines, sines = jnp.cos(block), jnp.sin(block)
    cx, cy, cz = (cosines[index : index + 1, :] for index in range(3))
    sx, sy, sz = (sines[index : index + 1, :] for index in range(3))
    inner = [
        [cy, sy * sx, sy * cx],
        [None, cx, -sx],
        [-sy, cy * sx, cy * cx],
    ]
    entries = [
        [cz * inner[0][0], cz * inner[0][1] - sz * inner[1][1], cz * inner[0][2] - sz * inner[1][2]],
        [sz * inner[0][0], sz * inner[0][1] + cz * inner[1][1], sz * inner[0][2] + cz * inner[1][2]],
        inner[2],
    ]
    for index, value in enumerate(entries[0] + entries[1] + entries[2]):
        geo_ref[index : index + 1, :] = value
    geo_ref[9:12, :] = block[3:6, :]
    for index in range(TILES_DEV):
        tile_id = lax.axis_index("img") * TILES_DEV + index
        tile_x = ((tile_id % TX * SIDE).astype(F32) + 0.5) * (2.0 / (TX * SIDE)) - 1.0
        tile_y = ((tile_id // TX * SIDE).astype(F32) + 0.5) * (2.0 / (height * SIDE)) - 1.0
        geo_ref[12 + index : 13 + index, :] = jnp.full((1, LANES), tile_x, F32)
        geo_ref[16 + index : 17 + index, :] = jnp.full((1, LANES), tile_y, F32)
    geo_ref[20:GEO, :] = jnp.zeros((GEO - 20, LANES), F32)


def camera_of(geo):
    entries = [spread(geo[index : index + 1, :], (8, LANES)) for index in range(12)]
    return [entries[0:3], entries[3:6], entries[6:9]], entries[9:12]


def camera_center(rotate, offset):
    return [
        -(rotate[0][col] * offset[0] + rotate[1][col] * offset[1] + rotate[2][col] * offset[2])
        for col in range(3)
    ]


def shape_matrix(log_scales, quaternion):
    scales = [jnp.exp(value) for value in log_scales]
    norm = lax.rsqrt(
        quaternion[0] * quaternion[0]
        + quaternion[1] * quaternion[1]
        + quaternion[2] * quaternion[2]
        + quaternion[3] * quaternion[3]
    )
    real, im_i, im_j, im_k = (part * norm for part in quaternion)
    local = [
        [1.0 - 2.0 * (im_j * im_j + im_k * im_k), 2.0 * (im_i * im_j - real * im_k), 2.0 * (im_i * im_k + real * im_j)],
        [2.0 * (im_i * im_j + real * im_k), 1.0 - 2.0 * (im_i * im_i + im_k * im_k), 2.0 * (im_j * im_k - real * im_i)],
        [2.0 * (im_i * im_k - real * im_j), 2.0 * (im_j * im_k + real * im_i), 1.0 - 2.0 * (im_i * im_i + im_j * im_j)],
    ]
    return [[local[row][col] * scales[col] for col in range(3)] for row in range(3)]


def harmonics(along_x, along_y, along_z):
    square_x, square_y, square_z = along_x * along_x, along_y * along_y, along_z * along_z
    return [
        jnp.full_like(along_x, SH_ZERO),
        -SH_ONE * along_y,
        SH_ONE * along_z,
        -SH_ONE * along_x,
        SH_TWO[0] * along_x * along_y,
        SH_TWO[1] * along_y * along_z,
        SH_TWO[2] * (2.0 * square_z - square_x - square_y),
        SH_TWO[3] * along_x * along_z,
        SH_TWO[4] * (square_x - square_y),
        SH_THREE[0] * along_y * (3.0 * square_x - square_y),
        SH_THREE[1] * along_x * along_y * along_z,
        SH_THREE[2] * along_y * (4.0 * square_z - square_x - square_y),
        SH_THREE[3] * along_z * (2.0 * square_z - 3.0 * square_x - 3.0 * square_y),
        SH_THREE[4] * along_x * (4.0 * square_z - square_x - square_y),
        SH_THREE[5] * along_z * (square_x - square_y),
        SH_THREE[6] * along_x * (square_x - 3.0 * square_y),
    ]


def screen_features(center, shape, rotate, offset):
    viewed = [
        rotate[row][0] * center[0] + rotate[row][1] * center[1] + rotate[row][2] * center[2] + offset[row]
        for row in range(3)
    ]
    depth_inv = 1.0 / viewed[2]
    near = FOCAL * depth_inv
    screen_x = viewed[0] * near
    screen_y = viewed[1] * near
    slope_x = -screen_x * depth_inv
    slope_y = -screen_y * depth_inv
    to_camera = [
        [near * rotate[0][col] + slope_x * rotate[2][col] for col in range(3)],
        [near * rotate[1][col] + slope_y * rotate[2][col] for col in range(3)],
    ]
    mapped = [
        [
            to_camera[row][0] * shape[0][col] + to_camera[row][1] * shape[1][col] + to_camera[row][2] * shape[2][col]
            for col in range(3)
        ]
        for row in range(2)
    ]
    first, second = mapped
    cov_a = first[0] * first[0] + first[1] * first[1] + first[2] * first[2] + DILATION
    cov_b = first[0] * second[0] + first[1] * second[1] + first[2] * second[2]
    cov_c = second[0] * second[0] + second[1] * second[1] + second[2] * second[2] + DILATION
    inverse = 1.0 / (cov_a * cov_c - cov_b * cov_b)
    return [screen_x, screen_y, cov_c * inverse, -cov_b * inverse, cov_a * inverse]


def direction_basis(center, eye):
    toward = [center[index] - eye[index] for index in range(3)]
    norm = lax.rsqrt(toward[0] * toward[0] + toward[1] * toward[1] + toward[2] * toward[2])
    return harmonics(toward[0] * norm, toward[1] * norm, toward[2] * norm)


def chunk_columns(chunk):
    return pl.ds(pl.multiple_of(chunk * CHUNK, CHUNK), CHUNK)


def spread_columns(params_ref, held_ref, chunk):
    for group in range(CHUNK // LANES):
        columns = pl.ds(pl.multiple_of(chunk * CHUNK + group * LANES, LANES), LANES)
        held_ref[chunk, group * PITCH : group * PITCH + PARAMS, :] = params_ref[:, columns]


def each_chunk(action):
    def body(chunk, carry):
        action(chunk)
        return carry

    lax.fori_loop(0, CHUNKS, body, 0)


def project_kernel(
    height, camera_hbm, params_ref, feats_ref, geo_ref, out_ref,
    staged_ref, held_ref, camera_ref, semaphores, out_semaphores, camera_semaphore,
):
    def fetch(chunk):
        columns = chunk_columns(chunk)
        return pltpu.make_async_copy(params_ref.at[:, columns], staged_ref.at[:, columns], semaphores.at[chunk])

    def keep(chunk):
        return pltpu.make_async_copy(held_ref.at[chunk], out_ref.at[chunk], out_semaphores.at[chunk])

    camera_copy = pltpu.make_async_copy(camera_hbm, camera_ref, camera_semaphore)
    camera_copy.start()
    each_chunk(lambda chunk: fetch(chunk).start())
    camera_copy.wait()
    write_geometry(height, camera_ref, geo_ref)
    rotate, offset = camera_of(geo_ref[...])
    eye = camera_center(rotate, offset)

    def step(chunk, carry):
        fetch(chunk).wait()
        spread_columns(staged_ref, held_ref, chunk)
        keep(chunk).start()

        def param(index):
            return held_ref[chunk, pl.ds(index, 8, stride=PITCH), :]

        center = [param(index) for index in range(3)]
        shape = shape_matrix([param(3 + index) for index in range(3)], [param(6 + index) for index in range(4)])
        screen = screen_features(center, shape, rotate, offset)
        basis = direction_basis(center, eye)
        opacity = 1.0 / (1.0 + jnp.exp(-param(10)))
        colors = []
        for channel in range(3):
            total = basis[0] * param(11 + channel)
            for term in range(1, 16):
                total = total + basis[term] * param(11 + 3 * term + channel)
            colors.append(total + 0.5)
        rows = pl.ds(pl.multiple_of(chunk * 8, 8), 8)
        for index, value in enumerate(screen + [opacity] + colors):
            feats_ref[index, rows, :] = value
        return carry

    lax.fori_loop(0, CHUNKS, step, 0)
    each_chunk(lambda chunk: keep(chunk).wait())


def route_kernel(lists_hbm, request_ref, aux_ref, lists_ref, semaphore):
    lists_copy = pltpu.make_async_copy(lists_hbm, lists_ref, semaphore)
    lists_copy.start()
    owner_iota = iota((OWNERS, LANES), 0)
    before = (iota((LANES, 2 * LANES), 0) < iota((LANES, 2 * LANES), 1)).astype(F32)
    before = before.astype(BF16)
    rank_iota = iota((CAP, LANES), 0)
    lane = iota((1, LANES), 1)
    carried = jnp.zeros((OWNERS, LANES), F32)
    table = jnp.zeros((4 * CAP, OWNERS), F32)
    lists_copy.wait()
    for row in range(8):
        ids = lists_ref[0, row // 2 : row // 2 + 1, (row % 2) * LANES : (row % 2 + 1) * LANES]
        owner = ids // G_DEV
        column = ids % G_DEV
        hot = owner_iota == spread(owner, (OWNERS, LANES))
        hot_f32 = hot.astype(F32)
        hot_bf16 = hot_f32.astype(BF16)
        counts = dot(hot_bf16, before)
        rank = jnp.sum(jnp.where(hot, counts[:, :LANES] + carried, 0.0), axis=0, keepdims=True)
        carried = carried + counts[:, LANES:]
        rank = rank.astype(jnp.int32)
        at_rank = rank_iota == spread(rank, (CAP, LANES))
        pieces = [column // LANES, column % LANES, lane * 0 + row, lane + 1]
        stacked = jnp.concatenate(
            [jnp.where(at_rank, spread(piece.astype(F32), (CAP, LANES)), 0.0) for piece in pieces], axis=0
        )
        table = table + dot_lanes(stacked.astype(BF16), hot_bf16)
        aux_ref[row : row + 1, :] = owner
        aux_ref[8 + row : 9 + row, :] = rank
    high, low, slot_row, slot_lane = (table[CAP * part : CAP * (part + 1)] for part in range(4))
    used = slot_lane > 0.5
    slot = jnp.where(used, slot_row * LANES + slot_lane - 1.0, -1.0)
    wanted = jnp.where(used, high * LANES + low, -1.0)
    aux_ref[16 : 16 + CAP, :] = slot.astype(jnp.int32)
    aux_ref[16 + CAP : 16 + 2 * CAP, :] = wanted.astype(jnp.int32)
    padded = jnp.concatenate([wanted, jnp.zeros((LANES - CAP, OWNERS), F32)], axis=0)
    request_ref[...] = padded.T.astype(jnp.int32)


LANE_GATHER = lax.GatherDimensionNumbers(
    offset_dims=(),
    collapsed_slice_dims=(1,),
    start_index_map=(1,),
    operand_batching_dims=(0,),
    start_indices_batching_dims=(0,),
)


def pick(row, lanes_at):
    return lax.gather(
        spread(row, (8, LANES)),
        lanes_at[:, :, None],
        LANE_GATHER,
        slice_sizes=(1, 1),
        mode=lax.GatherScatterMode.PROMISE_IN_BOUNDS,
    )


def store_rows(out_ref, table):
    out_ref[pl.ds(0, LANES, stride=2), :] = table[:LANES].T
    out_ref[pl.ds(1, LANES, stride=2), :] = table[LANES:].T


def gather_kernel(request_ref, feats_ref, out_ref):
    wanted = request_ref[...].astype(F32).T[:CAP].astype(jnp.int32)
    high, low = wanted >> 7, wanted & (LANES - 1)
    parts = [(high[:8], low[:8]), (high[8:], low[8:])]

    def step(group, found):
        found = list(found)
        for index in range(FEATS):
            row = feats_ref[index, pl.ds(group, 1), :]
            for part, (at_group, at_lane) in enumerate(parts):
                place = 2 * index + part
                found[place] = jnp.where(at_group == group, pick(row, at_lane), found[place])
        return tuple(found)

    start = tuple(jnp.zeros((8, LANES), F32) for _ in range(2 * FEATS))
    found = lax.fori_loop(0, GROUPS, step, start, unroll=16)
    table = jnp.concatenate(list(found) + [jnp.zeros((PACK - FEATS * CAP, LANES), F32)], axis=0)
    store_rows(out_ref, table)


PIX_CHUNK = 128


def render_kernel(
    height, lengths_ref, background_ref, geo_ref, arrived_ref, aux_ref, cotangent_ref, out_ref,
    slot_ref, table_ref, grad_ref, pixel_ref, weight_ref,
):
    table_ref[:LANES, :] = arrived_ref[pl.ds(0, LANES, stride=2), :].T
    table_ref[LANES:, :] = arrived_ref[pl.ds(1, LANES, stride=2), :].T
    owner = aux_ref[0:8, :]
    rank = aux_ref[8:16, :]
    at_rank = [rank == place for place in range(CAP)]
    for index in range(FEATS):
        value = jnp.zeros((8, LANES), F32)
        for place in range(CAP):
            row = table_ref[index * CAP + place : index * CAP + place + 1, :]
            value = jnp.where(at_rank[place], pick(row, owner), value)
        slot_ref[index * 8 : index * 8 + 8, :] = value

    within = iota((PIX, SLOTS), 0)
    pixel_ref[0] = (within % SIDE).astype(F32) * (2.0 / (TX * SIDE))
    pixel_ref[1] = (within // SIDE).astype(F32) * (2.0 / (height * SIDE))
    slot_row, slot_col = iota((SLOTS, SLOTS), 0), iota((SLOTS, SLOTS), 1)
    weight_ref[0] = (slot_row < slot_col).astype(F32).astype(BF16)
    weight_ref[1] = (slot_row > slot_col).astype(F32).astype(BF16)
    slot_place = iota((1, SLOTS), 1)
    def tile(index, carry):
        def slots(feature):
            return jnp.concatenate(
                [slot_ref[pl.ds(feature * 8 + 2 * index + half, 1), :] for half in range(2)], axis=1
            )

        tile_x, tile_y = geo_ref[pl.ds(12 + index, 1), :], geo_ref[pl.ds(16 + index, 1), :]
        at_x = slots(0) - jnp.concatenate([tile_x] * 2, axis=1)
        at_y = slots(1) - jnp.concatenate([tile_y] * 2, axis=1)
        conic_a, conic_b, conic_c = slots(2), slots(3), slots(4)
        opacity = slots(5)
        live_opacity = jnp.where(slot_place < lengths_ref[0, index], opacity, 0.0)
        colors = [slots(6 + channel) for channel in range(3)]
        scaled_a, scaled_b, scaled_c = (-0.5 * LOG2_E) * conic_a, -LOG2_E * conic_b, (-0.5 * LOG2_E) * conic_c
        shades = [cotangent_ref[0, channel, pl.ds(index, 1), :] for channel in range(3)]
        behind = (
            shades[0] * background_ref[0] + shades[1] * background_ref[1] + shades[2] * background_ref[2]
        )
        columns = jnp.concatenate(shades + [behind, jnp.zeros((4, PIX), F32)], axis=0).T

        def fold(values):
            return jnp.sum(values.reshape(PIX_CHUNK // 8, 8, SLOTS), axis=0)

        sums = [jnp.zeros((8, SLOTS), F32) for _ in range(9)]
        for chunk in range(PIX // PIX_CHUNK):
            rows = slice(chunk * PIX_CHUNK, (chunk + 1) * PIX_CHUNK)
            shape = (PIX_CHUNK, SLOTS)
            delta_x = pixel_ref[0, rows, :] - at_x
            delta_y = pixel_ref[1, rows, :] - at_y
            exponent = (scaled_a * delta_x + scaled_b * delta_y) * delta_x + scaled_c * delta_y * delta_y
            coverage = live_opacity * jnp.exp2(exponent)
            log_pass = jnp.log2(1.0 - coverage)
            high, low = halves(log_pass)
            prefix = dot(high, weight_ref[0]) + dot(low, weight_ref[0])
            weight = coverage * jnp.exp2(prefix)
            shade = [spread(columns[rows, channel : channel + 1], shape) for channel in range(3)]
            gain = shade[0] * colors[0] + shade[1] * colors[1] + shade[2] * colors[2]
            product = weight * gain
            high, low = halves(product)
            later = dot(high, weight_ref[1]) + dot(low, weight_ref[1])
            remain = jnp.exp2(prefix[:, SLOTS - 1 :] + log_pass[:, SLOTS - 1 :])
            later = later + spread(columns[rows, 3:4] * remain, shape)
            slope = product - coverage * jnp.exp2(-log_pass) * later
            slope_x = slope * delta_x
            slope_y = slope * delta_y
            parts = [slope, slope_x, slope_y, slope_x * delta_x, slope_x * delta_y, slope_y * delta_y]
            parts += [part * weight for part in shade]
            sums = [total + fold(part) for total, part in zip(sums, parts)]

        sums = [jnp.sum(part, axis=0, keepdims=True) for part in sums]
        total, sum_x, sum_y, sum_xx, sum_xy, sum_yy = (part * -0.5 for part in sums[:6])
        grads = [
            -2.0 * (conic_a * sum_x + conic_b * sum_y),
            -2.0 * (conic_b * sum_x + conic_c * sum_y),
            sum_xx,
            2.0 * sum_xy,
            sum_yy,
            -2.0 * total / opacity,
        ] + sums[6:]
        for feature, value in enumerate(grads):
            for half in range(2):
                grad_ref[pl.ds(feature * 8 + 2 * index + half, 1), :] = value[:, half * LANES : (half + 1) * LANES]
        return carry

    lax.fori_loop(0, TILES_DEV, tile, 0, unroll=TILES_DEV)

    slot = aux_ref[16 : 16 + CAP, :]
    wanted = aux_ref[16 + CAP : 16 + 2 * CAP, :].astype(F32)
    parts = [(slot[8 * part : 8 * part + 8] >> 7, slot[8 * part : 8 * part + 8] & (LANES - 1)) for part in range(2)]
    blocks = []
    for feature in range(FEATS):
        for at_row, at_lane in parts:
            value = jnp.zeros((8, LANES), F32)
            for row in range(8):
                grads = grad_ref[feature * 8 + row : feature * 8 + row + 1, :]
                value = jnp.where(at_row == row, pick(grads, at_lane), value)
            blocks.append(value)
    blocks += [wanted, geo_ref[0:16, :], jnp.zeros((PACK - FEATS * CAP - CAP - 16, LANES), F32)]
    store_rows(out_ref, jnp.concatenate(blocks, axis=0))


WIDE = 256
TALL = G_DEV // WIDE


def duplicate_kernel(returned_ref, own_ref, copies_ref, semaphores):
    own_ref[:LANES, :] = returned_ref[pl.ds(0, LANES, stride=2), :].T
    own_ref[LANES:, :] = returned_ref[pl.ds(1, LANES, stride=2), :].T[: SENT - LANES]
    copies = [
        pltpu.make_async_copy(own_ref, copies_ref.at[view], semaphores.at[view])
        for view in range(copies_ref.shape[0])
    ]
    for copy in copies:
        copy.start()
    for copy in copies:
        copy.wait()


def scatter_view(view, arrived_ref, place, grads_ref, camera_ref):
    tall_iota = iota((TALL, LANES), 0)
    wide_iota = iota((WIDE, LANES), 0)
    values = arrived_ref[view, : FEATS * CAP, :]
    wanted = arrived_ref[view, FEATS * CAP : FEATS * CAP + CAP, :].astype(jnp.int32)
    camera_ref[place] = arrived_ref[view, FEATS * CAP + CAP : SENT, :]
    high_place, low_place = wanted >> 8, wanted & (WIDE - 1)
    high, low = halves(values)
    high, low = high.astype(F32), low.astype(F32)
    lefts, rights = [], []
    for rank in range(CAP):
        at_high = tall_iota == spread(high_place[rank : rank + 1], (TALL, LANES))
        at_low = wide_iota == spread(low_place[rank : rank + 1], (WIDE, LANES))
        at_low = at_low.astype(F32).astype(BF16)
        for source in (high, low):
            rows = [source[index * CAP + rank : index * CAP + rank + 1] for index in range(FEATS)]
            left = [jnp.where(at_high, spread(row, (TALL, LANES)), 0.0) for row in rows]
            lefts.append(jnp.concatenate(left, axis=0).astype(BF16))
            rights.append(at_low)
    total = dot_lanes(jnp.concatenate(lefts, axis=1), jnp.concatenate(rights, axis=1))
    for half in range(2):
        grads_ref[place, pl.ds(half, FEATS * TALL, stride=2), :] = total[:, half * LANES : (half + 1) * LANES]


SHAPE_ROWS = (3, 4, 5, 6, 7, 8, 9, 59, 60)


def pull_view(chunk, place, center, shape, param, grads_ref, camera_ref, kept, keep):
    def cotangent(feature):
        return grads_ref[place, pl.ds(pl.multiple_of(feature * GROUPS + chunk * 8, 8), 8), :]

    def add(index, value):
        before = kept(index)
        keep(index, value if before is None else before + value)

    rotate, offset = camera_of(camera_ref[place])
    eye = camera_center(rotate, offset)
    basis, basis_back = jax.vjp(lambda spot: direction_basis(spot, eye), center)
    colors = [cotangent(6 + channel) for channel in range(3)]
    basis_grad = []
    for term in range(16):
        total = None
        for channel in range(3):
            index = 11 + 3 * term + channel
            add(index, basis[term] * colors[channel])
            piece = param(index) * colors[channel]
            total = piece if total is None else total + piece
        basis_grad.append(total)
    (along,) = basis_back(basis_grad)
    unused, screen_back = jax.vjp(
        lambda spot, matrix: screen_features(spot, matrix, rotate, offset), center, shape
    )
    moved, bent = screen_back([cotangent(index) for index in range(5)])
    for axis in range(3):
        add(axis, along[axis] + moved[axis])
    for row in range(3):
        for col in range(3):
            add(SHAPE_ROWS[3 * row + col], bent[row][col])
    add(10, cotangent(5))


def own_pullback_kernel(
    returned_ref, held_hbm, out_ref, held_ref, grads_ref, camera_ref, partial_ref, held_sems, semaphores
):
    def fetch(chunk):
        return pltpu.make_async_copy(held_hbm.at[chunk], held_ref.at[chunk], held_sems.at[chunk])

    def send(chunk):
        return pltpu.make_async_copy(partial_ref.at[chunk], out_ref.at[chunk], semaphores.at[chunk])

    each_chunk(lambda chunk: fetch(chunk).start())
    scatter_view(0, returned_ref, 0, grads_ref, camera_ref)

    def step(chunk, carry):
        fetch(chunk).wait()

        def param(index):
            return held_ref[chunk, pl.ds(index, 8, stride=PITCH), :]

        def keep(index, value):
            partial_ref[chunk, pl.ds(index, 8, stride=PITCH), :] = value

        center = [param(index) for index in range(3)]
        shape = shape_matrix([param(3 + index) for index in range(3)], [param(6 + index) for index in range(4)])
        pull_view(chunk, 0, center, shape, param, grads_ref, camera_ref, lambda index: None, keep)
        send(chunk).start()
        return carry

    lax.fori_loop(0, CHUNKS, step, 0)
    each_chunk(lambda chunk: send(chunk).wait())


def pullback_kernel(
    arrived_ref, held_hbm, partial_hbm, out_ref,
    held_ref, partial_ref, sums_ref, grads_ref, camera_ref, staged_ref, held_sems, partial_sems, semaphores,
):
    views = arrived_ref.shape[0]

    def fetch_held(chunk):
        return pltpu.make_async_copy(held_hbm.at[chunk], held_ref.at[chunk], held_sems.at[chunk])

    def fetch_partial(chunk):
        return pltpu.make_async_copy(partial_hbm.at[chunk], partial_ref.at[chunk], partial_sems.at[chunk])

    def start(chunk):
        fetch_held(chunk).start()
        fetch_partial(chunk).start()

    each_chunk(start)

    def one_view(place, carry):
        view = lax.rem(lax.axis_index("view") + 1 + place, views)
        scatter_view(view, arrived_ref, place, grads_ref, camera_ref)
        return carry

    lax.fori_loop(0, views - 1, one_view, 0)

    def send(chunk):
        columns = chunk_columns(chunk)
        return pltpu.make_async_copy(staged_ref.at[:, columns], out_ref.at[:, columns], semaphores.at[chunk])

    def step(chunk, carry):
        fetch_held(chunk).wait()
        fetch_partial(chunk).wait()

        def param(index):
            return held_ref[chunk, pl.ds(index, 8, stride=PITCH), :]

        def first(index):
            return partial_ref[chunk, pl.ds(index, 8, stride=PITCH), :]

        def keep(index, value):
            sums_ref[pl.ds(index, 8, stride=PITCH), :] = value

        def kept(index):
            return sums_ref[pl.ds(index, 8, stride=PITCH), :]

        center = [param(index) for index in range(3)]
        shape, shape_back = jax.vjp(
            shape_matrix, [param(3 + index) for index in range(3)], [param(6 + index) for index in range(4)]
        )
        for place in range(views - 1):
            pull_view(
                chunk, place, center, shape, param, grads_ref, camera_ref, kept if place else first, keep
            )
        scale_grad, quaternion_grad = shape_back(
            [[kept(SHAPE_ROWS[3 * row + col]) for col in range(3)] for row in range(3)]
        )
        opacity = 1.0 / (1.0 + jnp.exp(-param(10)))
        finals = list(scale_grad) + list(quaternion_grad) + [opacity * (1.0 - opacity) * kept(10)]
        for index, value in enumerate(finals):
            keep(3 + index, value)
        for group in range(CHUNK // LANES):
            columns = pl.ds(pl.multiple_of(chunk * CHUNK + group * LANES, LANES), LANES)
            staged_ref[:, columns] = sums_ref[group * PITCH : group * PITCH + PARAMS, :]
        send(chunk).start()
        return carry

    lax.fori_loop(0, CHUNKS, step, 0)
    each_chunk(lambda chunk: send(chunk).wait())


def call(kernel, out_shape, operands, smalls=(), scratch=(), **kwargs):
    spaces = [pltpu.SMEM if index < smalls else pltpu.VMEM for index in range(len(operands))]
    single = not isinstance(out_shape, (list, tuple))
    outs = pl.BlockSpec(memory_space=pltpu.VMEM)
    return pl.pallas_call(
        kernel,
        out_shape=out_shape,
        in_specs=[pl.BlockSpec(memory_space=space) for space in spaces],
        out_specs=outs if single else [outs] * len(out_shape),
        scratch_shapes=list(scratch),
        compiler_params=pltpu.CompilerParams(vmem_limit_bytes=VMEM_LIMIT),
        **kwargs,
    )(*operands)


HELD = jax.ShapeDtypeStruct((CHUNKS, 8 * PITCH, LANES), F32)


def route(tile_lists):
    return pl.pallas_call(
        route_kernel,
        out_shape=[
            jax.ShapeDtypeStruct((OWNERS, LANES), jnp.int32),
            jax.ShapeDtypeStruct((16 + 2 * CAP, LANES), jnp.int32),
        ],
        in_specs=[pl.BlockSpec(memory_space=pl.ANY)],
        out_specs=[pl.BlockSpec(memory_space=pltpu.VMEM)] * 2,
        scratch_shapes=[
            pltpu.VMEM(tile_lists.shape, jnp.int32),
            pltpu.SemaphoreType.DMA,
        ],
        compiler_params=pltpu.CompilerParams(vmem_limit_bytes=ROUTE_VMEM_LIMIT),
    )(tile_lists)


def project(height, camera, gauss_params):
    return pl.pallas_call(
        functools.partial(project_kernel, height),
        out_shape=[
            jax.ShapeDtypeStruct((FEATS, GROUPS, LANES), F32),
            jax.ShapeDtypeStruct((GEO, LANES), F32),
            HELD,
        ],
        in_specs=[pl.BlockSpec(memory_space=pl.ANY)] * 2,
        out_specs=[pl.BlockSpec(memory_space=space) for space in (pltpu.VMEM, pltpu.VMEM, pl.ANY)],
        scratch_shapes=[
            pltpu.VMEM((PARAMS, G_DEV), F32),
            pltpu.VMEM(HELD.shape, F32),
            pltpu.SMEM(camera.shape, F32),
            pltpu.SemaphoreType.DMA((CHUNKS,)),
            pltpu.SemaphoreType.DMA((CHUNKS,)),
            pltpu.SemaphoreType.DMA,
        ],
        compiler_params=pltpu.CompilerParams(vmem_limit_bytes=WIDE_VMEM_LIMIT),
    )(camera, gauss_params)


def gather(requested, features):
    return call(
        gather_kernel, jax.ShapeDtypeStruct((2 * OWNERS, LANES), F32), [requested, features], smalls=0
    )


def render(height, tile_lengths, background, geometry, arrived, aux, cotangent):
    return call(
        functools.partial(render_kernel, height),
        jax.ShapeDtypeStruct((2 * OWNERS, LANES), F32),
        [tile_lengths, background, geometry, arrived, aux, cotangent],
        smalls=2,
        scratch=[
            pltpu.VMEM((FEATS * 8, LANES), F32),
            pltpu.VMEM((2 * OWNERS, LANES), F32),
            pltpu.VMEM((FEATS * 8, LANES), F32),
            pltpu.VMEM((2, PIX, SLOTS), F32),
            pltpu.VMEM((2, SLOTS, SLOTS), BF16),
        ],
    )


def duplicate(returned, views):
    return pl.pallas_call(
        duplicate_kernel,
        out_shape=[
            jax.ShapeDtypeStruct((SENT, LANES), F32),
            jax.ShapeDtypeStruct((views, SENT, LANES), F32),
        ],
        in_specs=[pl.BlockSpec(memory_space=pltpu.VMEM)],
        out_specs=[pl.BlockSpec(memory_space=pltpu.VMEM), pl.BlockSpec(memory_space=pl.ANY)],
        scratch_shapes=[pltpu.SemaphoreType.DMA((views,))],
        compiler_params=pltpu.CompilerParams(vmem_limit_bytes=VMEM_LIMIT),
    )(returned)


def own_pullback(own, held):
    return pl.pallas_call(
        own_pullback_kernel,
        out_shape=HELD,
        in_specs=[pl.BlockSpec(memory_space=pltpu.VMEM), pl.BlockSpec(memory_space=pl.ANY)],
        out_specs=pl.BlockSpec(memory_space=pl.ANY),
        scratch_shapes=[
            pltpu.VMEM(HELD.shape, F32),
            pltpu.VMEM((1, FEATS * GROUPS, LANES), F32),
            pltpu.VMEM((1, 16, LANES), F32),
            pltpu.VMEM(HELD.shape, F32),
            pltpu.SemaphoreType.DMA((CHUNKS,)),
            pltpu.SemaphoreType.DMA((CHUNKS,)),
        ],
        compiler_params=pltpu.CompilerParams(vmem_limit_bytes=WIDE_VMEM_LIMIT),
        cost_estimate=pl.CostEstimate(flops=20_000_000, bytes_accessed=4_000_000, transcendentals=0),
    )(own.reshape((1,) + own.shape), held)


def pullback(arrived, held, partial):
    others = arrived.shape[0] - 1
    return pl.pallas_call(
        pullback_kernel,
        out_shape=jax.ShapeDtypeStruct((PARAMS, G_DEV), F32),
        in_specs=[
            pl.BlockSpec(memory_space=space) for space in (pltpu.VMEM, pl.ANY, pl.ANY)
        ],
        out_specs=pl.BlockSpec(memory_space=pl.ANY),
        scratch_shapes=[
            pltpu.VMEM(HELD.shape, F32),
            pltpu.VMEM(HELD.shape, F32),
            pltpu.VMEM((8 * PITCH, LANES), F32),
            pltpu.VMEM((others, FEATS * GROUPS, LANES), F32),
            pltpu.VMEM((others, 16, LANES), F32),
            pltpu.VMEM((PARAMS, G_DEV), F32),
            pltpu.SemaphoreType.DMA((CHUNKS,)),
            pltpu.SemaphoreType.DMA((CHUNKS,)),
            pltpu.SemaphoreType.DMA((CHUNKS,)),
        ],
        compiler_params=pltpu.CompilerParams(vmem_limit_bytes=WIDE_VMEM_LIMIT),
    )(arrived, held, partial)


def per_device(gauss_params, camera, background, tile_lists, tile_lengths, pixel_cotangent):
    owners_total = lax.axis_size("img")
    views = lax.axis_size("view")
    tiles_here = tile_lists.shape[1]
    height = tiles_here * owners_total // TX
    requests, aux = route(tile_lists)
    features, geometry, held = project(height, camera, gauss_params)
    requested = lax.all_to_all(requests, "img", split_axis=0, concat_axis=0, tiled=True)
    outgoing = gather(requested, features)
    arrived = lax.all_to_all(outgoing, "img", split_axis=0, concat_axis=0, tiled=True)
    slot_grads = render(height, tile_lengths, background, geometry, arrived, aux, pixel_cotangent)
    returned = lax.all_to_all(slot_grads, "img", split_axis=0, concat_axis=0, tiled=True)
    own, copies = duplicate(returned, views)
    everyone = lax.all_to_all(copies, "view", split_axis=0, concat_axis=0, tiled=True)
    partial = own_pullback(own, held)
    return pullback(everyone, held, partial)


def solution(mesh):
    placed = (
        P(None, "img"),
        P("view", None),
        P(),
        P("view", "img", None),
        P("view", "img"),
        P("view", None, "img", None),
    )
    return jax.shard_map(
        per_device, mesh=mesh, in_specs=placed, out_specs=P(None, "img"), check_vma=False
    )
```

```python
import functools

import jax
import jax.numpy as jnp
from jax import lax
from jax.experimental import pallas as pl
from jax.experimental.pallas import tpu as pltpu
from jax.sharding import PartitionSpec as P

SIDE = 16
TX = 16
PIX = 256
SLOTS = 256
TILES_DEV = 4
OWNERS = 128
CAP = 16
LANES = 128
G_DEV = 8192
GROUPS = G_DEV // LANES
PARAMS = 59
PITCH = 65
CHUNKS = 8
CHUNK = G_DEV // CHUNKS
FEATS = 9
PACK = 256
SENT = FEATS * CAP + CAP + 16

FOCAL = 2.0
DILATION = 0.0001
SH_ZERO = 0.28209479177387814
SH_ONE = 0.4886025119029199
SH_TWO = (
    1.0925484305920792,
    -1.0925484305920792,
    0.31539156525252005,
    -1.0925484305920792,
    0.5462742152960396,
)
SH_THREE = (
    -0.5900435899266435,
    2.890611442640554,
    -0.4570457994644658,
    0.3731763325901154,
    -0.4570457994644658,
    1.445305721320277,
    -0.5900435899266435,
)

LOG2_E = 1.4426950408889634
F32 = jnp.float32
BF16 = jnp.bfloat16
VMEM_LIMIT = 16 * 1024 * 1024
ROUTE_VMEM_LIMIT = 60 * 1024 * 1024
WIDE_VMEM_LIMIT = 52 * 1024 * 1024


def iota(shape, axis, dtype=jnp.int32):
    return lax.broadcasted_iota(dtype, shape, axis)


def spread(row, shape):
    return jnp.broadcast_to(row, shape)


def halves(values):
    high = values.astype(BF16)
    low = (values - high.astype(F32)).astype(BF16)
    return high, low


def dot(left, right):
    return jnp.dot(left, right, preferred_element_type=F32)


def dot_lanes(left, right):
    return lax.dot_general(left, right, (((1,), (1,)), ((), ())), preferred_element_type=F32)


GEO = 24


def write_geometry(height, camera_ref, geo_ref):
    row = iota((8, LANES), 0)
    block = jnp.zeros((8, LANES), F32)
    for index in range(6):
        block = jnp.where(row == index, camera_ref[0, index], block)
    cosines, sines = jnp.cos(block), jnp.sin(block)
    cx, cy, cz = (cosines[index : index + 1, :] for index in range(3))
    sx, sy, sz = (sines[index : index + 1, :] for index in range(3))
    inner = [
        [cy, sy * sx, sy * cx],
        [None, cx, -sx],
        [-sy, cy * sx, cy * cx],
    ]
    entries = [
        [cz * inner[0][0], cz * inner[0][1] - sz * inner[1][1], cz * inner[0][2] - sz * inner[1][2]],
        [sz * inner[0][0], sz * inner[0][1] + cz * inner[1][1], sz * inner[0][2] + cz * inner[1][2]],
        inner[2],
    ]
    for index, value in enumerate(entries[0] + entries[1] + entries[2]):
        geo_ref[index : index + 1, :] = value
    geo_ref[9:12, :] = block[3:6, :]
    for index in range(TILES_DEV):
        tile_id = lax.axis_index("img") * TILES_DEV + index
        tile_x = ((tile_id % TX * SIDE).astype(F32) + 0.5) * (2.0 / (TX * SIDE)) - 1.0
        tile_y = ((tile_id // TX * SIDE).astype(F32) + 0.5) * (2.0 / (height * SIDE)) - 1.0
        geo_ref[12 + index : 13 + index, :] = jnp.full((1, LANES), tile_x, F32)
        geo_ref[16 + index : 17 + index, :] = jnp.full((1, LANES), tile_y, F32)
    geo_ref[20:GEO, :] = jnp.zeros((GEO - 20, LANES), F32)


def camera_of(geo):
    entries = [spread(geo[index : index + 1, :], (8, LANES)) for index in range(12)]
    return [entries[0:3], entries[3:6], entries[6:9]], entries[9:12]


def camera_center(rotate, offset):
    return [
        -(rotate[0][col] * offset[0] + rotate[1][col] * offset[1] + rotate[2][col] * offset[2])
        for col in range(3)
    ]


def shape_matrix(log_scales, quaternion):
    scales = [jnp.exp(value) for value in log_scales]
    norm = lax.rsqrt(
        quaternion[0] * quaternion[0]
        + quaternion[1] * quaternion[1]
        + quaternion[2] * quaternion[2]
        + quaternion[3] * quaternion[3]
    )
    real, im_i, im_j, im_k = (part * norm for part in quaternion)
    local = [
        [1.0 - 2.0 * (im_j * im_j + im_k * im_k), 2.0 * (im_i * im_j - real * im_k), 2.0 * (im_i * im_k + real * im_j)],
        [2.0 * (im_i * im_j + real * im_k), 1.0 - 2.0 * (im_i * im_i + im_k * im_k), 2.0 * (im_j * im_k - real * im_i)],
        [2.0 * (im_i * im_k - real * im_j), 2.0 * (im_j * im_k + real * im_i), 1.0 - 2.0 * (im_i * im_i + im_j * im_j)],
    ]
    return [[local[row][col] * scales[col] for col in range(3)] for row in range(3)]


def harmonics(along_x, along_y, along_z):
    square_x, square_y, square_z = along_x * along_x, along_y * along_y, along_z * along_z
    return [
        jnp.full_like(along_x, SH_ZERO),
        -SH_ONE * along_y,
        SH_ONE * along_z,
        -SH_ONE * along_x,
        SH_TWO[0] * along_x * along_y,
        SH_TWO[1] * along_y * along_z,
        SH_TWO[2] * (2.0 * square_z - square_x - square_y),
        SH_TWO[3] * along_x * along_z,
        SH_TWO[4] * (square_x - square_y),
        SH_THREE[0] * along_y * (3.0 * square_x - square_y),
        SH_THREE[1] * along_x * along_y * along_z,
        SH_THREE[2] * along_y * (4.0 * square_z - square_x - square_y),
        SH_THREE[3] * along_z * (2.0 * square_z - 3.0 * square_x - 3.0 * square_y),
        SH_THREE[4] * along_x * (4.0 * square_z - square_x - square_y),
        SH_THREE[5] * along_z * (square_x - square_y),
        SH_THREE[6] * along_x * (square_x - 3.0 * square_y),
    ]


def screen_features(center, shape, rotate, offset):
    viewed = [
        rotate[row][0] * center[0] + rotate[row][1] * center[1] + rotate[row][2] * center[2] + offset[row]
        for row in range(3)
    ]
    depth_inv = 1.0 / viewed[2]
    near = FOCAL * depth_inv
    screen_x = viewed[0] * near
    screen_y = viewed[1] * near
    slope_x = -screen_x * depth_inv
    slope_y = -screen_y * depth_inv
    to_camera = [
        [near * rotate[0][col] + slope_x * rotate[2][col] for col in range(3)],
        [near * rotate[1][col] + slope_y * rotate[2][col] for col in range(3)],
    ]
    mapped = [
        [
            to_camera[row][0] * shape[0][col] + to_camera[row][1] * shape[1][col] + to_camera[row][2] * shape[2][col]
            for col in range(3)
        ]
        for row in range(2)
    ]
    first, second = mapped
    cov_a = first[0] * first[0] + first[1] * first[1] + first[2] * first[2] + DILATION
    cov_b = first[0] * second[0] + first[1] * second[1] + first[2] * second[2]
    cov_c = second[0] * second[0] + second[1] * second[1] + second[2] * second[2] + DILATION
    inverse = 1.0 / (cov_a * cov_c - cov_b * cov_b)
    return [screen_x, screen_y, cov_c * inverse, -cov_b * inverse, cov_a * inverse]


def direction_basis(center, eye):
    toward = [center[index] - eye[index] for index in range(3)]
    norm = lax.rsqrt(toward[0] * toward[0] + toward[1] * toward[1] + toward[2] * toward[2])
    return harmonics(toward[0] * norm, toward[1] * norm, toward[2] * norm)


def chunk_columns(chunk):
    return pl.ds(pl.multiple_of(chunk * CHUNK, CHUNK), CHUNK)


def spread_columns(params_ref, held_ref, chunk):
    for group in range(CHUNK // LANES):
        columns = pl.ds(pl.multiple_of(chunk * CHUNK + group * LANES, LANES), LANES)
        held_ref[chunk, group * PITCH : group * PITCH + PARAMS, :] = params_ref[:, columns]


def each_chunk(action):
    def body(chunk, carry):
        action(chunk)
        return carry

    lax.fori_loop(0, CHUNKS, body, 0)


def project_kernel(
    height, camera_hbm, params_ref, feats_ref, geo_ref, out_ref,
    staged_ref, held_ref, camera_ref, semaphores, out_semaphores, camera_semaphore,
):
    def fetch(chunk):
        columns = chunk_columns(chunk)
        return pltpu.make_async_copy(params_ref.at[:, columns], staged_ref.at[:, columns], semaphores.at[chunk])

    def keep(chunk):
        return pltpu.make_async_copy(held_ref.at[chunk], out_ref.at[chunk], out_semaphores.at[chunk])

    camera_copy = pltpu.make_async_copy(camera_hbm, camera_ref, camera_semaphore)
    camera_copy.start()
    each_chunk(lambda chunk: fetch(chunk).start())
    camera_copy.wait()
    write_geometry(height, camera_ref, geo_ref)
    rotate, offset = camera_of(geo_ref[...])
    eye = camera_center(rotate, offset)

    def step(chunk, carry):
        fetch(chunk).wait()
        spread_columns(staged_ref, held_ref, chunk)
        keep(chunk).start()

        def param(index):
            return held_ref[chunk, pl.ds(index, 8, stride=PITCH), :]

        center = [param(index) for index in range(3)]
        shape = shape_matrix([param(3 + index) for index in range(3)], [param(6 + index) for index in range(4)])
        screen = screen_features(center, shape, rotate, offset)
        basis = direction_basis(center, eye)
        opacity = 1.0 / (1.0 + jnp.exp(-param(10)))
        colors = []
        for channel in range(3):
            total = basis[0] * param(11 + channel)
            for term in range(1, 16):
                total = total + basis[term] * param(11 + 3 * term + channel)
            colors.append(total + 0.5)
        rows = pl.ds(pl.multiple_of(chunk * 8, 8), 8)
        for index, value in enumerate(screen + [opacity] + colors):
            feats_ref[index, rows, :] = value
        return carry

    lax.fori_loop(0, CHUNKS, step, 0)
    each_chunk(lambda chunk: keep(chunk).wait())


def route_kernel(lists_hbm, request_ref, aux_ref, lists_ref, semaphore):
    lists_copy = pltpu.make_async_copy(lists_hbm, lists_ref, semaphore)
    lists_copy.start()
    owner_iota = iota((OWNERS, LANES), 0)
    before = (iota((LANES, 2 * LANES), 0) < iota((LANES, 2 * LANES), 1)).astype(F32)
    before = before.astype(BF16)
    rank_iota = iota((CAP, LANES), 0)
    lane = iota((1, LANES), 1)
    carried = jnp.zeros((OWNERS, LANES), F32)
    table = jnp.zeros((4 * CAP, OWNERS), F32)
    lists_copy.wait()
    for row in range(8):
        ids = lists_ref[0, row // 2 : row // 2 + 1, (row % 2) * LANES : (row % 2 + 1) * LANES]
        owner = ids // G_DEV
        column = ids % G_DEV
        hot = owner_iota == spread(owner, (OWNERS, LANES))
        hot_f32 = hot.astype(F32)
        hot_bf16 = hot_f32.astype(BF16)
        counts = dot(hot_bf16, before)
        rank = jnp.sum(jnp.where(hot, counts[:, :LANES] + carried, 0.0), axis=0, keepdims=True)
        carried = carried + counts[:, LANES:]
        rank = rank.astype(jnp.int32)
        at_rank = rank_iota == spread(rank, (CAP, LANES))
        pieces = [column // LANES, column % LANES, lane * 0 + row, lane + 1]
        stacked = jnp.concatenate(
            [jnp.where(at_rank, spread(piece.astype(F32), (CAP, LANES)), 0.0) for piece in pieces], axis=0
        )
        table = table + dot_lanes(stacked.astype(BF16), hot_bf16)
        aux_ref[row : row + 1, :] = owner
        aux_ref[8 + row : 9 + row, :] = rank
    high, low, slot_row, slot_lane = (table[CAP * part : CAP * (part + 1)] for part in range(4))
    used = slot_lane > 0.5
    slot = jnp.where(used, slot_row * LANES + slot_lane - 1.0, -1.0)
    wanted = jnp.where(used, high * LANES + low, -1.0)
    aux_ref[16 : 16 + CAP, :] = slot.astype(jnp.int32)
    aux_ref[16 + CAP : 16 + 2 * CAP, :] = wanted.astype(jnp.int32)
    padded = jnp.concatenate([wanted, jnp.zeros((LANES - CAP, OWNERS), F32)], axis=0)
    request_ref[...] = padded.T.astype(jnp.int32)


LANE_GATHER = lax.GatherDimensionNumbers(
    offset_dims=(),
    collapsed_slice_dims=(1,),
    start_index_map=(1,),
    operand_batching_dims=(0,),
    start_indices_batching_dims=(0,),
)


def pick(row, lanes_at):
    return lax.gather(
        spread(row, (8, LANES)),
        lanes_at[:, :, None],
        LANE_GATHER,
        slice_sizes=(1, 1),
        mode=lax.GatherScatterMode.PROMISE_IN_BOUNDS,
    )


def store_rows(out_ref, table):
    out_ref[pl.ds(0, LANES, stride=2), :] = table[:LANES].T
    out_ref[pl.ds(1, LANES, stride=2), :] = table[LANES:].T


WIDE = 256
TALL = G_DEV // WIDE
EXACT = 2


def split(values, parts):
    pieces = []
    for _ in range(parts):
        piece = values.astype(BF16)
        pieces.append(piece)
        values = values - piece.astype(F32)
    return pieces


def gather_kernel(request_ref, feats_ref, out_ref, table_ref):
    wanted = request_ref[...].astype(F32).T[:CAP].astype(jnp.int32)
    high, low = wanted >> 7, wanted & (LANES - 1)
    parts = [(high[:8], low[:8]), (high[8:], low[8:])]
    high_place, low_place = wanted >> 8, wanted & (WIDE - 1)
    tall_iota, wide_iota = iota((TALL, LANES), 0), iota((WIDE, LANES), 0)

    pieces, counts = [], []
    for index in range(EXACT, FEATS):
        wide = jnp.concatenate(
            [feats_ref[index, pl.ds(half, TALL, stride=2), :] for half in range(2)], axis=1
        )
        counts.append(3 if index < 5 else 2)
        pieces += split(wide, counts[-1])
    left = jnp.concatenate(pieces, axis=0)

    found = [jnp.zeros((8, LANES), F32) for _ in range(2 * EXACT)]
    for pair in range(CAP // 2):
        rights = []
        for rank in (2 * pair, 2 * pair + 1):
            at_low = wide_iota == spread(low_place[rank : rank + 1], (WIDE, LANES))
            rights.append(at_low.astype(F32).astype(BF16))
        product = dot(left, jnp.concatenate(rights, axis=1))
        for group in range(pair * (GROUPS // 8), (pair + 1) * (GROUPS // 8)):
            for index in range(EXACT):
                row = feats_ref[index, group : group + 1, :]
                for part, (at_group, at_lane) in enumerate(parts):
                    place = 2 * index + part
                    found[place] = jnp.where(at_group == group, pick(row, at_lane), found[place])
        for half, rank in enumerate((2 * pair, 2 * pair + 1)):
            at_high = tall_iota == spread(high_place[rank : rank + 1], (TALL, LANES))
            lanes = slice(half * LANES, (half + 1) * LANES)
            first = 0
            for index, count in enumerate(counts):
                total = product[first : first + TALL, lanes]
                for piece in range(1, count):
                    total = total + product[first + piece * TALL : first + (piece + 1) * TALL, lanes]
                first += count * TALL
                value = jnp.sum(jnp.where(at_high, total, 0.0), axis=0, keepdims=True)
                place = (EXACT + index) * CAP + rank
                table_ref[place : place + 1, :] = value
    table_ref[: EXACT * CAP, :] = jnp.concatenate(found, axis=0)
    table_ref[FEATS * CAP :, :] = jnp.zeros((PACK - FEATS * CAP, LANES), F32)
    store_rows(out_ref, table_ref[...])


PIX_CHUNK = 128


def render_kernel(
    height, lengths_ref, background_ref, geo_ref, arrived_ref, aux_ref, cotangent_ref, out_ref,
    slot_ref, table_ref, grad_ref, pixel_ref, weight_ref,
):
    table_ref[:LANES, :] = arrived_ref[pl.ds(0, LANES, stride=2), :].T
    table_ref[LANES:, :] = arrived_ref[pl.ds(1, LANES, stride=2), :].T
    owner = aux_ref[0:8, :]
    rank = aux_ref[8:16, :]
    at_rank = [rank == place for place in range(CAP)]
    for index in range(FEATS):
        value = jnp.zeros((8, LANES), F32)
        for place in range(CAP):
            row = table_ref[index * CAP + place : index * CAP + place + 1, :]
            value = jnp.where(at_rank[place], pick(row, owner), value)
        slot_ref[index * 8 : index * 8 + 8, :] = value

    within = iota((PIX, SLOTS), 0)
    pixel_ref[0] = (within % SIDE).astype(F32) * (2.0 / (TX * SIDE))
    pixel_ref[1] = (within // SIDE).astype(F32) * (2.0 / (height * SIDE))
    slot_row, slot_col = iota((SLOTS, SLOTS), 0), iota((SLOTS, SLOTS), 1)
    weight_ref[0] = (slot_row < slot_col).astype(F32).astype(BF16)
    weight_ref[1] = (slot_row > slot_col).astype(F32).astype(BF16)
    slot_place = iota((1, SLOTS), 1)
    def tile(index, carry):
        def slots(feature):
            return jnp.concatenate(
                [slot_ref[pl.ds(feature * 8 + 2 * index + half, 1), :] for half in range(2)], axis=1
            )

        tile_x, tile_y = geo_ref[pl.ds(12 + index, 1), :], geo_ref[pl.ds(16 + index, 1), :]
        at_x = slots(0) - jnp.concatenate([tile_x] * 2, axis=1)
        at_y = slots(1) - jnp.concatenate([tile_y] * 2, axis=1)
        conic_a, conic_b, conic_c = slots(2), slots(3), slots(4)
        opacity = slots(5)
        live_opacity = jnp.where(slot_place < lengths_ref[0, index], opacity, 0.0)
        colors = [slots(6 + channel) for channel in range(3)]
        scaled_a, scaled_b, scaled_c = (-0.5 * LOG2_E) * conic_a, -LOG2_E * conic_b, (-0.5 * LOG2_E) * conic_c
        shades = [cotangent_ref[0, channel, pl.ds(index, 1), :] for channel in range(3)]
        behind = (
            shades[0] * background_ref[0] + shades[1] * background_ref[1] + shades[2] * background_ref[2]
        )
        columns = jnp.concatenate(shades + [behind, jnp.zeros((4, PIX), F32)], axis=0).T

        def fold(values):
            return jnp.sum(values.reshape(PIX_CHUNK // 8, 8, SLOTS), axis=0)

        sums = [jnp.zeros((8, SLOTS), F32) for _ in range(9)]
        for chunk in range(PIX // PIX_CHUNK):
            rows = slice(chunk * PIX_CHUNK, (chunk + 1) * PIX_CHUNK)
            shape = (PIX_CHUNK, SLOTS)
            delta_x = pixel_ref[0, rows, :] - at_x
            delta_y = pixel_ref[1, rows, :] - at_y
            exponent = (scaled_a * delta_x + scaled_b * delta_y) * delta_x + scaled_c * delta_y * delta_y
            coverage = live_opacity * jnp.exp2(exponent)
            log_pass = jnp.log2(1.0 - coverage)
            high, low = halves(log_pass)
            prefix = dot(high, weight_ref[0]) + dot(low, weight_ref[0])
            weight = coverage * jnp.exp2(prefix)
            shade = [spread(columns[rows, channel : channel + 1], shape) for channel in range(3)]
            gain = shade[0] * colors[0] + shade[1] * colors[1] + shade[2] * colors[2]
            product = weight * gain
            high, low = halves(product)
            later = dot(high, weight_ref[1]) + dot(low, weight_ref[1])
            remain = jnp.exp2(prefix[:, SLOTS - 1 :] + log_pass[:, SLOTS - 1 :])
            later = later + spread(columns[rows, 3:4] * remain, shape)
            slope = product - coverage * jnp.exp2(-log_pass) * later
            slope_x = slope * delta_x
            slope_y = slope * delta_y
            parts = [slope, slope_x, slope_y, slope_x * delta_x, slope_x * delta_y, slope_y * delta_y]
            parts += [part * weight for part in shade]
            sums = [total + fold(part) for total, part in zip(sums, parts)]

        sums = [jnp.sum(part, axis=0, keepdims=True) for part in sums]
        total, sum_x, sum_y, sum_xx, sum_xy, sum_yy = (part * -0.5 for part in sums[:6])
        grads = [
            -2.0 * (conic_a * sum_x + conic_b * sum_y),
            -2.0 * (conic_b * sum_x + conic_c * sum_y),
            sum_xx,
            2.0 * sum_xy,
            sum_yy,
            -2.0 * total / opacity,
        ] + sums[6:]
        for feature, value in enumerate(grads):
            for half in range(2):
                grad_ref[pl.ds(feature * 8 + 2 * index + half, 1), :] = value[:, half * LANES : (half + 1) * LANES]
        return carry

    lax.fori_loop(0, TILES_DEV, tile, 0, unroll=TILES_DEV)

    slot = aux_ref[16 : 16 + CAP, :]
    wanted = aux_ref[16 + CAP : 16 + 2 * CAP, :].astype(F32)
    parts = [(slot[8 * part : 8 * part + 8] >> 7, slot[8 * part : 8 * part + 8] & (LANES - 1)) for part in range(2)]
    blocks = []
    for feature in range(FEATS):
        for at_row, at_lane in parts:
            value = jnp.zeros((8, LANES), F32)
            for row in range(8):
                grads = grad_ref[feature * 8 + row : feature * 8 + row + 1, :]
                value = jnp.where(at_row == row, pick(grads, at_lane), value)
            blocks.append(value)
    blocks += [wanted, geo_ref[0:16, :], jnp.zeros((PACK - FEATS * CAP - CAP - 16, LANES), F32)]
    store_rows(out_ref, jnp.concatenate(blocks, axis=0))


def duplicate_kernel(returned_ref, own_ref, copies_ref, semaphores):
    own_ref[:LANES, :] = returned_ref[pl.ds(0, LANES, stride=2), :].T
    own_ref[LANES:, :] = returned_ref[pl.ds(1, LANES, stride=2), :].T[: SENT - LANES]
    copies = [
        pltpu.make_async_copy(own_ref, copies_ref.at[view], semaphores.at[view])
        for view in range(copies_ref.shape[0])
    ]
    for copy in copies:
        copy.start()
    for copy in copies:
        copy.wait()


def scatter_view(view, arrived_ref, place, grads_ref, camera_ref):
    tall_iota = iota((TALL, LANES), 0)
    wide_iota = iota((WIDE, LANES), 0)
    values = arrived_ref[view, : FEATS * CAP, :]
    wanted = arrived_ref[view, FEATS * CAP : FEATS * CAP + CAP, :].astype(jnp.int32)
    camera_ref[place] = arrived_ref[view, FEATS * CAP + CAP : SENT, :]
    high_place, low_place = wanted >> 8, wanted & (WIDE - 1)
    high, low = halves(values)
    high, low = high.astype(F32), low.astype(F32)
    lefts, rights = [], []
    for rank in range(CAP):
        at_high = tall_iota == spread(high_place[rank : rank + 1], (TALL, LANES))
        at_low = wide_iota == spread(low_place[rank : rank + 1], (WIDE, LANES))
        at_low = at_low.astype(F32).astype(BF16)
        for source in (high, low):
            rows = [source[index * CAP + rank : index * CAP + rank + 1] for index in range(FEATS)]
            left = [jnp.where(at_high, spread(row, (TALL, LANES)), 0.0) for row in rows]
            lefts.append(jnp.concatenate(left, axis=0).astype(BF16))
            rights.append(at_low)
    total = dot_lanes(jnp.concatenate(lefts, axis=1), jnp.concatenate(rights, axis=1))
    for half in range(2):
        grads_ref[place, pl.ds(half, FEATS * TALL, stride=2), :] = total[:, half * LANES : (half + 1) * LANES]


SHAPE_ROWS = (3, 4, 5, 6, 7, 8, 9, 59, 60)


def pull_view(chunk, place, center, shape, param, grads_ref, camera_ref, kept, keep):
    def cotangent(feature):
        return grads_ref[place, pl.ds(pl.multiple_of(feature * GROUPS + chunk * 8, 8), 8), :]

    def add(index, value):
        before = kept(index)
        keep(index, value if before is None else before + value)

    rotate, offset = camera_of(camera_ref[place])
    eye = camera_center(rotate, offset)
    basis, basis_back = jax.vjp(lambda spot: direction_basis(spot, eye), center)
    colors = [cotangent(6 + channel) for channel in range(3)]
    basis_grad = []
    for term in range(16):
        total = None
        for channel in range(3):
            index = 11 + 3 * term + channel
            add(index, basis[term] * colors[channel])
            piece = param(index) * colors[channel]
            total = piece if total is None else total + piece
        basis_grad.append(total)
    (along,) = basis_back(basis_grad)
    unused, screen_back = jax.vjp(
        lambda spot, matrix: screen_features(spot, matrix, rotate, offset), center, shape
    )
    moved, bent = screen_back([cotangent(index) for index in range(5)])
    for axis in range(3):
        add(axis, along[axis] + moved[axis])
    for row in range(3):
        for col in range(3):
            add(SHAPE_ROWS[3 * row + col], bent[row][col])
    add(10, cotangent(5))


def own_pullback_kernel(
    returned_ref, held_hbm, out_ref, held_ref, grads_ref, camera_ref, partial_ref, held_sems, semaphores
):
    def fetch(chunk):
        return pltpu.make_async_copy(held_hbm.at[chunk], held_ref.at[chunk], held_sems.at[chunk])

    def send(chunk):
        return pltpu.make_async_copy(partial_ref.at[chunk], out_ref.at[chunk], semaphores.at[chunk])

    each_chunk(lambda chunk: fetch(chunk).start())
    scatter_view(0, returned_ref, 0, grads_ref, camera_ref)

    def step(chunk, carry):
        fetch(chunk).wait()

        def param(index):
            return held_ref[chunk, pl.ds(index, 8, stride=PITCH), :]

        def keep(index, value):
            partial_ref[chunk, pl.ds(index, 8, stride=PITCH), :] = value

        center = [param(index) for index in range(3)]
        shape = shape_matrix([param(3 + index) for index in range(3)], [param(6 + index) for index in range(4)])
        pull_view(chunk, 0, center, shape, param, grads_ref, camera_ref, lambda index: None, keep)
        send(chunk).start()
        return carry

    lax.fori_loop(0, CHUNKS, step, 0)
    each_chunk(lambda chunk: send(chunk).wait())


def pullback_kernel(
    arrived_ref, held_hbm, partial_hbm, out_ref,
    held_ref, partial_ref, sums_ref, grads_ref, camera_ref, staged_ref, held_sems, partial_sems, semaphores,
):
    views = arrived_ref.shape[0]

    def fetch_held(chunk):
        return pltpu.make_async_copy(held_hbm.at[chunk], held_ref.at[chunk], held_sems.at[chunk])

    def fetch_partial(chunk):
        return pltpu.make_async_copy(partial_hbm.at[chunk], partial_ref.at[chunk], partial_sems.at[chunk])

    def start(chunk):
        fetch_held(chunk).start()
        fetch_partial(chunk).start()

    each_chunk(start)

    def one_view(place, carry):
        view = lax.rem(lax.axis_index("view") + 1 + place, views)
        scatter_view(view, arrived_ref, place, grads_ref, camera_ref)
        return carry

    lax.fori_loop(0, views - 1, one_view, 0, unroll=True)

    def send(chunk):
        columns = chunk_columns(chunk)
        return pltpu.make_async_copy(staged_ref.at[:, columns], out_ref.at[:, columns], semaphores.at[chunk])

    def step(chunk, carry):
        fetch_held(chunk).wait()
        fetch_partial(chunk).wait()

        def param(index):
            return held_ref[chunk, pl.ds(index, 8, stride=PITCH), :]

        def first(index):
            return partial_ref[chunk, pl.ds(index, 8, stride=PITCH), :]

        def keep(index, value):
            sums_ref[pl.ds(index, 8, stride=PITCH), :] = value

        def kept(index):
            return sums_ref[pl.ds(index, 8, stride=PITCH), :]

        center = [param(index) for index in range(3)]
        shape, shape_back = jax.vjp(
            shape_matrix, [param(3 + index) for index in range(3)], [param(6 + index) for index in range(4)]
        )
        for place in range(views - 1):
            pull_view(
                chunk, place, center, shape, param, grads_ref, camera_ref, kept if place else first, keep
            )
        scale_grad, quaternion_grad = shape_back(
            [[kept(SHAPE_ROWS[3 * row + col]) for col in range(3)] for row in range(3)]
        )
        opacity = 1.0 / (1.0 + jnp.exp(-param(10)))
        finals = list(scale_grad) + list(quaternion_grad) + [opacity * (1.0 - opacity) * kept(10)]
        for index, value in enumerate(finals):
            keep(3 + index, value)
        for group in range(CHUNK // LANES):
            columns = pl.ds(pl.multiple_of(chunk * CHUNK + group * LANES, LANES), LANES)
            staged_ref[:, columns] = sums_ref[group * PITCH : group * PITCH + PARAMS, :]
        send(chunk).start()
        return carry

    lax.fori_loop(0, CHUNKS, step, 0)
    each_chunk(lambda chunk: send(chunk).wait())


def call(kernel, out_shape, operands, smalls=(), scratch=(), **kwargs):
    spaces = [pltpu.SMEM if index < smalls else pltpu.VMEM for index in range(len(operands))]
    single = not isinstance(out_shape, (list, tuple))
    outs = pl.BlockSpec(memory_space=pltpu.VMEM)
    return pl.pallas_call(
        kernel,
        out_shape=out_shape,
        in_specs=[pl.BlockSpec(memory_space=space) for space in spaces],
        out_specs=outs if single else [outs] * len(out_shape),
        scratch_shapes=list(scratch),
        compiler_params=pltpu.CompilerParams(vmem_limit_bytes=VMEM_LIMIT),
        **kwargs,
    )(*operands)


HELD = jax.ShapeDtypeStruct((CHUNKS, 8 * PITCH, LANES), F32)


def route(tile_lists):
    return pl.pallas_call(
        route_kernel,
        out_shape=[
            jax.ShapeDtypeStruct((OWNERS, LANES), jnp.int32),
            jax.ShapeDtypeStruct((16 + 2 * CAP, LANES), jnp.int32),
        ],
        in_specs=[pl.BlockSpec(memory_space=pl.ANY)],
        out_specs=[pl.BlockSpec(memory_space=pltpu.VMEM)] * 2,
        scratch_shapes=[
            pltpu.VMEM(tile_lists.shape, jnp.int32),
            pltpu.SemaphoreType.DMA,
        ],
        compiler_params=pltpu.CompilerParams(vmem_limit_bytes=ROUTE_VMEM_LIMIT),
    )(tile_lists)


def project(height, camera, gauss_params):
    return pl.pallas_call(
        functools.partial(project_kernel, height),
        out_shape=[
            jax.ShapeDtypeStruct((FEATS, GROUPS, LANES), F32),
            jax.ShapeDtypeStruct((GEO, LANES), F32),
            HELD,
        ],
        in_specs=[pl.BlockSpec(memory_space=pl.ANY)] * 2,
        out_specs=[pl.BlockSpec(memory_space=space) for space in (pltpu.VMEM, pltpu.VMEM, pl.ANY)],
        scratch_shapes=[
            pltpu.VMEM((PARAMS, G_DEV), F32),
            pltpu.VMEM(HELD.shape, F32),
            pltpu.SMEM(camera.shape, F32),
            pltpu.SemaphoreType.DMA((CHUNKS,)),
            pltpu.SemaphoreType.DMA((CHUNKS,)),
            pltpu.SemaphoreType.DMA,
        ],
        compiler_params=pltpu.CompilerParams(vmem_limit_bytes=WIDE_VMEM_LIMIT),
    )(camera, gauss_params)


def gather(requested, features):
    return call(
        gather_kernel,
        jax.ShapeDtypeStruct((2 * OWNERS, LANES), F32),
        [requested, features],
        smalls=0,
        scratch=[pltpu.VMEM((PACK, LANES), F32)],
    )


def render(height, tile_lengths, background, geometry, arrived, aux, cotangent):
    return call(
        functools.partial(render_kernel, height),
        jax.ShapeDtypeStruct((2 * OWNERS, LANES), F32),
        [tile_lengths, background, geometry, arrived, aux, cotangent],
        smalls=2,
        scratch=[
            pltpu.VMEM((FEATS * 8, LANES), F32),
            pltpu.VMEM((2 * OWNERS, LANES), F32),
            pltpu.VMEM((FEATS * 8, LANES), F32),
            pltpu.VMEM((2, PIX, SLOTS), F32),
            pltpu.VMEM((2, SLOTS, SLOTS), BF16),
        ],
    )


def duplicate(returned, views):
    return pl.pallas_call(
        duplicate_kernel,
        out_shape=[
            jax.ShapeDtypeStruct((SENT, LANES), F32),
            jax.ShapeDtypeStruct((views, SENT, LANES), F32),
        ],
        in_specs=[pl.BlockSpec(memory_space=pltpu.VMEM)],
        out_specs=[pl.BlockSpec(memory_space=pltpu.VMEM), pl.BlockSpec(memory_space=pl.ANY)],
        scratch_shapes=[pltpu.SemaphoreType.DMA((views,))],
        compiler_params=pltpu.CompilerParams(vmem_limit_bytes=VMEM_LIMIT),
    )(returned)


def own_pullback(own, held):
    return pl.pallas_call(
        own_pullback_kernel,
        out_shape=HELD,
        in_specs=[pl.BlockSpec(memory_space=pltpu.VMEM), pl.BlockSpec(memory_space=pl.ANY)],
        out_specs=pl.BlockSpec(memory_space=pl.ANY),
        scratch_shapes=[
            pltpu.VMEM(HELD.shape, F32),
            pltpu.VMEM((1, FEATS * GROUPS, LANES), F32),
            pltpu.VMEM((1, 16, LANES), F32),
            pltpu.VMEM(HELD.shape, F32),
            pltpu.SemaphoreType.DMA((CHUNKS,)),
            pltpu.SemaphoreType.DMA((CHUNKS,)),
        ],
        compiler_params=pltpu.CompilerParams(vmem_limit_bytes=WIDE_VMEM_LIMIT),
        cost_estimate=pl.CostEstimate(flops=20_000_000, bytes_accessed=4_000_000, transcendentals=0),
    )(own.reshape((1,) + own.shape), held)


def pullback(arrived, held, partial):
    others = arrived.shape[0] - 1
    return pl.pallas_call(
        pullback_kernel,
        out_shape=jax.ShapeDtypeStruct((PARAMS, G_DEV), F32),
        in_specs=[
            pl.BlockSpec(memory_space=space) for space in (pltpu.VMEM, pl.ANY, pl.ANY)
        ],
        out_specs=pl.BlockSpec(memory_space=pl.ANY),
        scratch_shapes=[
            pltpu.VMEM(HELD.shape, F32),
            pltpu.VMEM(HELD.shape, F32),
            pltpu.VMEM((8 * PITCH, LANES), F32),
            pltpu.VMEM((others, FEATS * GROUPS, LANES), F32),
            pltpu.VMEM((others, 16, LANES), F32),
            pltpu.VMEM((PARAMS, G_DEV), F32),
            pltpu.SemaphoreType.DMA((CHUNKS,)),
            pltpu.SemaphoreType.DMA((CHUNKS,)),
            pltpu.SemaphoreType.DMA((CHUNKS,)),
        ],
        compiler_params=pltpu.CompilerParams(vmem_limit_bytes=WIDE_VMEM_LIMIT),
    )(arrived, held, partial)


def per_device(gauss_params, camera, background, tile_lists, tile_lengths, pixel_cotangent):
    owners_total = lax.axis_size("img")
    views = lax.axis_size("view")
    tiles_here = tile_lists.shape[1]
    height = tiles_here * owners_total // TX
    requests, aux = route(tile_lists)
    features, geometry, held = project(height, camera, gauss_params)
    requested = lax.all_to_all(requests, "img", split_axis=0, concat_axis=0, tiled=True)
    outgoing = gather(requested, features)
    arrived = lax.all_to_all(outgoing, "img", split_axis=0, concat_axis=0, tiled=True)
    slot_grads = render(height, tile_lengths, background, geometry, arrived, aux, pixel_cotangent)
    returned = lax.all_to_all(slot_grads, "img", split_axis=0, concat_axis=0, tiled=True)
    own, copies = duplicate(returned, views)
    everyone = lax.all_to_all(copies, "view", split_axis=0, concat_axis=0, tiled=True)
    partial = own_pullback(own, held)
    return pullback(everyone, held, partial)


def solution(mesh):
    placed = (
        P(None, "img"),
        P("view", None),
        P(),
        P("view", "img", None),
        P("view", "img"),
        P("view", None, "img", None),
    )
    return jax.shard_map(
        per_device, mesh=mesh, in_specs=placed, out_specs=P(None, "img"), check_vma=False
    )
```

```python
import functools

import jax
import jax.numpy as jnp
from jax import lax
from jax.experimental import pallas as pl
from jax.experimental.pallas import tpu as pltpu
from jax.sharding import PartitionSpec as P

SIDE = 16
TX = 16
PIX = 256
SLOTS = 256
TILES_DEV = 4
OWNERS = 128
CAP = 16
LANES = 128
G_DEV = 8192
GROUPS = G_DEV // LANES
PARAMS = 59
PITCH = 65
CHUNKS = 8
CHUNK = G_DEV // CHUNKS
FEATS = 9
PACK = 256
SENT = FEATS * CAP + CAP + 16

FOCAL = 2.0
DILATION = 0.0001
SH_ZERO = 0.28209479177387814
SH_ONE = 0.4886025119029199
SH_TWO = (
    1.0925484305920792,
    -1.0925484305920792,
    0.31539156525252005,
    -1.0925484305920792,
    0.5462742152960396,
)
SH_THREE = (
    -0.5900435899266435,
    2.890611442640554,
    -0.4570457994644658,
    0.3731763325901154,
    -0.4570457994644658,
    1.445305721320277,
    -0.5900435899266435,
)

LOG2_E = 1.4426950408889634
F32 = jnp.float32
BF16 = jnp.bfloat16
VMEM_LIMIT = 16 * 1024 * 1024
ROUTE_VMEM_LIMIT = 60 * 1024 * 1024
WIDE_VMEM_LIMIT = 52 * 1024 * 1024


def iota(shape, axis, dtype=jnp.int32):
    return lax.broadcasted_iota(dtype, shape, axis)


def spread(row, shape):
    return jnp.broadcast_to(row, shape)


def halves(values):
    high = values.astype(BF16)
    low = (values - high.astype(F32)).astype(BF16)
    return high, low


def dot(left, right):
    return jnp.dot(left, right, preferred_element_type=F32)


def dot_lanes(left, right):
    return lax.dot_general(left, right, (((1,), (1,)), ((), ())), preferred_element_type=F32)


GEO = 24


def write_geometry(height, camera_ref, geo_ref):
    row = iota((8, LANES), 0)
    block = jnp.zeros((8, LANES), F32)
    for index in range(6):
        block = jnp.where(row == index, camera_ref[0, index], block)
    cosines, sines = jnp.cos(block), jnp.sin(block)
    cx, cy, cz = (cosines[index : index + 1, :] for index in range(3))
    sx, sy, sz = (sines[index : index + 1, :] for index in range(3))
    inner = [
        [cy, sy * sx, sy * cx],
        [None, cx, -sx],
        [-sy, cy * sx, cy * cx],
    ]
    entries = [
        [cz * inner[0][0], cz * inner[0][1] - sz * inner[1][1], cz * inner[0][2] - sz * inner[1][2]],
        [sz * inner[0][0], sz * inner[0][1] + cz * inner[1][1], sz * inner[0][2] + cz * inner[1][2]],
        inner[2],
    ]
    for index, value in enumerate(entries[0] + entries[1] + entries[2]):
        geo_ref[index : index + 1, :] = value
    geo_ref[9:12, :] = block[3:6, :]
    for index in range(TILES_DEV):
        tile_id = lax.axis_index("img") * TILES_DEV + index
        tile_x = ((tile_id % TX * SIDE).astype(F32) + 0.5) * (2.0 / (TX * SIDE)) - 1.0
        tile_y = ((tile_id // TX * SIDE).astype(F32) + 0.5) * (2.0 / (height * SIDE)) - 1.0
        geo_ref[12 + index : 13 + index, :] = jnp.full((1, LANES), tile_x, F32)
        geo_ref[16 + index : 17 + index, :] = jnp.full((1, LANES), tile_y, F32)
    geo_ref[20:GEO, :] = jnp.zeros((GEO - 20, LANES), F32)


def camera_of(geo, rows=8):
    entries = [spread(geo[index : index + 1, :], (rows, LANES)) for index in range(12)]
    return [entries[0:3], entries[3:6], entries[6:9]], entries[9:12]


def camera_center(rotate, offset):
    return [
        -(rotate[0][col] * offset[0] + rotate[1][col] * offset[1] + rotate[2][col] * offset[2])
        for col in range(3)
    ]


def shape_matrix(log_scales, quaternion):
    scales = [jnp.exp(value) for value in log_scales]
    norm = lax.rsqrt(
        quaternion[0] * quaternion[0]
        + quaternion[1] * quaternion[1]
        + quaternion[2] * quaternion[2]
        + quaternion[3] * quaternion[3]
    )
    real, im_i, im_j, im_k = (part * norm for part in quaternion)
    local = [
        [1.0 - 2.0 * (im_j * im_j + im_k * im_k), 2.0 * (im_i * im_j - real * im_k), 2.0 * (im_i * im_k + real * im_j)],
        [2.0 * (im_i * im_j + real * im_k), 1.0 - 2.0 * (im_i * im_i + im_k * im_k), 2.0 * (im_j * im_k - real * im_i)],
        [2.0 * (im_i * im_k - real * im_j), 2.0 * (im_j * im_k + real * im_i), 1.0 - 2.0 * (im_i * im_i + im_j * im_j)],
    ]
    return [[local[row][col] * scales[col] for col in range(3)] for row in range(3)]


def harmonics(along_x, along_y, along_z):
    square_x, square_y, square_z = along_x * along_x, along_y * along_y, along_z * along_z
    return [
        jnp.full_like(along_x, SH_ZERO),
        -SH_ONE * along_y,
        SH_ONE * along_z,
        -SH_ONE * along_x,
        SH_TWO[0] * along_x * along_y,
        SH_TWO[1] * along_y * along_z,
        SH_TWO[2] * (2.0 * square_z - square_x - square_y),
        SH_TWO[3] * along_x * along_z,
        SH_TWO[4] * (square_x - square_y),
        SH_THREE[0] * along_y * (3.0 * square_x - square_y),
        SH_THREE[1] * along_x * along_y * along_z,
        SH_THREE[2] * along_y * (4.0 * square_z - square_x - square_y),
        SH_THREE[3] * along_z * (2.0 * square_z - 3.0 * square_x - 3.0 * square_y),
        SH_THREE[4] * along_x * (4.0 * square_z - square_x - square_y),
        SH_THREE[5] * along_z * (square_x - square_y),
        SH_THREE[6] * along_x * (square_x - 3.0 * square_y),
    ]


def screen_features(center, shape, rotate, offset):
    viewed = [
        rotate[row][0] * center[0] + rotate[row][1] * center[1] + rotate[row][2] * center[2] + offset[row]
        for row in range(3)
    ]
    depth_inv = 1.0 / viewed[2]
    near = FOCAL * depth_inv
    screen_x = viewed[0] * near
    screen_y = viewed[1] * near
    slope_x = -screen_x * depth_inv
    slope_y = -screen_y * depth_inv
    to_camera = [
        [near * rotate[0][col] + slope_x * rotate[2][col] for col in range(3)],
        [near * rotate[1][col] + slope_y * rotate[2][col] for col in range(3)],
    ]
    mapped = [
        [
            to_camera[row][0] * shape[0][col] + to_camera[row][1] * shape[1][col] + to_camera[row][2] * shape[2][col]
            for col in range(3)
        ]
        for row in range(2)
    ]
    first, second = mapped
    cov_a = first[0] * first[0] + first[1] * first[1] + first[2] * first[2] + DILATION
    cov_b = first[0] * second[0] + first[1] * second[1] + first[2] * second[2]
    cov_c = second[0] * second[0] + second[1] * second[1] + second[2] * second[2] + DILATION
    inverse = 1.0 / (cov_a * cov_c - cov_b * cov_b)
    return [screen_x, screen_y, cov_c * inverse, -cov_b * inverse, cov_a * inverse]


def direction_basis(center, eye):
    toward = [center[index] - eye[index] for index in range(3)]
    norm = lax.rsqrt(toward[0] * toward[0] + toward[1] * toward[1] + toward[2] * toward[2])
    return harmonics(toward[0] * norm, toward[1] * norm, toward[2] * norm)


def chunk_columns(chunk):
    return pl.ds(pl.multiple_of(chunk * CHUNK, CHUNK), CHUNK)


def spread_columns(params_ref, held_ref, chunk):
    for group in range(CHUNK // LANES):
        columns = pl.ds(pl.multiple_of(chunk * CHUNK + group * LANES, LANES), LANES)
        held_ref[chunk, group * PITCH : group * PITCH + PARAMS, :] = params_ref[:, columns]


def each_chunk(action):
    def body(chunk, carry):
        action(chunk)
        return carry

    lax.fori_loop(0, CHUNKS, body, 0)


def project_kernel(
    height, camera_hbm, params_ref, feats_ref, geo_ref, staged_ref, held_ref, camera_ref, semaphores, camera_semaphore
):
    def fetch(chunk):
        columns = chunk_columns(chunk)
        return pltpu.make_async_copy(params_ref.at[:, columns], staged_ref.at[:, columns], semaphores.at[chunk])

    camera_copy = pltpu.make_async_copy(camera_hbm, camera_ref, camera_semaphore)
    camera_copy.start()
    each_chunk(lambda chunk: fetch(chunk).start())
    camera_copy.wait()
    write_geometry(height, camera_ref, geo_ref)
    rotate, offset = camera_of(geo_ref[...])
    eye = camera_center(rotate, offset)

    def step(chunk, carry):
        fetch(chunk).wait()
        spread_columns(staged_ref, held_ref, chunk)

        def param(index):
            return held_ref[chunk, pl.ds(index, 8, stride=PITCH), :]

        center = [param(index) for index in range(3)]
        shape = shape_matrix([param(3 + index) for index in range(3)], [param(6 + index) for index in range(4)])
        screen = screen_features(center, shape, rotate, offset)
        basis = direction_basis(center, eye)
        opacity = 1.0 / (1.0 + jnp.exp(-param(10)))
        colors = []
        for channel in range(3):
            total = basis[0] * param(11 + channel)
            for term in range(1, 16):
                total = total + basis[term] * param(11 + 3 * term + channel)
            colors.append(total + 0.5)
        rows = pl.ds(pl.multiple_of(chunk * 8, 8), 8)
        for index, value in enumerate(screen + [opacity] + colors):
            feats_ref[index, rows, :] = value
        return carry

    lax.fori_loop(0, CHUNKS, step, 0)


def route_kernel(lists_hbm, request_ref, aux_ref, lists_ref, semaphore):
    lists_copy = pltpu.make_async_copy(lists_hbm, lists_ref, semaphore)
    lists_copy.start()
    owner_iota = iota((OWNERS, LANES), 0)
    before = (iota((LANES, 2 * LANES), 0) < iota((LANES, 2 * LANES), 1)).astype(F32)
    before = before.astype(BF16)
    rank_iota = iota((CAP, LANES), 0)
    lane = iota((1, LANES), 1)
    carried = jnp.zeros((OWNERS, LANES), F32)
    table = jnp.zeros((4 * CAP, OWNERS), F32)
    lists_copy.wait()
    for row in range(8):
        ids = lists_ref[0, row // 2 : row // 2 + 1, (row % 2) * LANES : (row % 2 + 1) * LANES]
        owner = ids // G_DEV
        column = ids % G_DEV
        hot = owner_iota == spread(owner, (OWNERS, LANES))
        hot_f32 = hot.astype(F32)
        hot_bf16 = hot_f32.astype(BF16)
        counts = dot(hot_bf16, before)
        rank = jnp.sum(jnp.where(hot, counts[:, :LANES] + carried, 0.0), axis=0, keepdims=True)
        carried = carried + counts[:, LANES:]
        rank = rank.astype(jnp.int32)
        at_rank = rank_iota == spread(rank, (CAP, LANES))
        pieces = [column // LANES, column % LANES, lane * 0 + row, lane + 1]
        stacked = jnp.concatenate(
            [jnp.where(at_rank, spread(piece.astype(F32), (CAP, LANES)), 0.0) for piece in pieces], axis=0
        )
        table = table + dot_lanes(stacked.astype(BF16), hot_bf16)
        aux_ref[row : row + 1, :] = owner
        aux_ref[8 + row : 9 + row, :] = rank
    high, low, slot_row, slot_lane = (table[CAP * part : CAP * (part + 1)] for part in range(4))
    used = slot_lane > 0.5
    slot = jnp.where(used, slot_row * LANES + slot_lane - 1.0, -1.0)
    wanted = jnp.where(used, high * LANES + low, -1.0)
    aux_ref[16 : 16 + CAP, :] = slot.astype(jnp.int32)
    aux_ref[16 + CAP : 16 + 2 * CAP, :] = wanted.astype(jnp.int32)
    padded = jnp.concatenate([wanted, jnp.zeros((LANES - CAP, OWNERS), F32)], axis=0)
    request_ref[...] = padded.T.astype(jnp.int32)


LANE_GATHER = lax.GatherDimensionNumbers(
    offset_dims=(),
    collapsed_slice_dims=(1,),
    start_index_map=(1,),
    operand_batching_dims=(0,),
    start_indices_batching_dims=(0,),
)


def pick(row, lanes_at):
    return lax.gather(
        spread(row, (8, LANES)),
        lanes_at[:, :, None],
        LANE_GATHER,
        slice_sizes=(1, 1),
        mode=lax.GatherScatterMode.PROMISE_IN_BOUNDS,
    )


def store_rows(out_ref, table):
    out_ref[pl.ds(0, LANES, stride=2), :] = table[:LANES].T
    out_ref[pl.ds(1, LANES, stride=2), :] = table[LANES:].T


WIDE = 256
TALL = G_DEV // WIDE
EXACT = 2


def split(values, parts):
    pieces = []
    for _ in range(parts):
        piece = values.astype(BF16)
        pieces.append(piece)
        values = values - piece.astype(F32)
    return pieces


def gather_kernel(request_ref, feats_ref, out_ref, table_ref):
    wanted = request_ref[...].astype(F32).T[:CAP].astype(jnp.int32)
    high, low = wanted >> 7, wanted & (LANES - 1)
    parts = [(high[:8], low[:8]), (high[8:], low[8:])]
    high_place, low_place = wanted >> 8, wanted & (WIDE - 1)
    tall_iota, wide_iota = iota((TALL, LANES), 0), iota((WIDE, LANES), 0)

    pieces, counts = [], []
    for index in range(EXACT, FEATS):
        wide = jnp.concatenate(
            [feats_ref[index, pl.ds(half, TALL, stride=2), :] for half in range(2)], axis=1
        )
        counts.append(3 if index < 5 else 2)
        pieces += split(wide, counts[-1])
    left = jnp.concatenate(pieces, axis=0)

    found = [jnp.zeros((8, LANES), F32) for _ in range(2 * EXACT)]
    for pair in range(CAP // 2):
        rights = []
        for rank in (2 * pair, 2 * pair + 1):
            at_low = wide_iota == spread(low_place[rank : rank + 1], (WIDE, LANES))
            rights.append(at_low.astype(F32).astype(BF16))
        product = dot(left, jnp.concatenate(rights, axis=1))
        for group in range(pair * (GROUPS // 8), (pair + 1) * (GROUPS // 8)):
            for index in range(EXACT):
                row = feats_ref[index, group : group + 1, :]
                for part, (at_group, at_lane) in enumerate(parts):
                    place = 2 * index + part
                    found[place] = jnp.where(at_group == group, pick(row, at_lane), found[place])
        for half, rank in enumerate((2 * pair, 2 * pair + 1)):
            at_high = tall_iota == spread(high_place[rank : rank + 1], (TALL, LANES))
            lanes = slice(half * LANES, (half + 1) * LANES)
            first = 0
            for index, count in enumerate(counts):
                total = product[first : first + TALL, lanes]
                for piece in range(1, count):
                    total = total + product[first + piece * TALL : first + (piece + 1) * TALL, lanes]
                first += count * TALL
                value = jnp.sum(jnp.where(at_high, total, 0.0), axis=0, keepdims=True)
                place = (EXACT + index) * CAP + rank
                table_ref[place : place + 1, :] = value
    table_ref[: EXACT * CAP, :] = jnp.concatenate(found, axis=0)
    table_ref[FEATS * CAP :, :] = jnp.zeros((PACK - FEATS * CAP, LANES), F32)
    store_rows(out_ref, table_ref[...])


PIX_CHUNK = 128


def render_kernel(
    height, lengths_ref, background_ref, geo_ref, arrived_ref, aux_ref, cotangent_ref, out_ref,
    slot_ref, table_ref, grad_ref, pixel_ref, weight_ref,
):
    table_ref[:LANES, :] = arrived_ref[pl.ds(0, LANES, stride=2), :].T
    table_ref[LANES:, :] = arrived_ref[pl.ds(1, LANES, stride=2), :].T
    owner = aux_ref[0:8, :]
    rank = aux_ref[8:16, :]
    at_rank = [rank == place for place in range(CAP)]
    for index in range(FEATS):
        value = jnp.zeros((8, LANES), F32)
        for place in range(CAP):
            row = table_ref[index * CAP + place : index * CAP + place + 1, :]
            value = jnp.where(at_rank[place], pick(row, owner), value)
        slot_ref[index * 8 : index * 8 + 8, :] = value

    within = iota((PIX, SLOTS), 0)
    pixel_ref[0] = (within % SIDE).astype(F32) * (2.0 / (TX * SIDE))
    pixel_ref[1] = (within // SIDE).astype(F32) * (2.0 / (height * SIDE))
    slot_row, slot_col = iota((SLOTS, SLOTS), 0), iota((SLOTS, SLOTS), 1)
    weight_ref[0] = (slot_row < slot_col).astype(F32).astype(BF16)
    weight_ref[1] = (slot_row > slot_col).astype(F32).astype(BF16)
    slot_place = iota((1, SLOTS), 1)
    def tile(index, carry):
        def slots(feature):
            return jnp.concatenate(
                [slot_ref[pl.ds(feature * 8 + 2 * index + half, 1), :] for half in range(2)], axis=1
            )

        tile_x, tile_y = geo_ref[pl.ds(12 + index, 1), :], geo_ref[pl.ds(16 + index, 1), :]
        at_x = slots(0) - jnp.concatenate([tile_x] * 2, axis=1)
        at_y = slots(1) - jnp.concatenate([tile_y] * 2, axis=1)
        conic_a, conic_b, conic_c = slots(2), slots(3), slots(4)
        opacity = slots(5)
        live_opacity = jnp.where(slot_place < lengths_ref[0, index], opacity, 0.0)
        colors = [slots(6 + channel) for channel in range(3)]
        scaled_a, scaled_b, scaled_c = (-0.5 * LOG2_E) * conic_a, -LOG2_E * conic_b, (-0.5 * LOG2_E) * conic_c
        shades = [cotangent_ref[0, channel, pl.ds(index, 1), :] for channel in range(3)]
        behind = (
            shades[0] * background_ref[0] + shades[1] * background_ref[1] + shades[2] * background_ref[2]
        )
        columns = jnp.concatenate(shades + [behind, jnp.zeros((4, PIX), F32)], axis=0).T

        def fold(values):
            return jnp.sum(values.reshape(PIX_CHUNK // 8, 8, SLOTS), axis=0)

        sums = [jnp.zeros((8, SLOTS), F32) for _ in range(9)]
        for chunk in range(PIX // PIX_CHUNK):
            rows = slice(chunk * PIX_CHUNK, (chunk + 1) * PIX_CHUNK)
            shape = (PIX_CHUNK, SLOTS)
            delta_x = pixel_ref[0, rows, :] - at_x
            delta_y = pixel_ref[1, rows, :] - at_y
            exponent = (scaled_a * delta_x + scaled_b * delta_y) * delta_x + scaled_c * delta_y * delta_y
            coverage = live_opacity * jnp.exp2(exponent)
            log_pass = jnp.log2(1.0 - coverage)
            high, low = halves(log_pass)
            prefix = dot(high, weight_ref[0]) + dot(low, weight_ref[0])
            weight = coverage * jnp.exp2(prefix)
            shade = [spread(columns[rows, channel : channel + 1], shape) for channel in range(3)]
            gain = shade[0] * colors[0] + shade[1] * colors[1] + shade[2] * colors[2]
            product = weight * gain
            high, low = halves(product)
            later = dot(high, weight_ref[1]) + dot(low, weight_ref[1])
            remain = jnp.exp2(prefix[:, SLOTS - 1 :] + log_pass[:, SLOTS - 1 :])
            later = later + spread(columns[rows, 3:4] * remain, shape)
            slope = product - coverage * jnp.exp2(-log_pass) * later
            slope_x = slope * delta_x
            slope_y = slope * delta_y
            parts = [slope, slope_x, slope_y, slope_x * delta_x, slope_x * delta_y, slope_y * delta_y]
            parts += [part * weight for part in shade]
            sums = [total + fold(part) for total, part in zip(sums, parts)]

        sums = [jnp.sum(part, axis=0, keepdims=True) for part in sums]
        total, sum_x, sum_y, sum_xx, sum_xy, sum_yy = (part * -0.5 for part in sums[:6])
        grads = [
            -2.0 * (conic_a * sum_x + conic_b * sum_y),
            -2.0 * (conic_b * sum_x + conic_c * sum_y),
            sum_xx,
            2.0 * sum_xy,
            sum_yy,
            -2.0 * total / opacity,
        ] + sums[6:]
        for feature, value in enumerate(grads):
            for half in range(2):
                grad_ref[pl.ds(feature * 8 + 2 * index + half, 1), :] = value[:, half * LANES : (half + 1) * LANES]
        return carry

    lax.fori_loop(0, TILES_DEV, tile, 0, unroll=TILES_DEV)

    slot = aux_ref[16 : 16 + CAP, :]
    wanted = aux_ref[16 + CAP : 16 + 2 * CAP, :].astype(F32)
    parts = [(slot[8 * part : 8 * part + 8] >> 7, slot[8 * part : 8 * part + 8] & (LANES - 1)) for part in range(2)]
    blocks = []
    for feature in range(FEATS):
        for at_row, at_lane in parts:
            value = jnp.zeros((8, LANES), F32)
            for row in range(8):
                grads = grad_ref[feature * 8 + row : feature * 8 + row + 1, :]
                value = jnp.where(at_row == row, pick(grads, at_lane), value)
            blocks.append(value)
    blocks += [wanted, geo_ref[0:16, :], jnp.zeros((PACK - FEATS * CAP - CAP - 16, LANES), F32)]
    store_rows(out_ref, jnp.concatenate(blocks, axis=0))


def duplicate_kernel(returned_ref, own_ref, copies_ref, semaphores):
    own_ref[:LANES, :] = returned_ref[pl.ds(0, LANES, stride=2), :].T
    own_ref[LANES:, :] = returned_ref[pl.ds(1, LANES, stride=2), :].T[: SENT - LANES]
    copies = [
        pltpu.make_async_copy(own_ref, copies_ref.at[view], semaphores.at[view])
        for view in range(copies_ref.shape[0])
    ]
    for copy in copies:
        copy.start()
    for copy in copies:
        copy.wait()


def scatter_view(view, arrived_ref, place, grads_ref, camera_ref):
    tall_iota = iota((TALL, LANES), 0)
    wide_iota = iota((WIDE, LANES), 0)
    values = arrived_ref[view, : FEATS * CAP, :]
    wanted = arrived_ref[view, FEATS * CAP : FEATS * CAP + CAP, :].astype(jnp.int32)
    camera_ref[place] = arrived_ref[view, FEATS * CAP + CAP : SENT, :]
    high_place, low_place = wanted >> 8, wanted & (WIDE - 1)
    high, low = halves(values)
    high, low = high.astype(F32), low.astype(F32)
    lefts, rights = [], []
    for rank in range(CAP):
        at_high = tall_iota == spread(high_place[rank : rank + 1], (TALL, LANES))
        at_low = wide_iota == spread(low_place[rank : rank + 1], (WIDE, LANES))
        at_low = at_low.astype(F32).astype(BF16)
        for source in (high, low):
            rows = [source[index * CAP + rank : index * CAP + rank + 1] for index in range(FEATS)]
            left = [jnp.where(at_high, spread(row, (TALL, LANES)), 0.0) for row in rows]
            lefts.append(jnp.concatenate(left, axis=0).astype(BF16))
            rights.append(at_low)
    total = dot_lanes(jnp.concatenate(lefts, axis=1), jnp.concatenate(rights, axis=1))
    for half in range(2):
        grads_ref[place, pl.ds(half, FEATS * TALL, stride=2), :] = total[:, half * LANES : (half + 1) * LANES]


SHAPE_ROWS = (3, 4, 5, 6, 7, 8, 9, 59, 60)


def read_chunks(ref, block, index):
    return jnp.concatenate(
        [ref[block * WIDTH + part, pl.ds(index, 8, stride=PITCH), :] for part in range(WIDTH)], axis=0
    )


def write_chunks(ref, block, index, value):
    for part in range(WIDTH):
        ref[block * WIDTH + part, pl.ds(index, 8, stride=PITCH), :] = value[8 * part : 8 * part + 8]


def pull_view(chunk, place, center, shape, param, grads_ref, camera_ref, kept, keep):
    def cotangent(feature):
        rows = 8 * WIDTH
        return grads_ref[place, pl.ds(pl.multiple_of(feature * GROUPS + chunk * rows, rows), rows), :]

    def add(index, value):
        before = kept(index)
        keep(index, value if before is None else before + value)

    rotate, offset = camera_of(camera_ref[place], 8 * WIDTH)
    eye = camera_center(rotate, offset)
    basis, basis_back = jax.vjp(lambda spot: direction_basis(spot, eye), center)
    colors = [cotangent(6 + channel) for channel in range(3)]
    basis_grad = []
    for term in range(16):
        total = None
        for channel in range(3):
            index = 11 + 3 * term + channel
            add(index, basis[term] * colors[channel])
            piece = param(index) * colors[channel]
            total = piece if total is None else total + piece
        basis_grad.append(total)
    (along,) = basis_back(basis_grad)
    unused, screen_back = jax.vjp(
        lambda spot, matrix: screen_features(spot, matrix, rotate, offset), center, shape
    )
    moved, bent = screen_back([cotangent(index) for index in range(5)])
    for axis in range(3):
        add(axis, along[axis] + moved[axis])
    for row in range(3):
        for col in range(3):
            add(SHAPE_ROWS[3 * row + col], bent[row][col])
    add(10, cotangent(5))


def own_pullback_kernel(
    returned_ref, params_ref, out_ref, held_hbm,
    staged_ref, held_ref, grads_ref, camera_ref, partial_ref, fetch_sems, held_sems, semaphores,
):
    def fetch(chunk):
        columns = chunk_columns(chunk)
        return pltpu.make_async_copy(params_ref.at[:, columns], staged_ref.at[:, columns], fetch_sems.at[chunk])

    def hold(chunk):
        return pltpu.make_async_copy(held_ref.at[chunk], held_hbm.at[chunk], held_sems.at[chunk])

    def send(chunk):
        return pltpu.make_async_copy(partial_ref.at[chunk], out_ref.at[chunk], semaphores.at[chunk])

    each_chunk(lambda chunk: fetch(chunk).start())
    scatter_view(0, returned_ref, 0, grads_ref, camera_ref)

    def step(block, carry):
        for part in range(WIDTH):
            chunk = block * WIDTH + part
            fetch(chunk).wait()
            spread_columns(staged_ref, held_ref, chunk)
            hold(chunk).start()

        def param(index):
            return read_chunks(held_ref, block, index)

        def keep(index, value):
            write_chunks(partial_ref, block, index, value)

        center = [param(index) for index in range(3)]
        shape = shape_matrix([param(3 + index) for index in range(3)], [param(6 + index) for index in range(4)])
        pull_view(block, 0, center, shape, param, grads_ref, camera_ref, lambda index: None, keep)
        for part in range(WIDTH):
            send(block * WIDTH + part).start()
        return carry

    lax.fori_loop(0, CHUNKS // WIDTH, step, 0)
    each_chunk(lambda chunk: send(chunk).wait())
    each_chunk(lambda chunk: hold(chunk).wait())


def pullback_kernel(
    arrived_ref, held_hbm, partial_hbm, out_ref,
    held_ref, partial_ref, grads_ref, camera_ref, staged_ref, held_sems, partial_sems, semaphores,
):
    views = arrived_ref.shape[0]

    def fetch_held(chunk):
        return pltpu.make_async_copy(held_hbm.at[chunk], held_ref.at[chunk], held_sems.at[chunk])

    def fetch_partial(chunk):
        return pltpu.make_async_copy(partial_hbm.at[chunk], partial_ref.at[chunk], partial_sems.at[chunk])

    def start(chunk):
        fetch_held(chunk).start()
        fetch_partial(chunk).start()

    each_chunk(start)

    def one_view(place, carry):
        view = lax.rem(lax.axis_index("view") + 1 + place, views)
        scatter_view(view, arrived_ref, place, grads_ref, camera_ref)
        return carry

    lax.fori_loop(0, views - 1, one_view, 0, unroll=True)

    def send(chunk):
        columns = chunk_columns(chunk)
        return pltpu.make_async_copy(staged_ref.at[:, columns], out_ref.at[:, columns], semaphores.at[chunk])

    def step(block, carry):
        for part in range(WIDTH):
            fetch_held(block * WIDTH + part).wait()
            fetch_partial(block * WIDTH + part).wait()

        def param(index):
            return read_chunks(held_ref, block, index)

        def keep(index, value):
            write_chunks(partial_ref, block, index, value)

        def kept(index):
            return read_chunks(partial_ref, block, index)

        center = [param(index) for index in range(3)]
        shape, shape_back = jax.vjp(
            shape_matrix, [param(3 + index) for index in range(3)], [param(6 + index) for index in range(4)]
        )
        for place in range(views - 1):
            pull_view(block, place, center, shape, param, grads_ref, camera_ref, kept, keep)
        scale_grad, quaternion_grad = shape_back(
            [[kept(SHAPE_ROWS[3 * row + col]) for col in range(3)] for row in range(3)]
        )
        opacity = 1.0 / (1.0 + jnp.exp(-param(10)))
        finals = list(scale_grad) + list(quaternion_grad) + [opacity * (1.0 - opacity) * kept(10)]
        for index, value in enumerate(finals):
            keep(3 + index, value)
        for part in range(WIDTH):
            chunk = block * WIDTH + part
            for group in range(CHUNK // LANES):
                columns = pl.ds(pl.multiple_of(chunk * CHUNK + group * LANES, LANES), LANES)
                staged_ref[:, columns] = partial_ref[chunk, group * PITCH : group * PITCH + PARAMS, :]
            send(chunk).start()
        return carry

    lax.fori_loop(0, CHUNKS // WIDTH, step, 0)
    each_chunk(lambda chunk: send(chunk).wait())


def call(kernel, out_shape, operands, smalls=(), scratch=(), **kwargs):
    spaces = [pltpu.SMEM if index < smalls else pltpu.VMEM for index in range(len(operands))]
    single = not isinstance(out_shape, (list, tuple))
    outs = pl.BlockSpec(memory_space=pltpu.VMEM)
    return pl.pallas_call(
        kernel,
        out_shape=out_shape,
        in_specs=[pl.BlockSpec(memory_space=space) for space in spaces],
        out_specs=outs if single else [outs] * len(out_shape),
        scratch_shapes=list(scratch),
        compiler_params=pltpu.CompilerParams(vmem_limit_bytes=VMEM_LIMIT),
        **kwargs,
    )(*operands)


WIDTH = 2
HELD = jax.ShapeDtypeStruct((CHUNKS, 8 * PITCH, LANES), F32)


def route(tile_lists):
    return pl.pallas_call(
        route_kernel,
        out_shape=[
            jax.ShapeDtypeStruct((OWNERS, LANES), jnp.int32),
            jax.ShapeDtypeStruct((16 + 2 * CAP, LANES), jnp.int32),
        ],
        in_specs=[pl.BlockSpec(memory_space=pl.ANY)],
        out_specs=[pl.BlockSpec(memory_space=pltpu.VMEM)] * 2,
        scratch_shapes=[
            pltpu.VMEM(tile_lists.shape, jnp.int32),
            pltpu.SemaphoreType.DMA,
        ],
        compiler_params=pltpu.CompilerParams(vmem_limit_bytes=ROUTE_VMEM_LIMIT),
    )(tile_lists)


def project(height, camera, gauss_params):
    return pl.pallas_call(
        functools.partial(project_kernel, height),
        out_shape=[
            jax.ShapeDtypeStruct((FEATS, GROUPS, LANES), F32),
            jax.ShapeDtypeStruct((GEO, LANES), F32),
        ],
        in_specs=[pl.BlockSpec(memory_space=pl.ANY)] * 2,
        out_specs=[pl.BlockSpec(memory_space=pltpu.VMEM)] * 2,
        scratch_shapes=[
            pltpu.VMEM((PARAMS, G_DEV), F32),
            pltpu.VMEM(HELD.shape, F32),
            pltpu.SMEM(camera.shape, F32),
            pltpu.SemaphoreType.DMA((CHUNKS,)),
            pltpu.SemaphoreType.DMA,
        ],
        compiler_params=pltpu.CompilerParams(vmem_limit_bytes=WIDE_VMEM_LIMIT),
    )(camera, gauss_params)


def gather(requested, features):
    return call(
        gather_kernel,
        jax.ShapeDtypeStruct((2 * OWNERS, LANES), F32),
        [requested, features],
        smalls=0,
        scratch=[pltpu.VMEM((PACK, LANES), F32)],
    )


def render(height, tile_lengths, background, geometry, arrived, aux, cotangent):
    return call(
        functools.partial(render_kernel, height),
        jax.ShapeDtypeStruct((2 * OWNERS, LANES), F32),
        [tile_lengths, background, geometry, arrived, aux, cotangent],
        smalls=2,
        scratch=[
            pltpu.VMEM((FEATS * 8, LANES), F32),
            pltpu.VMEM((2 * OWNERS, LANES), F32),
            pltpu.VMEM((FEATS * 8, LANES), F32),
            pltpu.VMEM((2, PIX, SLOTS), F32),
            pltpu.VMEM((2, SLOTS, SLOTS), BF16),
        ],
    )


def duplicate(returned, views):
    return pl.pallas_call(
        duplicate_kernel,
        out_shape=[
            jax.ShapeDtypeStruct((SENT, LANES), F32),
            jax.ShapeDtypeStruct((views, SENT, LANES), F32),
        ],
        in_specs=[pl.BlockSpec(memory_space=pltpu.VMEM)],
        out_specs=[pl.BlockSpec(memory_space=pltpu.VMEM), pl.BlockSpec(memory_space=pl.ANY)],
        scratch_shapes=[pltpu.SemaphoreType.DMA((views,))],
        compiler_params=pltpu.CompilerParams(vmem_limit_bytes=VMEM_LIMIT),
    )(returned)


def own_pullback(own, gauss_params):
    return pl.pallas_call(
        own_pullback_kernel,
        out_shape=[HELD, HELD],
        in_specs=[pl.BlockSpec(memory_space=pltpu.VMEM), pl.BlockSpec(memory_space=pl.ANY)],
        out_specs=[pl.BlockSpec(memory_space=pl.ANY)] * 2,
        scratch_shapes=[
            pltpu.VMEM((PARAMS, G_DEV), F32),
            pltpu.VMEM(HELD.shape, F32),
            pltpu.VMEM((1, FEATS * GROUPS, LANES), F32),
            pltpu.VMEM((1, 16, LANES), F32),
            pltpu.VMEM(HELD.shape, F32),
            pltpu.SemaphoreType.DMA((CHUNKS,)),
            pltpu.SemaphoreType.DMA((CHUNKS,)),
            pltpu.SemaphoreType.DMA((CHUNKS,)),
        ],
        compiler_params=pltpu.CompilerParams(vmem_limit_bytes=WIDE_VMEM_LIMIT),
        cost_estimate=pl.CostEstimate(flops=20_000_000, bytes_accessed=4_000_000, transcendentals=0),
    )(own.reshape((1,) + own.shape), gauss_params)


def pullback(arrived, held, partial):
    others = arrived.shape[0] - 1
    return pl.pallas_call(
        pullback_kernel,
        out_shape=jax.ShapeDtypeStruct((PARAMS, G_DEV), F32),
        in_specs=[
            pl.BlockSpec(memory_space=space) for space in (pltpu.VMEM, pl.ANY, pl.ANY)
        ],
        out_specs=pl.BlockSpec(memory_space=pl.ANY),
        scratch_shapes=[
            pltpu.VMEM(HELD.shape, F32),
            pltpu.VMEM(HELD.shape, F32),
            pltpu.VMEM((others, FEATS * GROUPS, LANES), F32),
            pltpu.VMEM((others, 16, LANES), F32),
            pltpu.VMEM((PARAMS, G_DEV), F32),
            pltpu.SemaphoreType.DMA((CHUNKS,)),
            pltpu.SemaphoreType.DMA((CHUNKS,)),
            pltpu.SemaphoreType.DMA((CHUNKS,)),
        ],
        compiler_params=pltpu.CompilerParams(vmem_limit_bytes=WIDE_VMEM_LIMIT),
    )(arrived, held, partial)


def per_device(gauss_params, camera, background, tile_lists, tile_lengths, pixel_cotangent):
    owners_total = lax.axis_size("img")
    views = lax.axis_size("view")
    tiles_here = tile_lists.shape[1]
    height = tiles_here * owners_total // TX
    requests, aux = route(tile_lists)
    features, geometry = project(height, camera, gauss_params)
    requested = lax.all_to_all(requests, "img", split_axis=0, concat_axis=0, tiled=True)
    outgoing = gather(requested, features)
    arrived = lax.all_to_all(outgoing, "img", split_axis=0, concat_axis=0, tiled=True)
    slot_grads = render(height, tile_lengths, background, geometry, arrived, aux, pixel_cotangent)
    returned = lax.all_to_all(slot_grads, "img", split_axis=0, concat_axis=0, tiled=True)
    own, copies = duplicate(returned, views)
    everyone = lax.all_to_all(copies, "view", split_axis=0, concat_axis=0, tiled=True)
    partial, held = own_pullback(own, gauss_params)
    return pullback(everyone, held, partial)


def solution(mesh):
    placed = (
        P(None, "img"),
        P("view", None),
        P(),
        P("view", "img", None),
        P("view", "img"),
        P("view", None, "img", None),
    )
    return jax.shard_map(
        per_device, mesh=mesh, in_specs=placed, out_specs=P(None, "img"), check_vma=False
    )
```

```python
import functools

import jax
import jax.numpy as jnp
from jax import lax
from jax.experimental import pallas as pl
from jax.experimental.pallas import tpu as pltpu
from jax.sharding import PartitionSpec as P

SIDE = 16
TX = 16
PIX = 256
SLOTS = 256
TILES_DEV = 4
OWNERS = 128
CAP = 16
LANES = 128
G_DEV = 8192
GROUPS = G_DEV // LANES
PARAMS = 59
PITCH = 65
CHUNKS = 8
CHUNK = G_DEV // CHUNKS
FEATS = 9
PACK = 256
SENT = FEATS * CAP + CAP + 16

FOCAL = 2.0
DILATION = 0.0001
SH_ZERO = 0.28209479177387814
SH_ONE = 0.4886025119029199
SH_TWO = (
    1.0925484305920792,
    -1.0925484305920792,
    0.31539156525252005,
    -1.0925484305920792,
    0.5462742152960396,
)
SH_THREE = (
    -0.5900435899266435,
    2.890611442640554,
    -0.4570457994644658,
    0.3731763325901154,
    -0.4570457994644658,
    1.445305721320277,
    -0.5900435899266435,
)

LOG2_E = 1.4426950408889634
F32 = jnp.float32
BF16 = jnp.bfloat16
VMEM_LIMIT = 16 * 1024 * 1024
ROUTE_VMEM_LIMIT = 60 * 1024 * 1024
WIDE_VMEM_LIMIT = 52 * 1024 * 1024


def iota(shape, axis, dtype=jnp.int32):
    return lax.broadcasted_iota(dtype, shape, axis)


def spread(row, shape):
    return jnp.broadcast_to(row, shape)


def halves(values):
    high = values.astype(BF16)
    low = (values - high.astype(F32)).astype(BF16)
    return high, low


def dot(left, right):
    return jnp.dot(left, right, preferred_element_type=F32)


def dot_lanes(left, right):
    return lax.dot_general(left, right, (((1,), (1,)), ((), ())), preferred_element_type=F32)


GEO = 24


def write_geometry(height, camera_ref, geo_ref):
    row = iota((8, LANES), 0)
    block = jnp.zeros((8, LANES), F32)
    for index in range(6):
        block = jnp.where(row == index, camera_ref[0, index], block)
    cosines, sines = jnp.cos(block), jnp.sin(block)
    cx, cy, cz = (cosines[index : index + 1, :] for index in range(3))
    sx, sy, sz = (sines[index : index + 1, :] for index in range(3))
    inner = [
        [cy, sy * sx, sy * cx],
        [None, cx, -sx],
        [-sy, cy * sx, cy * cx],
    ]
    entries = [
        [cz * inner[0][0], cz * inner[0][1] - sz * inner[1][1], cz * inner[0][2] - sz * inner[1][2]],
        [sz * inner[0][0], sz * inner[0][1] + cz * inner[1][1], sz * inner[0][2] + cz * inner[1][2]],
        inner[2],
    ]
    for index, value in enumerate(entries[0] + entries[1] + entries[2]):
        geo_ref[index : index + 1, :] = value
    geo_ref[9:12, :] = block[3:6, :]
    for index in range(TILES_DEV):
        tile_id = lax.axis_index("img") * TILES_DEV + index
        tile_x = ((tile_id % TX * SIDE).astype(F32) + 0.5) * (2.0 / (TX * SIDE)) - 1.0
        tile_y = ((tile_id // TX * SIDE).astype(F32) + 0.5) * (2.0 / (height * SIDE)) - 1.0
        geo_ref[12 + index : 13 + index, :] = jnp.full((1, LANES), tile_x, F32)
        geo_ref[16 + index : 17 + index, :] = jnp.full((1, LANES), tile_y, F32)
    geo_ref[20:GEO, :] = jnp.zeros((GEO - 20, LANES), F32)


def camera_of(geo, rows=8):
    entries = [spread(geo[index : index + 1, :], (rows, LANES)) for index in range(12)]
    return [entries[0:3], entries[3:6], entries[6:9]], entries[9:12]


def camera_center(rotate, offset):
    return [
        -(rotate[0][col] * offset[0] + rotate[1][col] * offset[1] + rotate[2][col] * offset[2])
        for col in range(3)
    ]


def shape_matrix(log_scales, quaternion):
    scales = [jnp.exp(value) for value in log_scales]
    norm = lax.rsqrt(
        quaternion[0] * quaternion[0]
        + quaternion[1] * quaternion[1]
        + quaternion[2] * quaternion[2]
        + quaternion[3] * quaternion[3]
    )
    real, im_i, im_j, im_k = (part * norm for part in quaternion)
    local = [
        [1.0 - 2.0 * (im_j * im_j + im_k * im_k), 2.0 * (im_i * im_j - real * im_k), 2.0 * (im_i * im_k + real * im_j)],
        [2.0 * (im_i * im_j + real * im_k), 1.0 - 2.0 * (im_i * im_i + im_k * im_k), 2.0 * (im_j * im_k - real * im_i)],
        [2.0 * (im_i * im_k - real * im_j), 2.0 * (im_j * im_k + real * im_i), 1.0 - 2.0 * (im_i * im_i + im_j * im_j)],
    ]
    return [[local[row][col] * scales[col] for col in range(3)] for row in range(3)]


def harmonics(along_x, along_y, along_z):
    square_x, square_y, square_z = along_x * along_x, along_y * along_y, along_z * along_z
    return [
        jnp.full_like(along_x, SH_ZERO),
        -SH_ONE * along_y,
        SH_ONE * along_z,
        -SH_ONE * along_x,
        SH_TWO[0] * along_x * along_y,
        SH_TWO[1] * along_y * along_z,
        SH_TWO[2] * (2.0 * square_z - square_x - square_y),
        SH_TWO[3] * along_x * along_z,
        SH_TWO[4] * (square_x - square_y),
        SH_THREE[0] * along_y * (3.0 * square_x - square_y),
        SH_THREE[1] * along_x * along_y * along_z,
        SH_THREE[2] * along_y * (4.0 * square_z - square_x - square_y),
        SH_THREE[3] * along_z * (2.0 * square_z - 3.0 * square_x - 3.0 * square_y),
        SH_THREE[4] * along_x * (4.0 * square_z - square_x - square_y),
        SH_THREE[5] * along_z * (square_x - square_y),
        SH_THREE[6] * along_x * (square_x - 3.0 * square_y),
    ]


def screen_features(center, shape, rotate, offset):
    viewed = [
        rotate[row][0] * center[0] + rotate[row][1] * center[1] + rotate[row][2] * center[2] + offset[row]
        for row in range(3)
    ]
    depth_inv = 1.0 / viewed[2]
    near = FOCAL * depth_inv
    screen_x = viewed[0] * near
    screen_y = viewed[1] * near
    slope_x = -screen_x * depth_inv
    slope_y = -screen_y * depth_inv
    to_camera = [
        [near * rotate[0][col] + slope_x * rotate[2][col] for col in range(3)],
        [near * rotate[1][col] + slope_y * rotate[2][col] for col in range(3)],
    ]
    mapped = [
        [
            to_camera[row][0] * shape[0][col] + to_camera[row][1] * shape[1][col] + to_camera[row][2] * shape[2][col]
            for col in range(3)
        ]
        for row in range(2)
    ]
    first, second = mapped
    cov_a = first[0] * first[0] + first[1] * first[1] + first[2] * first[2] + DILATION
    cov_b = first[0] * second[0] + first[1] * second[1] + first[2] * second[2]
    cov_c = second[0] * second[0] + second[1] * second[1] + second[2] * second[2] + DILATION
    inverse = 1.0 / (cov_a * cov_c - cov_b * cov_b)
    return [screen_x, screen_y, cov_c * inverse, -cov_b * inverse, cov_a * inverse]


def direction_basis(center, eye):
    toward = [center[index] - eye[index] for index in range(3)]
    norm = lax.rsqrt(toward[0] * toward[0] + toward[1] * toward[1] + toward[2] * toward[2])
    return harmonics(toward[0] * norm, toward[1] * norm, toward[2] * norm)


def chunk_columns(chunk):
    return pl.ds(pl.multiple_of(chunk * CHUNK, CHUNK), CHUNK)


def spread_columns(params_ref, held_ref, chunk):
    for group in range(CHUNK // LANES):
        columns = pl.ds(pl.multiple_of(chunk * CHUNK + group * LANES, LANES), LANES)
        held_ref[chunk, group * PITCH : group * PITCH + PARAMS, :] = params_ref[:, columns]


def each_chunk(action):
    def body(chunk, carry):
        action(chunk)
        return carry

    lax.fori_loop(0, CHUNKS, body, 0)


def project_kernel(
    height, camera_hbm, params_ref, feats_ref, geo_ref, staged_ref, held_ref, camera_ref, semaphores, camera_semaphore
):
    def fetch(chunk):
        columns = chunk_columns(chunk)
        return pltpu.make_async_copy(params_ref.at[:, columns], staged_ref.at[:, columns], semaphores.at[chunk])

    camera_copy = pltpu.make_async_copy(camera_hbm, camera_ref, camera_semaphore)
    camera_copy.start()
    each_chunk(lambda chunk: fetch(chunk).start())
    camera_copy.wait()
    write_geometry(height, camera_ref, geo_ref)
    rotate, offset = camera_of(geo_ref[...])
    eye = camera_center(rotate, offset)

    def step(chunk, carry):
        fetch(chunk).wait()
        spread_columns(staged_ref, held_ref, chunk)

        def param(index):
            return held_ref[chunk, pl.ds(index, 8, stride=PITCH), :]

        center = [param(index) for index in range(3)]
        shape = shape_matrix([param(3 + index) for index in range(3)], [param(6 + index) for index in range(4)])
        screen = screen_features(center, shape, rotate, offset)
        basis = direction_basis(center, eye)
        opacity = 1.0 / (1.0 + jnp.exp(-param(10)))
        colors = []
        for channel in range(3):
            total = basis[0] * param(11 + channel)
            for term in range(1, 16):
                total = total + basis[term] * param(11 + 3 * term + channel)
            colors.append(total + 0.5)
        rows = pl.ds(pl.multiple_of(chunk * 8, 8), 8)
        for index, value in enumerate(screen + [opacity] + colors):
            feats_ref[index, rows, :] = value
        return carry

    lax.fori_loop(0, CHUNKS, step, 0)


def route_kernel(lists_hbm, request_ref, aux_ref, lists_ref, semaphore):
    lists_copy = pltpu.make_async_copy(lists_hbm, lists_ref, semaphore)
    lists_copy.start()
    owner_iota = iota((OWNERS, LANES), 0)
    before = (iota((LANES, 2 * LANES), 0) < iota((LANES, 2 * LANES), 1)).astype(F32)
    before = before.astype(BF16)
    rank_iota = iota((CAP, LANES), 0)
    lane = iota((1, LANES), 1)
    carried = jnp.zeros((OWNERS, LANES), F32)
    table = jnp.zeros((4 * CAP, OWNERS), F32)
    lists_copy.wait()
    for row in range(8):
        ids = lists_ref[0, row // 2 : row // 2 + 1, (row % 2) * LANES : (row % 2 + 1) * LANES]
        owner = ids // G_DEV
        column = ids % G_DEV
        hot = owner_iota == spread(owner, (OWNERS, LANES))
        hot_f32 = hot.astype(F32)
        hot_bf16 = hot_f32.astype(BF16)
        counts = dot(hot_bf16, before)
        rank = jnp.sum(jnp.where(hot, counts[:, :LANES] + carried, 0.0), axis=0, keepdims=True)
        carried = carried + counts[:, LANES:]
        rank = rank.astype(jnp.int32)
        at_rank = rank_iota == spread(rank, (CAP, LANES))
        pieces = [column // LANES, column % LANES, lane * 0 + row, lane + 1]
        stacked = jnp.concatenate(
            [jnp.where(at_rank, spread(piece.astype(F32), (CAP, LANES)), 0.0) for piece in pieces], axis=0
        )
        table = table + dot_lanes(stacked.astype(BF16), hot_bf16)
        aux_ref[row : row + 1, :] = owner
        aux_ref[8 + row : 9 + row, :] = rank
    high, low, slot_row, slot_lane = (table[CAP * part : CAP * (part + 1)] for part in range(4))
    used = slot_lane > 0.5
    slot = jnp.where(used, slot_row * LANES + slot_lane - 1.0, -1.0)
    wanted = jnp.where(used, high * LANES + low, -1.0)
    aux_ref[16 : 16 + CAP, :] = slot.astype(jnp.int32)
    aux_ref[16 + CAP : 16 + 2 * CAP, :] = wanted.astype(jnp.int32)
    padded = jnp.concatenate([wanted, jnp.zeros((LANES - CAP, OWNERS), F32)], axis=0)
    request_ref[...] = padded.T.astype(jnp.int32)


LANE_GATHER = lax.GatherDimensionNumbers(
    offset_dims=(),
    collapsed_slice_dims=(1,),
    start_index_map=(1,),
    operand_batching_dims=(0,),
    start_indices_batching_dims=(0,),
)


def pick(row, lanes_at):
    return lax.gather(
        spread(row, (8, LANES)),
        lanes_at[:, :, None],
        LANE_GATHER,
        slice_sizes=(1, 1),
        mode=lax.GatherScatterMode.PROMISE_IN_BOUNDS,
    )


def store_rows(out_ref, table):
    out_ref[pl.ds(0, LANES, stride=2), :] = table[:LANES].T
    out_ref[pl.ds(1, LANES, stride=2), :] = table[LANES:].T


WIDE = 256
TALL = G_DEV // WIDE
EXACT = 2


def split(values, parts):
    pieces = []
    for _ in range(parts):
        piece = values.astype(BF16)
        pieces.append(piece)
        values = values - piece.astype(F32)
    return pieces


def gather_kernel(request_ref, feats_ref, out_ref, table_ref):
    wanted = request_ref[...].astype(F32).T[:CAP].astype(jnp.int32)
    high, low = wanted >> 7, wanted & (LANES - 1)
    parts = [(high[:8], low[:8]), (high[8:], low[8:])]
    high_place, low_place = wanted >> 8, wanted & (WIDE - 1)
    tall_iota, wide_iota = iota((TALL, LANES), 0), iota((WIDE, LANES), 0)

    pieces, counts = [], []
    for index in range(EXACT, FEATS):
        wide = jnp.concatenate(
            [feats_ref[index, pl.ds(half, TALL, stride=2), :] for half in range(2)], axis=1
        )
        counts.append(3 if index < 5 else 2)
        pieces += split(wide, counts[-1])
    left = jnp.concatenate(pieces, axis=0)

    found = [jnp.zeros((8, LANES), F32) for _ in range(2 * EXACT)]
    for pair in range(CAP // 2):
        rights = []
        for rank in (2 * pair, 2 * pair + 1):
            at_low = wide_iota == spread(low_place[rank : rank + 1], (WIDE, LANES))
            rights.append(at_low.astype(F32).astype(BF16))
        product = dot(left, jnp.concatenate(rights, axis=1))
        for group in range(pair * (GROUPS // 8), (pair + 1) * (GROUPS // 8)):
            for index in range(EXACT):
                row = feats_ref[index, group : group + 1, :]
                for part, (at_group, at_lane) in enumerate(parts):
                    place = 2 * index + part
                    found[place] = jnp.where(at_group == group, pick(row, at_lane), found[place])
        for half, rank in enumerate((2 * pair, 2 * pair + 1)):
            at_high = tall_iota == spread(high_place[rank : rank + 1], (TALL, LANES))
            lanes = slice(half * LANES, (half + 1) * LANES)
            first = 0
            for index, count in enumerate(counts):
                total = product[first : first + TALL, lanes]
                for piece in range(1, count):
                    total = total + product[first + piece * TALL : first + (piece + 1) * TALL, lanes]
                first += count * TALL
                value = jnp.sum(jnp.where(at_high, total, 0.0), axis=0, keepdims=True)
                place = (EXACT + index) * CAP + rank
                table_ref[place : place + 1, :] = value
    table_ref[: EXACT * CAP, :] = jnp.concatenate(found, axis=0)
    table_ref[FEATS * CAP :, :] = jnp.zeros((PACK - FEATS * CAP, LANES), F32)
    store_rows(out_ref, table_ref[...])


PIX_CHUNK = 256


def render_kernel(
    height, lengths_ref, background_ref, geo_ref, arrived_ref, aux_ref, cotangent_ref, out_ref,
    slot_ref, table_ref, grad_ref, rows_ref, weight_ref,
):
    table_ref[:LANES, :] = arrived_ref[pl.ds(0, LANES, stride=2), :].T
    table_ref[LANES:, :] = arrived_ref[pl.ds(1, LANES, stride=2), :].T
    owner = aux_ref[0:8, :]
    rank = aux_ref[8:16, :]
    at_rank = [rank == place for place in range(CAP)]
    for index in range(FEATS):
        value = jnp.zeros((8, LANES), F32)
        for place in range(CAP):
            row = table_ref[index * CAP + place : index * CAP + place + 1, :]
            value = jnp.where(at_rank[place], pick(row, owner), value)
        slot_ref[index * 8 : index * 8 + 8, :] = value

    along = iota((SIDE, SLOTS), 0).astype(F32)
    slot_row, slot_col = iota((SLOTS, SLOTS), 0), iota((SLOTS, SLOTS), 1)
    weight_ref[0] = (slot_row < slot_col).astype(F32).astype(BF16)
    weight_ref[1] = (slot_row > slot_col).astype(F32).astype(BF16)
    slot_place = iota((1, SLOTS), 1)
    def tile(index, carry):
        def slots(feature):
            return jnp.concatenate(
                [slot_ref[pl.ds(feature * 8 + 2 * index + half, 1), :] for half in range(2)], axis=1
            )

        tile_x, tile_y = geo_ref[pl.ds(12 + index, 1), :], geo_ref[pl.ds(16 + index, 1), :]
        at_x = slots(0) - jnp.concatenate([tile_x] * 2, axis=1)
        at_y = slots(1) - jnp.concatenate([tile_y] * 2, axis=1)
        conic_a, conic_b, conic_c = slots(2), slots(3), slots(4)
        opacity = slots(5)
        live_opacity = jnp.where(slot_place < lengths_ref[0, index], opacity, 0.0)
        colors = [slots(6 + channel) for channel in range(3)]
        scaled_a, scaled_b, scaled_c = (-0.5 * LOG2_E) * conic_a, -LOG2_E * conic_b, (-0.5 * LOG2_E) * conic_c
        shades = [cotangent_ref[0, channel, pl.ds(index, 1), :] for channel in range(3)]
        behind = (
            shades[0] * background_ref[0] + shades[1] * background_ref[1] + shades[2] * background_ref[2]
        )
        columns = jnp.concatenate(shades + [behind, jnp.zeros((4, PIX), F32)], axis=0).T

        shade_high, shade_low = (part.astype(F32) for part in halves(jnp.concatenate(shades, axis=0)))
        color_high, color_low = (part.astype(F32) for part in halves(jnp.concatenate(colors, axis=0)))
        filler = jnp.zeros((7, PIX), F32)
        gains = lax.dot_general(
            jnp.concatenate([shade_high, shade_high, shade_low, filler], axis=0).astype(BF16),
            jnp.concatenate([color_high, color_low, color_high, filler], axis=0).astype(BF16),
            (((0,), (0,)), ((), ())),
            preferred_element_type=F32,
        )
        delta_x = along * (2.0 / (TX * SIDE)) - at_x
        slope_a = scaled_a * delta_x
        delta_y = along * (2.0 / (height * SIDE)) - at_y
        rows_ref[index, 0] = delta_y
        rows_ref[index, 1] = scaled_b * delta_y
        rows_ref[index, 2] = scaled_c * delta_y * delta_y

        def fold(values):
            return jnp.sum(values.reshape(PIX_CHUNK // 8, 8, SLOTS), axis=0)

        sums = [jnp.zeros((8, SLOTS), F32) for _ in range(9)]
        for chunk in range(PIX // PIX_CHUNK):
            rows = slice(chunk * PIX_CHUNK, (chunk + 1) * PIX_CHUNK)
            shape = (PIX_CHUNK, SLOTS)
            lines = range(chunk * PIX_CHUNK // SIDE, (chunk + 1) * PIX_CHUNK // SIDE)
            exponent = jnp.concatenate(
                [
                    (slope_a + rows_ref[index, 1, line : line + 1, :]) * delta_x
                    + rows_ref[index, 2, line : line + 1, :]
                    for line in lines
                ],
                axis=0,
            )
            coverage = live_opacity * jnp.exp2(exponent)
            log_pass = jnp.log2(1.0 - coverage)
            high, low = halves(log_pass)
            prefix = dot(high, weight_ref[0]) + dot(low, weight_ref[0])
            weight = coverage * jnp.exp2(prefix)
            shade = [spread(columns[rows, channel : channel + 1], shape) for channel in range(3)]
            product = weight * gains[rows]
            high, low = halves(product)
            later = dot(high, weight_ref[1]) + dot(low, weight_ref[1])
            remain = jnp.exp2(prefix[:, SLOTS - 1 :] + log_pass[:, SLOTS - 1 :])
            later = later + spread(columns[rows, 3:4] * remain, shape)
            slope = product - coverage * jnp.exp2(-log_pass) * later
            total, sum_x, sum_y, sum_xx, sum_xy, sum_yy = sums[:6]
            for place, line in enumerate(lines):
                down = rows_ref[index, 0, line : line + 1, :]
                part = slope[place * SIDE : (place + 1) * SIDE]
                part_x = part * delta_x
                part_xx = part_x * delta_x
                part, part_x, part_xx = (value[:8] + value[8:] for value in (part, part_x, part_xx))
                part_y = part * down
                total, sum_x, sum_xx = total + part, sum_x + part_x, sum_xx + part_xx
                sum_y, sum_yy, sum_xy = sum_y + part_y, sum_yy + part_y * down, sum_xy + part_x * down
            sums = [total, sum_x, sum_y, sum_xx, sum_xy, sum_yy] + [
                past + fold(value * weight) for past, value in zip(sums[6:], shade)
            ]

        sums = [jnp.sum(part, axis=0, keepdims=True) for part in sums]
        total, sum_x, sum_y, sum_xx, sum_xy, sum_yy = (part * -0.5 for part in sums[:6])
        grads = [
            -2.0 * (conic_a * sum_x + conic_b * sum_y),
            -2.0 * (conic_b * sum_x + conic_c * sum_y),
            sum_xx,
            2.0 * sum_xy,
            sum_yy,
            -2.0 * total / opacity,
        ] + sums[6:]
        for feature, value in enumerate(grads):
            for half in range(2):
                grad_ref[pl.ds(feature * 8 + 2 * index + half, 1), :] = value[:, half * LANES : (half + 1) * LANES]
        return carry

    lax.fori_loop(0, TILES_DEV, tile, 0, unroll=TILES_DEV)

    slot = aux_ref[16 : 16 + CAP, :]
    wanted = aux_ref[16 + CAP : 16 + 2 * CAP, :].astype(F32)
    parts = [(slot[8 * part : 8 * part + 8] >> 7, slot[8 * part : 8 * part + 8] & (LANES - 1)) for part in range(2)]
    blocks = []
    for feature in range(FEATS):
        for at_row, at_lane in parts:
            value = jnp.zeros((8, LANES), F32)
            for row in range(8):
                grads = grad_ref[feature * 8 + row : feature * 8 + row + 1, :]
                value = jnp.where(at_row == row, pick(grads, at_lane), value)
            blocks.append(value)
    blocks += [wanted, geo_ref[0:16, :], jnp.zeros((PACK - FEATS * CAP - CAP - 16, LANES), F32)]
    store_rows(out_ref, jnp.concatenate(blocks, axis=0))


def duplicate_kernel(returned_ref, own_ref, copies_ref, semaphores):
    own_ref[:LANES, :] = returned_ref[pl.ds(0, LANES, stride=2), :].T
    own_ref[LANES:, :] = returned_ref[pl.ds(1, LANES, stride=2), :].T[: SENT - LANES]
    copies = [
        pltpu.make_async_copy(own_ref, copies_ref.at[view], semaphores.at[view])
        for view in range(copies_ref.shape[0])
    ]
    for copy in copies:
        copy.start()
    for copy in copies:
        copy.wait()


def scatter_view(view, arrived_ref, place, grads_ref, camera_ref):
    tall_iota = iota((TALL, LANES), 0)
    wide_iota = iota((WIDE, LANES), 0)
    values = arrived_ref[view, : FEATS * CAP, :]
    wanted = arrived_ref[view, FEATS * CAP : FEATS * CAP + CAP, :].astype(jnp.int32)
    camera_ref[place] = arrived_ref[view, FEATS * CAP + CAP : SENT, :]
    high_place, low_place = wanted >> 8, wanted & (WIDE - 1)
    high, low = halves(values)
    high, low = high.astype(F32), low.astype(F32)
    lefts, rights = [], []
    for rank in range(CAP):
        at_high = tall_iota == spread(high_place[rank : rank + 1], (TALL, LANES))
        at_low = wide_iota == spread(low_place[rank : rank + 1], (WIDE, LANES))
        at_low = at_low.astype(F32).astype(BF16)
        for source in (high, low):
            rows = [source[index * CAP + rank : index * CAP + rank + 1] for index in range(FEATS)]
            left = [jnp.where(at_high, spread(row, (TALL, LANES)), 0.0) for row in rows]
            lefts.append(jnp.concatenate(left, axis=0).astype(BF16))
            rights.append(at_low)
    total = dot_lanes(jnp.concatenate(lefts, axis=1), jnp.concatenate(rights, axis=1))
    for half in range(2):
        grads_ref[place, pl.ds(half, FEATS * TALL, stride=2), :] = total[:, half * LANES : (half + 1) * LANES]


SHAPE_ROWS = (3, 4, 5, 6, 7, 8, 9, 59, 60)


def read_chunks(ref, block, index):
    return jnp.concatenate(
        [ref[block * WIDTH + part, pl.ds(index, 8, stride=PITCH), :] for part in range(WIDTH)], axis=0
    )


def write_chunks(ref, block, index, value):
    for part in range(WIDTH):
        ref[block * WIDTH + part, pl.ds(index, 8, stride=PITCH), :] = value[8 * part : 8 * part + 8]


def pull_view(chunk, place, center, shape, param, grads_ref, camera_ref, kept, keep):
    def cotangent(feature):
        rows = 8 * WIDTH
        return grads_ref[place, pl.ds(pl.multiple_of(feature * GROUPS + chunk * rows, rows), rows), :]

    def add(index, value):
        before = kept(index)
        keep(index, value if before is None else before + value)

    rotate, offset = camera_of(camera_ref[place], 8 * WIDTH)
    eye = camera_center(rotate, offset)
    basis, basis_back = jax.vjp(lambda spot: direction_basis(spot, eye), center)
    colors = [cotangent(6 + channel) for channel in range(3)]
    basis_grad = []
    for term in range(16):
        total = None
        for channel in range(3):
            index = 11 + 3 * term + channel
            add(index, basis[term] * colors[channel])
            piece = param(index) * colors[channel]
            total = piece if total is None else total + piece
        basis_grad.append(total)
    (along,) = basis_back(basis_grad)
    unused, screen_back = jax.vjp(
        lambda spot, matrix: screen_features(spot, matrix, rotate, offset), center, shape
    )
    moved, bent = screen_back([cotangent(index) for index in range(5)])
    for axis in range(3):
        add(axis, along[axis] + moved[axis])
    for row in range(3):
        for col in range(3):
            add(SHAPE_ROWS[3 * row + col], bent[row][col])
    add(10, cotangent(5))


def own_pullback_kernel(
    returned_ref, params_ref, out_ref, held_hbm,
    staged_ref, held_ref, grads_ref, camera_ref, partial_ref, fetch_sems, held_sems, semaphores,
):
    def fetch(chunk):
        columns = chunk_columns(chunk)
        return pltpu.make_async_copy(params_ref.at[:, columns], staged_ref.at[:, columns], fetch_sems.at[chunk])

    def hold(chunk):
        return pltpu.make_async_copy(held_ref.at[chunk], held_hbm.at[chunk], held_sems.at[chunk])

    def send(chunk):
        return pltpu.make_async_copy(partial_ref.at[chunk], out_ref.at[chunk], semaphores.at[chunk])

    each_chunk(lambda chunk: fetch(chunk).start())
    scatter_view(0, returned_ref, 0, grads_ref, camera_ref)

    def step(block, carry):
        for part in range(WIDTH):
            chunk = block * WIDTH + part
            fetch(chunk).wait()
            spread_columns(staged_ref, held_ref, chunk)
            hold(chunk).start()

        def param(index):
            return read_chunks(held_ref, block, index)

        def keep(index, value):
            write_chunks(partial_ref, block, index, value)

        center = [param(index) for index in range(3)]
        shape = shape_matrix([param(3 + index) for index in range(3)], [param(6 + index) for index in range(4)])
        pull_view(block, 0, center, shape, param, grads_ref, camera_ref, lambda index: None, keep)
        for part in range(WIDTH):
            send(block * WIDTH + part).start()
        return carry

    lax.fori_loop(0, CHUNKS // WIDTH, step, 0)
    each_chunk(lambda chunk: send(chunk).wait())
    each_chunk(lambda chunk: hold(chunk).wait())


def pullback_kernel(
    arrived_ref, held_hbm, partial_hbm, out_ref,
    held_ref, partial_ref, grads_ref, camera_ref, staged_ref, held_sems, partial_sems, semaphores,
):
    views = arrived_ref.shape[0]

    def fetch_held(chunk):
        return pltpu.make_async_copy(held_hbm.at[chunk], held_ref.at[chunk], held_sems.at[chunk])

    def fetch_partial(chunk):
        return pltpu.make_async_copy(partial_hbm.at[chunk], partial_ref.at[chunk], partial_sems.at[chunk])

    def start(chunk):
        fetch_held(chunk).start()
        fetch_partial(chunk).start()

    each_chunk(start)

    def one_view(place, carry):
        view = lax.rem(lax.axis_index("view") + 1 + place, views)
        scatter_view(view, arrived_ref, place, grads_ref, camera_ref)
        return carry

    lax.fori_loop(0, views - 1, one_view, 0, unroll=True)

    def send(chunk):
        columns = chunk_columns(chunk)
        return pltpu.make_async_copy(staged_ref.at[:, columns], out_ref.at[:, columns], semaphores.at[chunk])

    def step(block, carry):
        for part in range(WIDTH):
            fetch_held(block * WIDTH + part).wait()
            fetch_partial(block * WIDTH + part).wait()

        def param(index):
            return read_chunks(held_ref, block, index)

        def keep(index, value):
            write_chunks(partial_ref, block, index, value)

        def kept(index):
            return read_chunks(partial_ref, block, index)

        center = [param(index) for index in range(3)]
        shape, shape_back = jax.vjp(
            shape_matrix, [param(3 + index) for index in range(3)], [param(6 + index) for index in range(4)]
        )
        for place in range(views - 1):
            pull_view(block, place, center, shape, param, grads_ref, camera_ref, kept, keep)
        scale_grad, quaternion_grad = shape_back(
            [[kept(SHAPE_ROWS[3 * row + col]) for col in range(3)] for row in range(3)]
        )
        opacity = 1.0 / (1.0 + jnp.exp(-param(10)))
        finals = list(scale_grad) + list(quaternion_grad) + [opacity * (1.0 - opacity) * kept(10)]
        for index, value in enumerate(finals):
            keep(3 + index, value)
        for part in range(WIDTH):
            chunk = block * WIDTH + part
            for group in range(CHUNK // LANES):
                columns = pl.ds(pl.multiple_of(chunk * CHUNK + group * LANES, LANES), LANES)
                staged_ref[:, columns] = partial_ref[chunk, group * PITCH : group * PITCH + PARAMS, :]
            send(chunk).start()
        return carry

    lax.fori_loop(0, CHUNKS // WIDTH, step, 0)
    each_chunk(lambda chunk: send(chunk).wait())


def call(kernel, out_shape, operands, smalls=(), scratch=(), **kwargs):
    spaces = [pltpu.SMEM if index < smalls else pltpu.VMEM for index in range(len(operands))]
    single = not isinstance(out_shape, (list, tuple))
    outs = pl.BlockSpec(memory_space=pltpu.VMEM)
    return pl.pallas_call(
        kernel,
        out_shape=out_shape,
        in_specs=[pl.BlockSpec(memory_space=space) for space in spaces],
        out_specs=outs if single else [outs] * len(out_shape),
        scratch_shapes=list(scratch),
        compiler_params=pltpu.CompilerParams(vmem_limit_bytes=VMEM_LIMIT),
        **kwargs,
    )(*operands)


WIDTH = 2
HELD = jax.ShapeDtypeStruct((CHUNKS, 8 * PITCH, LANES), F32)


def route(tile_lists):
    return pl.pallas_call(
        route_kernel,
        out_shape=[
            jax.ShapeDtypeStruct((OWNERS, LANES), jnp.int32),
            jax.ShapeDtypeStruct((16 + 2 * CAP, LANES), jnp.int32),
        ],
        in_specs=[pl.BlockSpec(memory_space=pl.ANY)],
        out_specs=[pl.BlockSpec(memory_space=pltpu.VMEM)] * 2,
        scratch_shapes=[
            pltpu.VMEM(tile_lists.shape, jnp.int32),
            pltpu.SemaphoreType.DMA,
        ],
        compiler_params=pltpu.CompilerParams(vmem_limit_bytes=ROUTE_VMEM_LIMIT),
    )(tile_lists)


def project(height, camera, gauss_params):
    return pl.pallas_call(
        functools.partial(project_kernel, height),
        out_shape=[
            jax.ShapeDtypeStruct((FEATS, GROUPS, LANES), F32),
            jax.ShapeDtypeStruct((GEO, LANES), F32),
        ],
        in_specs=[pl.BlockSpec(memory_space=pl.ANY)] * 2,
        out_specs=[pl.BlockSpec(memory_space=pltpu.VMEM)] * 2,
        scratch_shapes=[
            pltpu.VMEM((PARAMS, G_DEV), F32),
            pltpu.VMEM(HELD.shape, F32),
            pltpu.SMEM(camera.shape, F32),
            pltpu.SemaphoreType.DMA((CHUNKS,)),
            pltpu.SemaphoreType.DMA,
        ],
        compiler_params=pltpu.CompilerParams(vmem_limit_bytes=WIDE_VMEM_LIMIT),
    )(camera, gauss_params)


def gather(requested, features):
    return call(
        gather_kernel,
        jax.ShapeDtypeStruct((2 * OWNERS, LANES), F32),
        [requested, features],
        smalls=0,
        scratch=[pltpu.VMEM((PACK, LANES), F32)],
    )


def render(height, tile_lengths, background, geometry, arrived, aux, cotangent):
    return call(
        functools.partial(render_kernel, height),
        jax.ShapeDtypeStruct((2 * OWNERS, LANES), F32),
        [tile_lengths, background, geometry, arrived, aux, cotangent],
        smalls=2,
        scratch=[
            pltpu.VMEM((FEATS * 8, LANES), F32),
            pltpu.VMEM((2 * OWNERS, LANES), F32),
            pltpu.VMEM((FEATS * 8, LANES), F32),
            pltpu.VMEM((TILES_DEV, 3, SIDE, SLOTS), F32),
            pltpu.VMEM((2, SLOTS, SLOTS), BF16),
        ],
    )


def duplicate(returned, views):
    return pl.pallas_call(
        duplicate_kernel,
        out_shape=[
            jax.ShapeDtypeStruct((SENT, LANES), F32),
            jax.ShapeDtypeStruct((views, SENT, LANES), F32),
        ],
        in_specs=[pl.BlockSpec(memory_space=pltpu.VMEM)],
        out_specs=[pl.BlockSpec(memory_space=pltpu.VMEM), pl.BlockSpec(memory_space=pl.ANY)],
        scratch_shapes=[pltpu.SemaphoreType.DMA((views,))],
        compiler_params=pltpu.CompilerParams(vmem_limit_bytes=VMEM_LIMIT),
    )(returned)


def own_pullback(own, gauss_params):
    return pl.pallas_call(
        own_pullback_kernel,
        out_shape=[HELD, HELD],
        in_specs=[pl.BlockSpec(memory_space=pltpu.VMEM), pl.BlockSpec(memory_space=pl.ANY)],
        out_specs=[pl.BlockSpec(memory_space=pl.ANY)] * 2,
        scratch_shapes=[
            pltpu.VMEM((PARAMS, G_DEV), F32),
            pltpu.VMEM(HELD.shape, F32),
            pltpu.VMEM((1, FEATS * GROUPS, LANES), F32),
            pltpu.VMEM((1, 16, LANES), F32),
            pltpu.VMEM(HELD.shape, F32),
            pltpu.SemaphoreType.DMA((CHUNKS,)),
            pltpu.SemaphoreType.DMA((CHUNKS,)),
            pltpu.SemaphoreType.DMA((CHUNKS,)),
        ],
        compiler_params=pltpu.CompilerParams(vmem_limit_bytes=WIDE_VMEM_LIMIT),
        cost_estimate=pl.CostEstimate(flops=20_000_000, bytes_accessed=4_000_000, transcendentals=0),
    )(own.reshape((1,) + own.shape), gauss_params)


def pullback(arrived, held, partial):
    others = arrived.shape[0] - 1
    return pl.pallas_call(
        pullback_kernel,
        out_shape=jax.ShapeDtypeStruct((PARAMS, G_DEV), F32),
        in_specs=[
            pl.BlockSpec(memory_space=space) for space in (pltpu.VMEM, pl.ANY, pl.ANY)
        ],
        out_specs=pl.BlockSpec(memory_space=pl.ANY),
        scratch_shapes=[
            pltpu.VMEM(HELD.shape, F32),
            pltpu.VMEM(HELD.shape, F32),
            pltpu.VMEM((others, FEATS * GROUPS, LANES), F32),
            pltpu.VMEM((others, 16, LANES), F32),
            pltpu.VMEM((PARAMS, G_DEV), F32),
            pltpu.SemaphoreType.DMA((CHUNKS,)),
            pltpu.SemaphoreType.DMA((CHUNKS,)),
            pltpu.SemaphoreType.DMA((CHUNKS,)),
        ],
        compiler_params=pltpu.CompilerParams(vmem_limit_bytes=WIDE_VMEM_LIMIT),
    )(arrived, held, partial)


def per_device(gauss_params, camera, background, tile_lists, tile_lengths, pixel_cotangent):
    owners_total = lax.axis_size("img")
    views = lax.axis_size("view")
    tiles_here = tile_lists.shape[1]
    height = tiles_here * owners_total // TX
    requests, aux = route(tile_lists)
    features, geometry = project(height, camera, gauss_params)
    requested = lax.all_to_all(requests, "img", split_axis=0, concat_axis=0, tiled=True)
    outgoing = gather(requested, features)
    arrived = lax.all_to_all(outgoing, "img", split_axis=0, concat_axis=0, tiled=True)
    slot_grads = render(height, tile_lengths, background, geometry, arrived, aux, pixel_cotangent)
    returned = lax.all_to_all(slot_grads, "img", split_axis=0, concat_axis=0, tiled=True)
    own, copies = duplicate(returned, views)
    everyone = lax.all_to_all(copies, "view", split_axis=0, concat_axis=0, tiled=True)
    partial, held = own_pullback(own, gauss_params)
    return pullback(everyone, held, partial)


def solution(mesh):
    placed = (
        P(None, "img"),
        P("view", None),
        P(),
        P("view", "img", None),
        P("view", "img"),
        P("view", None, "img", None),
    )
    return jax.shard_map(
        per_device, mesh=mesh, in_specs=placed, out_specs=P(None, "img"), check_vma=False
    )
```

```python
import functools

import jax
import jax.numpy as jnp
from jax import lax
from jax.experimental import pallas as pl
from jax.experimental.pallas import tpu as pltpu
from jax.sharding import PartitionSpec as P

SIDE = 16
TX = 16
PIX = 256
SLOTS = 256
TILES_DEV = 4
OWNERS = 128
CAP = 16
LANES = 128
G_DEV = 8192
GROUPS = G_DEV // LANES
PARAMS = 59
PITCH = 65
CHUNKS = 8
CHUNK = G_DEV // CHUNKS
FEATS = 9
PACK = 256
SENT = FEATS * CAP + CAP + 16

FOCAL = 2.0
DILATION = 0.0001
SH_ZERO = 0.28209479177387814
SH_ONE = 0.4886025119029199
SH_TWO = (
    1.0925484305920792,
    -1.0925484305920792,
    0.31539156525252005,
    -1.0925484305920792,
    0.5462742152960396,
)
SH_THREE = (
    -0.5900435899266435,
    2.890611442640554,
    -0.4570457994644658,
    0.3731763325901154,
    -0.4570457994644658,
    1.445305721320277,
    -0.5900435899266435,
)

LOG2_E = 1.4426950408889634
F32 = jnp.float32
BF16 = jnp.bfloat16
VMEM_LIMIT = 16 * 1024 * 1024
ROUTE_VMEM_LIMIT = 60 * 1024 * 1024
WIDE_VMEM_LIMIT = 52 * 1024 * 1024


def iota(shape, axis, dtype=jnp.int32):
    return lax.broadcasted_iota(dtype, shape, axis)


def spread(row, shape):
    return jnp.broadcast_to(row, shape)


def halves(values):
    high = values.astype(BF16)
    low = (values - high.astype(F32)).astype(BF16)
    return high, low


def dot(left, right):
    return jnp.dot(left, right, preferred_element_type=F32)


def dot_lanes(left, right):
    return lax.dot_general(left, right, (((1,), (1,)), ((), ())), preferred_element_type=F32)


GEO = 24


def write_geometry(height, camera_ref, geo_ref):
    row = iota((8, LANES), 0)
    block = jnp.zeros((8, LANES), F32)
    for index in range(6):
        block = jnp.where(row == index, camera_ref[0, index], block)
    cosines, sines = jnp.cos(block), jnp.sin(block)
    cx, cy, cz = (cosines[index : index + 1, :] for index in range(3))
    sx, sy, sz = (sines[index : index + 1, :] for index in range(3))
    inner = [
        [cy, sy * sx, sy * cx],
        [None, cx, -sx],
        [-sy, cy * sx, cy * cx],
    ]
    entries = [
        [cz * inner[0][0], cz * inner[0][1] - sz * inner[1][1], cz * inner[0][2] - sz * inner[1][2]],
        [sz * inner[0][0], sz * inner[0][1] + cz * inner[1][1], sz * inner[0][2] + cz * inner[1][2]],
        inner[2],
    ]
    for index, value in enumerate(entries[0] + entries[1] + entries[2]):
        geo_ref[index : index + 1, :] = value
    geo_ref[9:12, :] = block[3:6, :]
    for index in range(TILES_DEV):
        tile_id = lax.axis_index("img") * TILES_DEV + index
        tile_x = ((tile_id % TX * SIDE).astype(F32) + 0.5) * (2.0 / (TX * SIDE)) - 1.0
        tile_y = ((tile_id // TX * SIDE).astype(F32) + 0.5) * (2.0 / (height * SIDE)) - 1.0
        geo_ref[12 + index : 13 + index, :] = jnp.full((1, LANES), tile_x, F32)
        geo_ref[16 + index : 17 + index, :] = jnp.full((1, LANES), tile_y, F32)
    geo_ref[20:GEO, :] = jnp.zeros((GEO - 20, LANES), F32)


def camera_of(geo, rows=8):
    entries = [spread(geo[index : index + 1, :], (rows, LANES)) for index in range(12)]
    return [entries[0:3], entries[3:6], entries[6:9]], entries[9:12]


def camera_center(rotate, offset):
    return [
        -(rotate[0][col] * offset[0] + rotate[1][col] * offset[1] + rotate[2][col] * offset[2])
        for col in range(3)
    ]


def shape_matrix(log_scales, quaternion):
    scales = [jnp.exp(value) for value in log_scales]
    norm = lax.rsqrt(
        quaternion[0] * quaternion[0]
        + quaternion[1] * quaternion[1]
        + quaternion[2] * quaternion[2]
        + quaternion[3] * quaternion[3]
    )
    real, im_i, im_j, im_k = (part * norm for part in quaternion)
    local = [
        [1.0 - 2.0 * (im_j * im_j + im_k * im_k), 2.0 * (im_i * im_j - real * im_k), 2.0 * (im_i * im_k + real * im_j)],
        [2.0 * (im_i * im_j + real * im_k), 1.0 - 2.0 * (im_i * im_i + im_k * im_k), 2.0 * (im_j * im_k - real * im_i)],
        [2.0 * (im_i * im_k - real * im_j), 2.0 * (im_j * im_k + real * im_i), 1.0 - 2.0 * (im_i * im_i + im_j * im_j)],
    ]
    return [[local[row][col] * scales[col] for col in range(3)] for row in range(3)]


def harmonics(along_x, along_y, along_z):
    square_x, square_y, square_z = along_x * along_x, along_y * along_y, along_z * along_z
    return [
        jnp.full_like(along_x, SH_ZERO),
        -SH_ONE * along_y,
        SH_ONE * along_z,
        -SH_ONE * along_x,
        SH_TWO[0] * along_x * along_y,
        SH_TWO[1] * along_y * along_z,
        SH_TWO[2] * (2.0 * square_z - square_x - square_y),
        SH_TWO[3] * along_x * along_z,
        SH_TWO[4] * (square_x - square_y),
        SH_THREE[0] * along_y * (3.0 * square_x - square_y),
        SH_THREE[1] * along_x * along_y * along_z,
        SH_THREE[2] * along_y * (4.0 * square_z - square_x - square_y),
        SH_THREE[3] * along_z * (2.0 * square_z - 3.0 * square_x - 3.0 * square_y),
        SH_THREE[4] * along_x * (4.0 * square_z - square_x - square_y),
        SH_THREE[5] * along_z * (square_x - square_y),
        SH_THREE[6] * along_x * (square_x - 3.0 * square_y),
    ]


def screen_features(center, shape, rotate, offset):
    viewed = [
        rotate[row][0] * center[0] + rotate[row][1] * center[1] + rotate[row][2] * center[2] + offset[row]
        for row in range(3)
    ]
    depth_inv = 1.0 / viewed[2]
    near = FOCAL * depth_inv
    screen_x = viewed[0] * near
    screen_y = viewed[1] * near
    slope_x = -screen_x * depth_inv
    slope_y = -screen_y * depth_inv
    to_camera = [
        [near * rotate[0][col] + slope_x * rotate[2][col] for col in range(3)],
        [near * rotate[1][col] + slope_y * rotate[2][col] for col in range(3)],
    ]
    mapped = [
        [
            to_camera[row][0] * shape[0][col] + to_camera[row][1] * shape[1][col] + to_camera[row][2] * shape[2][col]
            for col in range(3)
        ]
        for row in range(2)
    ]
    first, second = mapped
    cov_a = first[0] * first[0] + first[1] * first[1] + first[2] * first[2] + DILATION
    cov_b = first[0] * second[0] + first[1] * second[1] + first[2] * second[2]
    cov_c = second[0] * second[0] + second[1] * second[1] + second[2] * second[2] + DILATION
    inverse = 1.0 / (cov_a * cov_c - cov_b * cov_b)
    return [screen_x, screen_y, cov_c * inverse, -cov_b * inverse, cov_a * inverse]


def direction_basis(center, eye):
    toward = [center[index] - eye[index] for index in range(3)]
    norm = lax.rsqrt(toward[0] * toward[0] + toward[1] * toward[1] + toward[2] * toward[2])
    return harmonics(toward[0] * norm, toward[1] * norm, toward[2] * norm)


def chunk_columns(chunk):
    return pl.ds(pl.multiple_of(chunk * CHUNK, CHUNK), CHUNK)


def spread_columns(params_ref, held_ref, chunk):
    for group in range(CHUNK // LANES):
        columns = pl.ds(pl.multiple_of(chunk * CHUNK + group * LANES, LANES), LANES)
        held_ref[chunk, group * PITCH : group * PITCH + PARAMS, :] = params_ref[:, columns]


def each_chunk(action):
    def body(chunk, carry):
        action(chunk)
        return carry

    lax.fori_loop(0, CHUNKS, body, 0)


def project_kernel(
    height, camera_hbm, params_ref, feats_ref, geo_ref, staged_ref, held_ref, camera_ref, semaphores, camera_semaphore
):
    def fetch(chunk):
        columns = chunk_columns(chunk)
        return pltpu.make_async_copy(params_ref.at[:, columns], staged_ref.at[:, columns], semaphores.at[chunk])

    camera_copy = pltpu.make_async_copy(camera_hbm, camera_ref, camera_semaphore)
    camera_copy.start()
    each_chunk(lambda chunk: fetch(chunk).start())
    camera_copy.wait()
    write_geometry(height, camera_ref, geo_ref)
    rotate, offset = camera_of(geo_ref[...])
    eye = camera_center(rotate, offset)

    def step(chunk, carry):
        fetch(chunk).wait()
        spread_columns(staged_ref, held_ref, chunk)

        def param(index):
            return held_ref[chunk, pl.ds(index, 8, stride=PITCH), :]

        center = [param(index) for index in range(3)]
        shape = shape_matrix([param(3 + index) for index in range(3)], [param(6 + index) for index in range(4)])
        screen = screen_features(center, shape, rotate, offset)
        basis = direction_basis(center, eye)
        opacity = 1.0 / (1.0 + jnp.exp(-param(10)))
        colors = []
        for channel in range(3):
            total = basis[0] * param(11 + channel)
            for term in range(1, 16):
                total = total + basis[term] * param(11 + 3 * term + channel)
            colors.append(total + 0.5)
        rows = pl.ds(pl.multiple_of(chunk * 8, 8), 8)
        for index, value in enumerate(screen + [opacity] + colors):
            feats_ref[index, rows, :] = value
        return carry

    lax.fori_loop(0, CHUNKS, step, 0)


def route_kernel(lists_hbm, request_ref, aux_ref, lists_ref, semaphore):
    lists_copy = pltpu.make_async_copy(lists_hbm, lists_ref, semaphore)
    lists_copy.start()
    owner_iota = iota((OWNERS, LANES), 0)
    before = (iota((LANES, 2 * LANES), 0) < iota((LANES, 2 * LANES), 1)).astype(F32)
    before = before.astype(BF16)
    rank_iota = iota((CAP, LANES), 0)
    lane = iota((1, LANES), 1)
    carried = jnp.zeros((OWNERS, LANES), F32)
    table = jnp.zeros((4 * CAP, OWNERS), F32)
    lists_copy.wait()
    for row in range(8):
        ids = lists_ref[0, row // 2 : row // 2 + 1, (row % 2) * LANES : (row % 2 + 1) * LANES]
        owner = ids // G_DEV
        column = ids % G_DEV
        hot = owner_iota == spread(owner, (OWNERS, LANES))
        hot_f32 = hot.astype(F32)
        hot_bf16 = hot_f32.astype(BF16)
        counts = dot(hot_bf16, before)
        rank = jnp.sum(jnp.where(hot, counts[:, :LANES] + carried, 0.0), axis=0, keepdims=True)
        carried = carried + counts[:, LANES:]
        rank = rank.astype(jnp.int32)
        at_rank = rank_iota == spread(rank, (CAP, LANES))
        pieces = [column // LANES, column % LANES, lane * 0 + row, lane + 1]
        stacked = jnp.concatenate(
            [jnp.where(at_rank, spread(piece.astype(F32), (CAP, LANES)), 0.0) for piece in pieces], axis=0
        )
        table = table + dot_lanes(stacked.astype(BF16), hot_bf16)
        aux_ref[row : row + 1, :] = owner
        aux_ref[8 + row : 9 + row, :] = rank
    high, low, slot_row, slot_lane = (table[CAP * part : CAP * (part + 1)] for part in range(4))
    used = slot_lane > 0.5
    slot = jnp.where(used, slot_row * LANES + slot_lane - 1.0, -1.0)
    wanted = jnp.where(used, high * LANES + low, -1.0)
    aux_ref[16 : 16 + CAP, :] = slot.astype(jnp.int32)
    aux_ref[16 + CAP : 16 + 2 * CAP, :] = wanted.astype(jnp.int32)
    padded = jnp.concatenate([wanted, jnp.zeros((LANES - CAP, OWNERS), F32)], axis=0)
    request_ref[...] = padded.T.astype(jnp.int32)


LANE_GATHER = lax.GatherDimensionNumbers(
    offset_dims=(),
    collapsed_slice_dims=(1,),
    start_index_map=(1,),
    operand_batching_dims=(0,),
    start_indices_batching_dims=(0,),
)


def pick(row, lanes_at):
    return lax.gather(
        spread(row, (8, LANES)),
        lanes_at[:, :, None],
        LANE_GATHER,
        slice_sizes=(1, 1),
        mode=lax.GatherScatterMode.PROMISE_IN_BOUNDS,
    )


def store_rows(out_ref, table):
    out_ref[pl.ds(0, LANES, stride=2), :] = table[:LANES].T
    out_ref[pl.ds(1, LANES, stride=2), :] = table[LANES:].T


WIDE = 256
TALL = G_DEV // WIDE
EXACT = 2


def split(values, parts):
    pieces = []
    for _ in range(parts):
        piece = values.astype(BF16)
        pieces.append(piece)
        values = values - piece.astype(F32)
    return pieces


def gather_kernel(request_ref, feats_ref, out_ref, table_ref):
    wanted = request_ref[...].astype(F32).T[:CAP].astype(jnp.int32)
    high, low = wanted >> 7, wanted & (LANES - 1)
    parts = [(high[:8], low[:8]), (high[8:], low[8:])]
    high_place, low_place = wanted >> 8, wanted & (WIDE - 1)
    tall_iota, wide_iota = iota((TALL, LANES), 0), iota((WIDE, LANES), 0)

    pieces, counts = [], []
    for index in range(EXACT, FEATS):
        wide = jnp.concatenate(
            [feats_ref[index, pl.ds(half, TALL, stride=2), :] for half in range(2)], axis=1
        )
        counts.append(3 if index < 5 else 2)
        pieces += split(wide, counts[-1])
    left = jnp.concatenate(pieces, axis=0)

    found = [jnp.zeros((8, LANES), F32) for _ in range(2 * EXACT)]
    for pair in range(CAP // 2):
        rights = []
        for rank in (2 * pair, 2 * pair + 1):
            at_low = wide_iota == spread(low_place[rank : rank + 1], (WIDE, LANES))
            rights.append(at_low.astype(F32).astype(BF16))
        product = dot(left, jnp.concatenate(rights, axis=1))
        for group in range(pair * (GROUPS // 8), (pair + 1) * (GROUPS // 8)):
            for index in range(EXACT):
                row = feats_ref[index, group : group + 1, :]
                for part, (at_group, at_lane) in enumerate(parts):
                    place = 2 * index + part
                    found[place] = jnp.where(at_group == group, pick(row, at_lane), found[place])
        for half, rank in enumerate((2 * pair, 2 * pair + 1)):
            at_high = tall_iota == spread(high_place[rank : rank + 1], (TALL, LANES))
            lanes = slice(half * LANES, (half + 1) * LANES)
            first = 0
            for index, count in enumerate(counts):
                total = product[first : first + TALL, lanes]
                for piece in range(1, count):
                    total = total + product[first + piece * TALL : first + (piece + 1) * TALL, lanes]
                first += count * TALL
                value = jnp.sum(jnp.where(at_high, total, 0.0), axis=0, keepdims=True)
                place = (EXACT + index) * CAP + rank
                table_ref[place : place + 1, :] = value
    table_ref[: EXACT * CAP, :] = jnp.concatenate(found, axis=0)
    table_ref[FEATS * CAP :, :] = jnp.zeros((PACK - FEATS * CAP, LANES), F32)
    store_rows(out_ref, table_ref[...])


PIX_CHUNK = 256


def render_kernel(
    height, lengths_ref, background_ref, geo_ref, arrived_ref, aux_ref, cotangent_ref, out_ref,
    slot_ref, table_ref, grad_ref, rows_ref, weight_ref,
):
    table_ref[:LANES, :] = arrived_ref[pl.ds(0, LANES, stride=2), :].T
    table_ref[LANES:, :] = arrived_ref[pl.ds(1, LANES, stride=2), :].T
    owner = aux_ref[0:8, :]
    rank = aux_ref[8:16, :]
    at_rank = [rank == place for place in range(CAP)]
    for index in range(FEATS):
        value = jnp.zeros((8, LANES), F32)
        for place in range(CAP):
            row = table_ref[index * CAP + place : index * CAP + place + 1, :]
            value = jnp.where(at_rank[place], pick(row, owner), value)
        slot_ref[index * 8 : index * 8 + 8, :] = value

    along = iota((SIDE, SLOTS), 0).astype(F32)
    slot_row, slot_col = iota((SLOTS, SLOTS), 0), iota((SLOTS, SLOTS), 1)
    weight_ref[0] = (slot_row < slot_col).astype(F32).astype(BF16)
    weight_ref[1] = (slot_row > slot_col).astype(F32).astype(BF16)
    slot_place = iota((1, SLOTS), 1)
    def tile(index, carry):
        def slots(feature):
            return jnp.concatenate(
                [slot_ref[pl.ds(feature * 8 + 2 * index + half, 1), :] for half in range(2)], axis=1
            )

        tile_x, tile_y = geo_ref[pl.ds(12 + index, 1), :], geo_ref[pl.ds(16 + index, 1), :]
        at_x = slots(0) - jnp.concatenate([tile_x] * 2, axis=1)
        at_y = slots(1) - jnp.concatenate([tile_y] * 2, axis=1)
        conic_a, conic_b, conic_c = slots(2), slots(3), slots(4)
        opacity = slots(5)
        live_opacity = jnp.where(slot_place < lengths_ref[0, index], opacity, 0.0)
        colors = [slots(6 + channel) for channel in range(3)]
        scaled_a, scaled_b, scaled_c = (-0.5 * LOG2_E) * conic_a, -LOG2_E * conic_b, (-0.5 * LOG2_E) * conic_c
        shades = [cotangent_ref[0, channel, pl.ds(index, 1), :] for channel in range(3)]
        behind = (
            shades[0] * background_ref[0] + shades[1] * background_ref[1] + shades[2] * background_ref[2]
        )
        columns = jnp.concatenate(shades + [behind, jnp.zeros((4, PIX), F32)], axis=0).T

        shade_high, shade_low = (part.astype(F32) for part in halves(jnp.concatenate(shades, axis=0)))
        color_high, color_low = (part.astype(F32) for part in halves(jnp.concatenate(colors, axis=0)))
        filler = jnp.zeros((7, PIX), F32)
        gains = lax.dot_general(
            jnp.concatenate([shade_high, shade_high, shade_low, filler], axis=0).astype(BF16),
            jnp.concatenate([color_high, color_low, color_high, filler], axis=0).astype(BF16),
            (((0,), (0,)), ((), ())),
            preferred_element_type=F32,
        )
        delta_x = along * (2.0 / (TX * SIDE)) - at_x
        slope_a = scaled_a * delta_x
        delta_y = along * (2.0 / (height * SIDE)) - at_y
        rows_ref[index, 0] = delta_y
        rows_ref[index, 1] = scaled_b * delta_y
        rows_ref[index, 2] = scaled_c * delta_y * delta_y

        def fold(values):
            return jnp.sum(values.reshape(PIX_CHUNK // 8, 8, SLOTS), axis=0)

        sums = [jnp.zeros((8, SLOTS), F32) for _ in range(9)]
        for chunk in range(PIX // PIX_CHUNK):
            rows = slice(chunk * PIX_CHUNK, (chunk + 1) * PIX_CHUNK)
            shape = (PIX_CHUNK, SLOTS)
            lines = range(chunk * PIX_CHUNK // SIDE, (chunk + 1) * PIX_CHUNK // SIDE)
            exponent = jnp.concatenate(
                [
                    (slope_a + rows_ref[index, 1, line : line + 1, :]) * delta_x
                    + rows_ref[index, 2, line : line + 1, :]
                    for line in lines
                ],
                axis=0,
            )
            coverage = live_opacity * jnp.exp2(exponent)
            log_pass = jnp.log2(1.0 - coverage)
            high, low = halves(log_pass)
            prefix = dot(high, weight_ref[0]) + dot(low, weight_ref[0])
            weight = coverage * jnp.exp2(prefix)
            shade = [spread(columns[rows, channel : channel + 1], shape) for channel in range(3)]
            product = weight * gains[rows]
            high, low = halves(product)
            later = dot(high, weight_ref[1]) + dot(low, weight_ref[1])
            remain = jnp.exp2(prefix[:, SLOTS - 1 :] + log_pass[:, SLOTS - 1 :])
            later = later + spread(columns[rows, 3:4] * remain, shape)
            slope = product - coverage * jnp.exp2(-log_pass) * later
            total, sum_x, sum_y, sum_xx, sum_xy, sum_yy = sums[:6]
            for place, line in enumerate(lines):
                down = rows_ref[index, 0, line : line + 1, :]
                part = slope[place * SIDE : (place + 1) * SIDE]
                part_x = part * delta_x
                part_xx = part_x * delta_x
                part, part_x, part_xx = (value[:8] + value[8:] for value in (part, part_x, part_xx))
                part_y = part * down
                total, sum_x, sum_xx = total + part, sum_x + part_x, sum_xx + part_xx
                sum_y, sum_yy, sum_xy = sum_y + part_y, sum_yy + part_y * down, sum_xy + part_x * down
            sums = [total, sum_x, sum_y, sum_xx, sum_xy, sum_yy] + [
                past + fold(value * weight) for past, value in zip(sums[6:], shade)
            ]

        sums = [jnp.sum(part, axis=0, keepdims=True) for part in sums]
        total, sum_x, sum_y, sum_xx, sum_xy, sum_yy = (part * -0.5 for part in sums[:6])
        grads = [
            -2.0 * (conic_a * sum_x + conic_b * sum_y),
            -2.0 * (conic_b * sum_x + conic_c * sum_y),
            sum_xx,
            2.0 * sum_xy,
            sum_yy,
            -2.0 * total / opacity,
        ] + sums[6:]
        for feature, value in enumerate(grads):
            for half in range(2):
                grad_ref[pl.ds(feature * 8 + 2 * index + half, 1), :] = value[:, half * LANES : (half + 1) * LANES]
        return carry

    lax.fori_loop(0, TILES_DEV, tile, 0, unroll=TILES_DEV)

    slot = aux_ref[16 : 16 + CAP, :]
    wanted = aux_ref[16 + CAP : 16 + 2 * CAP, :].astype(F32)
    parts = [(slot[8 * part : 8 * part + 8] >> 7, slot[8 * part : 8 * part + 8] & (LANES - 1)) for part in range(2)]
    blocks = []
    for feature in range(FEATS):
        for at_row, at_lane in parts:
            value = jnp.zeros((8, LANES), F32)
            for row in range(8):
                grads = grad_ref[feature * 8 + row : feature * 8 + row + 1, :]
                value = jnp.where(at_row == row, pick(grads, at_lane), value)
            blocks.append(value)
    blocks += [wanted, geo_ref[0:16, :], jnp.zeros((PACK - FEATS * CAP - CAP - 16, LANES), F32)]
    store_rows(out_ref, jnp.concatenate(blocks, axis=0))


def duplicate_kernel(returned_ref, own_ref, copies_ref, semaphores):
    copies = []
    for part, rows in enumerate((slice(0, LANES), slice(LANES, SENT))):
        own_ref[rows, :] = returned_ref[pl.ds(part, LANES, stride=2), :].T[: rows.stop - rows.start]
        for view in range(copies_ref.shape[0]):
            copy = pltpu.make_async_copy(own_ref.at[rows], copies_ref.at[view, rows], semaphores.at[view, part])
            copy.start()
            copies.append(copy)
    for copy in copies:
        copy.wait()


def scatter_view(view, arrived_ref, place, grads_ref, camera_ref):
    tall_iota = iota((TALL, LANES), 0)
    wide_iota = iota((WIDE, LANES), 0)
    values = arrived_ref[view, : FEATS * CAP, :]
    wanted = arrived_ref[view, FEATS * CAP : FEATS * CAP + CAP, :].astype(jnp.int32)
    camera_ref[place] = arrived_ref[view, FEATS * CAP + CAP : SENT, :]
    high_place, low_place = wanted >> 8, wanted & (WIDE - 1)
    high, low = halves(values)
    high, low = high.astype(F32), low.astype(F32)
    lefts, rights = [], []
    for rank in range(CAP):
        at_high = tall_iota == spread(high_place[rank : rank + 1], (TALL, LANES))
        at_low = wide_iota == spread(low_place[rank : rank + 1], (WIDE, LANES))
        at_low = at_low.astype(F32).astype(BF16)
        for source in (high, low):
            rows = [source[index * CAP + rank : index * CAP + rank + 1] for index in range(FEATS)]
            left = [jnp.where(at_high, spread(row, (TALL, LANES)), 0.0) for row in rows]
            lefts.append(jnp.concatenate(left, axis=0).astype(BF16))
            rights.append(at_low)
    total = dot_lanes(jnp.concatenate(lefts, axis=1), jnp.concatenate(rights, axis=1))
    for half in range(2):
        grads_ref[place, pl.ds(half, FEATS * TALL, stride=2), :] = total[:, half * LANES : (half + 1) * LANES]


SHAPE_ROWS = (3, 4, 5, 6, 7, 8, 9, 59, 60)


def read_chunks(ref, block, index):
    return jnp.concatenate(
        [ref[block * WIDTH + part, pl.ds(index, 8, stride=PITCH), :] for part in range(WIDTH)], axis=0
    )


def write_chunks(ref, block, index, value):
    for part in range(WIDTH):
        ref[block * WIDTH + part, pl.ds(index, 8, stride=PITCH), :] = value[8 * part : 8 * part + 8]


def pull_view(chunk, place, center, shape, param, grads_ref, camera_ref, kept, keep):
    def cotangent(feature):
        rows = 8 * WIDTH
        return grads_ref[place, pl.ds(pl.multiple_of(feature * GROUPS + chunk * rows, rows), rows), :]

    def add(index, value):
        before = kept(index)
        keep(index, value if before is None else before + value)

    rotate, offset = camera_of(camera_ref[place], 8 * WIDTH)
    eye = camera_center(rotate, offset)
    basis, basis_back = jax.vjp(lambda spot: direction_basis(spot, eye), center)
    colors = [cotangent(6 + channel) for channel in range(3)]
    basis_grad = []
    for term in range(16):
        total = None
        for channel in range(3):
            index = 11 + 3 * term + channel
            add(index, basis[term] * colors[channel])
            piece = param(index) * colors[channel]
            total = piece if total is None else total + piece
        basis_grad.append(total)
    (along,) = basis_back(basis_grad)
    unused, screen_back = jax.vjp(
        lambda spot, matrix: screen_features(spot, matrix, rotate, offset), center, shape
    )
    moved, bent = screen_back([cotangent(index) for index in range(5)])
    for axis in range(3):
        add(axis, along[axis] + moved[axis])
    for row in range(3):
        for col in range(3):
            add(SHAPE_ROWS[3 * row + col], bent[row][col])
    add(10, cotangent(5))


def own_pullback_kernel(
    returned_ref, params_ref, out_ref, held_hbm,
    staged_ref, held_ref, grads_ref, camera_ref, partial_ref, fetch_sems, held_sems, semaphores,
):
    def fetch(chunk):
        columns = chunk_columns(chunk)
        return pltpu.make_async_copy(params_ref.at[:, columns], staged_ref.at[:, columns], fetch_sems.at[chunk])

    def hold(chunk):
        return pltpu.make_async_copy(held_ref.at[chunk], held_hbm.at[chunk], held_sems.at[chunk])

    def send(chunk):
        return pltpu.make_async_copy(partial_ref.at[chunk], out_ref.at[chunk], semaphores.at[chunk])

    each_chunk(lambda chunk: fetch(chunk).start())
    scatter_view(0, returned_ref, 0, grads_ref, camera_ref)

    def step(block, carry):
        for part in range(WIDTH):
            chunk = block * WIDTH + part
            fetch(chunk).wait()
            spread_columns(staged_ref, held_ref, chunk)
            hold(chunk).start()

        def param(index):
            return read_chunks(held_ref, block, index)

        def keep(index, value):
            write_chunks(partial_ref, block, index, value)

        center = [param(index) for index in range(3)]
        shape = shape_matrix([param(3 + index) for index in range(3)], [param(6 + index) for index in range(4)])
        pull_view(block, 0, center, shape, param, grads_ref, camera_ref, lambda index: None, keep)
        for part in range(WIDTH):
            send(block * WIDTH + part).start()
        return carry

    lax.fori_loop(0, CHUNKS // WIDTH, step, 0)
    each_chunk(lambda chunk: send(chunk).wait())
    each_chunk(lambda chunk: hold(chunk).wait())


def pullback_kernel(
    arrived_ref, held_hbm, partial_hbm, out_ref,
    held_ref, partial_ref, grads_ref, camera_ref, staged_ref, held_sems, partial_sems, semaphores,
):
    views = arrived_ref.shape[0]

    def fetch_held(chunk):
        return pltpu.make_async_copy(held_hbm.at[chunk], held_ref.at[chunk], held_sems.at[chunk])

    def fetch_partial(chunk):
        return pltpu.make_async_copy(partial_hbm.at[chunk], partial_ref.at[chunk], partial_sems.at[chunk])

    def start(chunk):
        fetch_held(chunk).start()
        fetch_partial(chunk).start()

    each_chunk(start)

    def one_view(place, carry):
        view = lax.rem(lax.axis_index("view") + 1 + place, views)
        scatter_view(view, arrived_ref, place, grads_ref, camera_ref)
        return carry

    lax.fori_loop(0, views - 1, one_view, 0, unroll=True)

    def send(chunk):
        columns = chunk_columns(chunk)
        return pltpu.make_async_copy(staged_ref.at[:, columns], out_ref.at[:, columns], semaphores.at[chunk])

    def step(block, carry):
        for part in range(WIDTH):
            fetch_held(block * WIDTH + part).wait()
            fetch_partial(block * WIDTH + part).wait()

        def param(index):
            return read_chunks(held_ref, block, index)

        def keep(index, value):
            write_chunks(partial_ref, block, index, value)

        def kept(index):
            return read_chunks(partial_ref, block, index)

        center = [param(index) for index in range(3)]
        shape, shape_back = jax.vjp(
            shape_matrix, [param(3 + index) for index in range(3)], [param(6 + index) for index in range(4)]
        )
        for place in range(views - 1):
            pull_view(block, place, center, shape, param, grads_ref, camera_ref, kept, keep)
        scale_grad, quaternion_grad = shape_back(
            [[kept(SHAPE_ROWS[3 * row + col]) for col in range(3)] for row in range(3)]
        )
        opacity = 1.0 / (1.0 + jnp.exp(-param(10)))
        finals = list(scale_grad) + list(quaternion_grad) + [opacity * (1.0 - opacity) * kept(10)]
        for index, value in enumerate(finals):
            keep(3 + index, value)
        for part in range(WIDTH):
            chunk = block * WIDTH + part
            for group in range(CHUNK // LANES):
                columns = pl.ds(pl.multiple_of(chunk * CHUNK + group * LANES, LANES), LANES)
                staged_ref[:, columns] = partial_ref[chunk, group * PITCH : group * PITCH + PARAMS, :]
            send(chunk).start()
        return carry

    lax.fori_loop(0, CHUNKS // WIDTH, step, 0)
    each_chunk(lambda chunk: send(chunk).wait())


def call(kernel, out_shape, operands, smalls=(), scratch=(), **kwargs):
    spaces = [pltpu.SMEM if index < smalls else pltpu.VMEM for index in range(len(operands))]
    single = not isinstance(out_shape, (list, tuple))
    outs = pl.BlockSpec(memory_space=pltpu.VMEM)
    return pl.pallas_call(
        kernel,
        out_shape=out_shape,
        in_specs=[pl.BlockSpec(memory_space=space) for space in spaces],
        out_specs=outs if single else [outs] * len(out_shape),
        scratch_shapes=list(scratch),
        compiler_params=pltpu.CompilerParams(vmem_limit_bytes=VMEM_LIMIT),
        **kwargs,
    )(*operands)


WIDTH = 2
HELD = jax.ShapeDtypeStruct((CHUNKS, 8 * PITCH, LANES), F32)


def route(tile_lists):
    return pl.pallas_call(
        route_kernel,
        out_shape=[
            jax.ShapeDtypeStruct((OWNERS, LANES), jnp.int32),
            jax.ShapeDtypeStruct((16 + 2 * CAP, LANES), jnp.int32),
        ],
        in_specs=[pl.BlockSpec(memory_space=pl.ANY)],
        out_specs=[pl.BlockSpec(memory_space=pltpu.VMEM)] * 2,
        scratch_shapes=[
            pltpu.VMEM(tile_lists.shape, jnp.int32),
            pltpu.SemaphoreType.DMA,
        ],
        compiler_params=pltpu.CompilerParams(vmem_limit_bytes=ROUTE_VMEM_LIMIT),
    )(tile_lists)


def project(height, camera, gauss_params):
    return pl.pallas_call(
        functools.partial(project_kernel, height),
        out_shape=[
            jax.ShapeDtypeStruct((FEATS, GROUPS, LANES), F32),
            jax.ShapeDtypeStruct((GEO, LANES), F32),
        ],
        in_specs=[pl.BlockSpec(memory_space=pl.ANY)] * 2,
        out_specs=[pl.BlockSpec(memory_space=pltpu.VMEM)] * 2,
        scratch_shapes=[
            pltpu.VMEM((PARAMS, G_DEV), F32),
            pltpu.VMEM(HELD.shape, F32),
            pltpu.SMEM(camera.shape, F32),
            pltpu.SemaphoreType.DMA((CHUNKS,)),
            pltpu.SemaphoreType.DMA,
        ],
        compiler_params=pltpu.CompilerParams(vmem_limit_bytes=WIDE_VMEM_LIMIT),
    )(camera, gauss_params)


def gather(requested, features):
    return call(
        gather_kernel,
        jax.ShapeDtypeStruct((2 * OWNERS, LANES), F32),
        [requested, features],
        smalls=0,
        scratch=[pltpu.VMEM((PACK, LANES), F32)],
    )


def render(height, tile_lengths, background, geometry, arrived, aux, cotangent):
    return call(
        functools.partial(render_kernel, height),
        jax.ShapeDtypeStruct((2 * OWNERS, LANES), F32),
        [tile_lengths, background, geometry, arrived, aux, cotangent],
        smalls=2,
        scratch=[
            pltpu.VMEM((FEATS * 8, LANES), F32),
            pltpu.VMEM((2 * OWNERS, LANES), F32),
            pltpu.VMEM((FEATS * 8, LANES), F32),
            pltpu.VMEM((TILES_DEV, 3, SIDE, SLOTS), F32),
            pltpu.VMEM((2, SLOTS, SLOTS), BF16),
        ],
    )


def duplicate(returned, views):
    return pl.pallas_call(
        duplicate_kernel,
        out_shape=[
            jax.ShapeDtypeStruct((SENT, LANES), F32),
            jax.ShapeDtypeStruct((views, SENT, LANES), F32),
        ],
        in_specs=[pl.BlockSpec(memory_space=pltpu.VMEM)],
        out_specs=[pl.BlockSpec(memory_space=pltpu.VMEM), pl.BlockSpec(memory_space=pl.ANY)],
        scratch_shapes=[pltpu.SemaphoreType.DMA((views, 2))],
        compiler_params=pltpu.CompilerParams(vmem_limit_bytes=VMEM_LIMIT),
    )(returned)


def own_pullback(own, gauss_params):
    return pl.pallas_call(
        own_pullback_kernel,
        out_shape=[HELD, HELD],
        in_specs=[pl.BlockSpec(memory_space=pltpu.VMEM), pl.BlockSpec(memory_space=pl.ANY)],
        out_specs=[pl.BlockSpec(memory_space=pl.ANY)] * 2,
        scratch_shapes=[
            pltpu.VMEM((PARAMS, G_DEV), F32),
            pltpu.VMEM(HELD.shape, F32),
            pltpu.VMEM((1, FEATS * GROUPS, LANES), F32),
            pltpu.VMEM((1, 16, LANES), F32),
            pltpu.VMEM(HELD.shape, F32),
            pltpu.SemaphoreType.DMA((CHUNKS,)),
            pltpu.SemaphoreType.DMA((CHUNKS,)),
            pltpu.SemaphoreType.DMA((CHUNKS,)),
        ],
        compiler_params=pltpu.CompilerParams(vmem_limit_bytes=WIDE_VMEM_LIMIT),
        cost_estimate=pl.CostEstimate(flops=20_000_000, bytes_accessed=4_000_000, transcendentals=0),
    )(own.reshape((1,) + own.shape), gauss_params)


def pullback(arrived, held, partial):
    others = arrived.shape[0] - 1
    return pl.pallas_call(
        pullback_kernel,
        out_shape=jax.ShapeDtypeStruct((PARAMS, G_DEV), F32),
        in_specs=[
            pl.BlockSpec(memory_space=space) for space in (pltpu.VMEM, pl.ANY, pl.ANY)
        ],
        out_specs=pl.BlockSpec(memory_space=pl.ANY),
        scratch_shapes=[
            pltpu.VMEM(HELD.shape, F32),
            pltpu.VMEM(HELD.shape, F32),
            pltpu.VMEM((others, FEATS * GROUPS, LANES), F32),
            pltpu.VMEM((others, 16, LANES), F32),
            pltpu.VMEM((PARAMS, G_DEV), F32),
            pltpu.SemaphoreType.DMA((CHUNKS,)),
            pltpu.SemaphoreType.DMA((CHUNKS,)),
            pltpu.SemaphoreType.DMA((CHUNKS,)),
        ],
        compiler_params=pltpu.CompilerParams(vmem_limit_bytes=WIDE_VMEM_LIMIT),
    )(arrived, held, partial)


def per_device(gauss_params, camera, background, tile_lists, tile_lengths, pixel_cotangent):
    owners_total = lax.axis_size("img")
    views = lax.axis_size("view")
    tiles_here = tile_lists.shape[1]
    height = tiles_here * owners_total // TX
    requests, aux = route(tile_lists)
    features, geometry = project(height, camera, gauss_params)
    requested = lax.all_to_all(requests, "img", split_axis=0, concat_axis=0, tiled=True)
    outgoing = gather(requested, features)
    arrived = lax.all_to_all(outgoing, "img", split_axis=0, concat_axis=0, tiled=True)
    slot_grads = render(height, tile_lengths, background, geometry, arrived, aux, pixel_cotangent)
    returned = lax.all_to_all(slot_grads, "img", split_axis=0, concat_axis=0, tiled=True)
    own, copies = duplicate(returned, views)
    everyone = lax.all_to_all(copies, "view", split_axis=0, concat_axis=0, tiled=True)
    partial, held = own_pullback(own, gauss_params)
    return pullback(everyone, held, partial)


def solution(mesh):
    placed = (
        P(None, "img"),
        P("view", None),
        P(),
        P("view", "img", None),
        P("view", "img"),
        P("view", None, "img", None),
    )
    return jax.shard_map(
        per_device, mesh=mesh, in_specs=placed, out_specs=P(None, "img"), check_vma=False
    )
```
